32 devices in a mesh: rad: 4 (over z), azi: 8 (over y, x, core).
Axes of the slice: x: 2, y: 2, z: 4, core: 2. Of those that a mesh axis runs over, the one named last changes fastest.
Arguments:
- fields: float32 [5, 1, 512, 512], P(None, None, 'azi', 'rad'), may hold values from -2 to 2, as said below
- shifts: int32 [3, 512], P(None, 'rad'), may hold values from 0 to 192, as said below
Outputs:
- advanced: float32 [5, 1, 512, 512], P(None, None, 'azi', 'rad')
The draws below stay inside these ranges and needn't reach their ends.
Inputs may be any that keep to these rules, and one draw needn't show every extreme that they name: `fields`: every field component lies within -2 to 2; temperature within 0.5 to 1.5. `shifts`: each step has a row with shift 192 and a row with shift 0.
All inputs are finite; a program needn't handle non-finite values.
Results may differ from the reference program's by a relative error of at most 0.00002.
Values sent between devices are 32-bit elements; how exact they have to be, the bound alone decides.
A program may use at most 64 MiB of HBM per device.

```python
import jax
import jax.numpy as jnp

POL = 1
STEPS = 3
SMAX = 192
NR = 512
NPHI = 512


def draw_fields(key, part):
    keys = jax.random.split(key, 6)
    shape = (POL, NPHI, NR)
    log_rho = jnp.clip(0.5 * jax.random.normal(keys[0], shape, jnp.float32), -2.0, 2.0)
    vels = [jax.random.uniform(keys[i], shape, jnp.float32, -1.0, 1.0) for i in (1, 2, 3)]
    temper = jax.random.uniform(keys[4], shape, jnp.float32, 0.5, 1.5)
    return jnp.stack([log_rho, vels[0], vels[1], vels[2], temper]).astype(jnp.float32)


def draw_shifts(key, part):
    values = jax.random.randint(key, (STEPS, NR), 0, SMAX + 1, dtype=jnp.int32)
    values = values.at[:, 0].set(SMAX)
    values = values.at[:, 1].set(0)
    return values.astype(jnp.int32)


def setup_inputs(seed: int = 0) -> dict:
    streams_of = jax.random.split(jax.random.key(seed), 3)
    fields = draw_fields(jax.random.fold_in(streams_of[2], 71), 0)
    shifts = draw_shifts(jax.random.fold_in(streams_of[2], 71), 0)
    return dict(fields=fields, shifts=shifts)


courant = 0.2
viscous = 0.1


def update(padded, inverse):
    centre = padded[:, :, 1:-1, 1:-1]
    inner = padded[:, :, 1:-1, :-2]
    outer = padded[:, :, 1:-1, 2:]
    behind = padded[:, :, :-2, 1:-1]
    ahead = padded[:, :, 2:, 1:-1]
    polar_pad = jnp.concatenate([centre[:, :1], centre, centre[:, -1:]], axis=1)
    polar_sum = polar_pad[:, 2:] + polar_pad[:, :-2]
    radial_vel = centre[1]
    azim_vel = centre[2]
    advect = courant * (jnp.maximum(radial_vel, 0.0) * (centre - inner) + jnp.minimum(radial_vel, 0.0) * (outer - centre)
                        + inverse * (jnp.maximum(azim_vel, 0.0) * (centre - behind) + jnp.minimum(azim_vel, 0.0) * (ahead - centre)))
    laplace = (outer + inner - 2.0 * centre) + inverse * inverse * (ahead + behind - 2.0 * centre) + (polar_sum - 2.0 * centre)
    radial_diff = (outer - inner) * 0.5
    azim_diff = (ahead - behind) * 0.5
    diverge = radial_diff[1] + inverse * azim_diff[2]
    log_rho = centre[0]
    temper = centre[4]
    new_log = log_rho - advect[0] - courant * diverge
    new_radial = radial_vel - advect[1] - courant * (temper * radial_diff[0] + radial_diff[4]) + 0.5 * courant * inverse * azim_vel * azim_vel + viscous * laplace[1]
    new_azim = azim_vel - advect[2] - courant * inverse * (temper * azim_diff[0] + azim_diff[4]) - 0.5 * courant * inverse * radial_vel * azim_vel + viscous * laplace[2]
    new_polar = centre[3] - advect[3] + viscous * laplace[3]
    new_temper = temper - advect[4] - courant * 0.4 * temper * diverge + viscous * laplace[4]
    return jnp.stack([new_log, new_radial, new_azim, new_polar, new_temper])


def reference(fields, shifts):
    radius = 1.0 + (jnp.arange(NR).astype(jnp.float32) + 0.5) / jnp.float32(NR)
    inverse = 1.0 / radius
    cells = jnp.arange(NPHI, dtype=jnp.int32)
    for step in range(STEPS):
        radial_pad = jnp.pad(fields, ((0, 0), (0, 0), (0, 0), (1, 1)))
        padded = jnp.concatenate([radial_pad[:, :, -1:], radial_pad, radial_pad[:, :, :1]], axis=2)
        fields = update(padded, inverse)
        source = jnp.mod(cells[:, None] - shifts[step][None, :], NPHI).astype(jnp.int32)
        source = jnp.broadcast_to(source[None, None], fields.shape)
        fields = jnp.take_along_axis(fields, source, axis=2)
    return fields
```

```python
import functools

import jax
import jax.numpy as jnp
from jax import lax
from jax.experimental import pallas as pl
from jax.experimental.pallas import tpu as pltpu
from jax.sharding import PartitionSpec as P

STEPS = 3
SMAX = 192
FIELDS = 5
LANES = 128
SUB = 8
HALF = 64

courant = 0.2
viscous = 0.1


def halves(a, b, low):
    first = jnp.where(low, a, pltpu.roll(b, HALF, b.ndim - 1))
    second = jnp.where(low, pltpu.roll(a, HALF, a.ndim - 1), b)
    return first, second


def step_update(f, inverse):
    inner = [pltpu.roll(u, 1, 0) for u in f]
    outer = [pltpu.roll(u, u.shape[0] - 1, 0) for u in f]
    behind = [pltpu.roll(u, 1, 1) for u in f]
    ahead = [pltpu.roll(u, u.shape[1] - 1, 1) for u in f]
    log_rho, vr, vp, _, temper = f
    r_pos = courant * jnp.maximum(vr, 0.0)
    r_neg = courant * jnp.minimum(vr, 0.0)
    cg = courant * inverse
    p_pos = cg * jnp.maximum(vp, 0.0)
    p_neg = cg * jnp.minimum(vp, 0.0)
    vg2 = viscous * inverse * inverse

    def moved(i):
        u = f[i]
        d_in, d_out = u - inner[i], outer[i] - u
        d_back, d_fwd = u - behind[i], ahead[i] - u
        base = u - (r_pos * d_in + r_neg * d_out + p_pos * d_back + p_neg * d_fwd)
        if i == 0:
            return base
        polar = (u + u) - 2.0 * u
        return base + (viscous * ((d_out - d_in) + polar) + vg2 * (d_fwd - d_back))

    def dr(i):
        return (outer[i] - inner[i]) * 0.5

    def dp(i):
        return (ahead[i] - behind[i]) * 0.5

    diverge = dr(1) + inverse * dp(2)
    new_log = moved(0) - courant * diverge
    new_vr = moved(1) - courant * (temper * dr(0) + dr(4)) + (0.5 * cg) * vp * vp
    new_vp = moved(2) - cg * (temper * dp(0) + dp(4)) - (0.5 * cg) * vr * vp
    new_vz = moved(3)
    new_t = moved(4) - (courant * 0.4) * temper * diverge
    return [new_log, new_vr, new_vp, new_vz, new_t]


def rotate(u, index, lag):
    tiles = u.shape[1] // LANES
    g = [
        jnp.take_along_axis(u[:, q * LANES : (q + 1) * LANES], index, axis=1)
        for q in range(tiles)
    ]
    out = []
    for q in range(tiles):
        value = g[(q - (SMAX // LANES + 1)) % tiles]
        for back in range(SMAX // LANES, -1, -1):
            value = jnp.where(lag == back, g[(q - back) % tiles], value)
        out.append(value)
    return jnp.concatenate(out, axis=1)


def kernel(
    n, nr, f_ref, s_ref, o_ref, z, send, recv, edge, send2, recv2,
    ssem, rsem, esend, erecv, ssem2, rsem2,
):
    r = lax.axis_index("rad")
    t = lax.axis_index("azi")
    tiles = f_ref.shape[3] // SUB
    peers = [lax.rem(t + d, n) for d in range(1, n)]
    top_edge = (t == 0) & (r > 0)
    bottom_edge = (t == n - 1) & (r < nr - 1)

    barrier = pltpu.get_barrier_semaphore()
    for peer in peers:
        pl.semaphore_signal(barrier, inc=1, device_id={"azi": peer})

    @pl.when(top_edge)
    def _():
        for b in range(n):
            pl.semaphore_signal(barrier, inc=1, device_id={"rad": r - 1, "azi": b})

    @pl.when(bottom_edge)
    def _():
        for b in range(n):
            pl.semaphore_signal(barrier, inc=1, device_id={"rad": r + 1, "azi": b})

    sub = lax.broadcasted_iota(jnp.int32, (SUB, LANES), 0)
    lane = lax.broadcasted_iota(jnp.int32, (SUB, LANES), 1)
    low = lane < HALF

    shifts = s_ref[...].astype(jnp.float32)
    rest = jnp.zeros((HALF - STEPS, LANES), jnp.float32)
    stacks = [
        f_ref[0:2, 0].reshape(LANES, LANES),
        f_ref[2:4, 0].reshape(LANES, LANES),
        jnp.concatenate([f_ref[4, 0], shifts, rest], axis=0),
    ]
    for p, stack in enumerate(stacks):
        z[:, p] = stack.T.reshape(tiles, SUB, LANES)

    for k in range(n):
        a, b = 2 * k, 2 * k + 1
        for p in range(2):
            send[k, 2 * p] = z[a, p]
            send[k, 2 * p + 1] = z[b, p]
        send[k, 4] = jnp.where(low, z[a, 2], pltpu.roll(z[b, 2], HALF, 1))
        above, below = max(a - 1, 0), min(b + 1, tiles - 1)
        for p in range(3):
            send[k, 5 + p] = jnp.where(sub >= SUB - STEPS, z[above, p], z[below, p])

    needed = n - 1 + (r > 0).astype(jnp.int32) + (r < nr - 1).astype(jnp.int32)
    pl.semaphore_wait(barrier, needed)

    def edge_copy(which, row, slot, device):
        return pltpu.make_async_remote_copy(
            src_ref=z.at[row], dst_ref=edge.at[slot], send_sem=esend.at[which],
            recv_sem=erecv.at[slot], device_id=device,
        )

    to_inner = edge_copy(0, 0, t, {"rad": r - 1, "azi": n - 1})
    to_outer = edge_copy(1, tiles - 1, t, {"rad": r + 1, "azi": 0})

    @pl.when(r > 0)
    def _():
        to_inner.start()

    @pl.when(r < nr - 1)
    def _():
        to_outer.start()

    copies = []
    for d, peer in enumerate(peers):
        copy = pltpu.make_async_remote_copy(
            src_ref=send.at[peer], dst_ref=recv.at[t], send_sem=ssem.at[d],
            recv_sem=rsem.at[d], device_id={"azi": peer},
        )
        copy.start()
        copies.append(copy)
    recv[t] = send[t]

    rows = 3 * SUB
    width = n * HALF
    row = lax.broadcasted_iota(jnp.int32, (rows, width), 0)
    row = jnp.where(row < 2 * SUB + SUB // 2, row, row - rows)
    row = row + (r * f_ref.shape[3] + t * (2 * SUB))
    total = nr * f_ref.shape[3]
    inside = (row >= 0) & (row < total)
    radius = 1.0 + (row.astype(jnp.float32) + 0.5) / jnp.float32(total)
    inverse = 1.0 / radius

    for copy in copies:
        copy.wait_recv()

    @pl.when(top_edge | bottom_edge)
    def _():
        first = jnp.where(t == 0, SUB - STEPS, 0)
        last = jnp.where(t == 0, SUB, STEPS)
        take = (sub >= first) & (sub < last)
        for b in range(n):
            edge_copy(0, 0, b, {"rad": lax.rem(r + 1, nr), "azi": 0}).wait_recv()
            for p in range(3):
                recv[b, 5 + p] = jnp.where(take, edge[b, p], recv[b, 5 + p])

    fields = [[] for _ in range(FIELDS)]
    for q in range(n // 2):
        got = [halves(recv[2 * q, i], recv[2 * q + 1, i], low) for i in range(8)]
        for p in range(2):
            for h in range(2):
                fields[2 * p + h].append(
                    jnp.concatenate([got[2 * p][h], got[2 * p + 1][h], got[5 + p][h]], axis=0)
                )
        fields[4].append(jnp.concatenate([got[4][0], got[4][1], got[7][0]], axis=0))
    fields = [jnp.where(inside, jnp.concatenate(u, axis=1), 0.0) for u in fields]

    carried = jnp.concatenate([z[2 * t, 2], z[2 * t + 1, 2], recv[0, 7]], axis=0)
    lanes = lax.broadcasted_iota(jnp.int32, (rows, LANES), 1)
    for step in range(STEPS):
        shift = carried[:, HALF + step : HALF + step + 1].astype(jnp.int32)
        shift = jnp.broadcast_to(shift, (rows, LANES))
        whole = jnp.where(shift >= LANES, 1, 0)
        part = shift - whole * LANES
        index = jnp.bitwise_and(lanes - part, LANES - 1)
        lag = whole + jnp.where(lanes < part, 1, 0)
        fields = [jnp.where(inside, u, 0.0) for u in step_update(fields, inverse)]
        fields = [rotate(u, index, lag) for u in fields]

    for q in range(n // 2):
        f = [u[:, q * LANES : (q + 1) * LANES] for u in fields]
        for p in range(2):
            for i in range(2):
                rs = slice(i * SUB, (i + 1) * SUB)
                even, odd = halves(f[2 * p][rs], f[2 * p + 1][rs], low)
                send2[2 * q, 2 * p + i] = even
                send2[2 * q + 1, 2 * p + i] = odd
        even, odd = halves(f[4][:SUB], f[4][SUB : 2 * SUB], low)
        send2[2 * q, 4] = even
        send2[2 * q + 1, 4] = odd

    backs = []
    for d, peer in enumerate(peers):
        copy = pltpu.make_async_remote_copy(
            src_ref=send2.at[peer], dst_ref=recv2.at[t], send_sem=ssem2.at[d],
            recv_sem=rsem2.at[d], device_id={"azi": peer},
        )
        copy.start()
        backs.append(copy)
    recv2[t] = send2[t]

    for copy in copies:
        copy.wait_send()

    @pl.when(r > 0)
    def _():
        to_inner.wait_send()

    @pl.when(r < nr - 1)
    def _():
        to_outer.wait_send()

    for copy in backs:
        copy.wait_recv()

    for p in range(2):
        block = recv2[:, 2 * p : 2 * p + 2].reshape(LANES, LANES)
        o_ref[2 * p : 2 * p + 2, 0] = block.T.reshape(2, HALF, LANES)
    parts = []
    for b in range(n):
        tile = recv2[b, 4]
        parts += [tile, pltpu.roll(tile, HALF, 1)]
    o_ref[4, 0] = jnp.concatenate(parts, axis=0).T[:HALF]

    for copy in backs:
        copy.wait_send()


def by_cycles(n, nr, fields, shifts):
    tiles = fields.shape[3] // SUB
    tile = (SUB, LANES)
    dma = pltpu.SemaphoreType.DMA
    return pl.pallas_call(
        functools.partial(kernel, n, nr),
        out_shape=jax.ShapeDtypeStruct(fields.shape, fields.dtype),
        in_specs=[pl.BlockSpec(memory_space=pltpu.VMEM)] * 2,
        out_specs=pl.BlockSpec(memory_space=pltpu.VMEM),
        scratch_shapes=[
            pltpu.VMEM((tiles, 3) + tile, jnp.float32),
            pltpu.VMEM((n, 8) + tile, jnp.float32),
            pltpu.VMEM((n, 8) + tile, jnp.float32),
            pltpu.VMEM((n, 3) + tile, jnp.float32),
            pltpu.VMEM((n, 5) + tile, jnp.float32),
            pltpu.VMEM((n, 5) + tile, jnp.float32),
            dma((n - 1,)),
            dma((n - 1,)),
            dma((2,)),
            dma((n,)),
            dma((n - 1,)),
            dma((n - 1,)),
        ],
        compiler_params=pltpu.CompilerParams(
            collective_id=0, has_side_effects=True, vmem_limit_bytes=16 * 1024 * 1024
        ),
    )(fields, shifts)


def passed_along(value, axis, steps):
    count = lax.axis_size(axis)
    pairs = [(source, (source + steps) % count) for source in range(count)]
    return lax.ppermute(value, axis, pairs)


def padded_2(value, sides, width, wrap):
    for axis, dim in sides:
        count, length = (lax.axis_size(axis), value.shape[dim])
        up = [(i, (i + 1) % count) for i in range(count if wrap else count - 1)]
        down = [(j, i) for i, j in up]
        last = lax.slice_in_dim(value, length - width, length, axis=dim)
        initial = lax.slice_in_dim(value, 0, width, axis=dim)
        before = lax.ppermute(last, axis, up)
        after = lax.ppermute(initial, axis, down)
        value = jnp.concatenate([before, value, after], axis=dim)
    return value


def update(padded, inverse):
    centre = padded[:, :, 1:-1, 1:-1]
    inner = padded[:, :, 1:-1, :-2]
    outer = padded[:, :, 1:-1, 2:]
    behind = padded[:, :, :-2, 1:-1]
    ahead = padded[:, :, 2:, 1:-1]
    polar_pad = jnp.concatenate([centre, centre, centre], axis=1)
    polar_sum = polar_pad[:, 2:] + polar_pad[:, :-2]
    radial_vel = centre[1]
    azim_vel = centre[2]
    advect = courant * (
        jnp.maximum(radial_vel, 0.0) * (centre - inner)
        + jnp.minimum(radial_vel, 0.0) * (outer - centre)
        + inverse
        * (
            jnp.maximum(azim_vel, 0.0) * (centre - behind)
            + jnp.minimum(azim_vel, 0.0) * (ahead - centre)
        )
    )
    laplace = (
        outer
        + inner
        - 2.0 * centre
        + inverse * inverse * (ahead + behind - 2.0 * centre)
        + (polar_sum - 2.0 * centre)
    )
    radial_diff = (outer - inner) * 0.5
    azim_diff = (ahead - behind) * 0.5
    diverge = radial_diff[1] + inverse * azim_diff[2]
    log_rho = centre[0]
    temper = centre[4]
    new_log = log_rho - advect[0] - courant * diverge
    new_radial = (
        radial_vel
        - advect[1]
        - courant * (temper * radial_diff[0] + radial_diff[4])
        + 0.5 * courant * inverse * azim_vel * azim_vel
        + viscous * laplace[1]
    )
    new_azim = (
        azim_vel
        - advect[2]
        - courant * inverse * (temper * azim_diff[0] + azim_diff[4])
        - 0.5 * courant * inverse * radial_vel * azim_vel
        + viscous * laplace[2]
    )
    new_polar = centre[3] - advect[3] + viscous * laplace[3]
    new_temper = temper - advect[4] - courant * 0.4 * temper * diverge + viscous * laplace[4]
    return jnp.stack([new_log, new_radial, new_azim, new_polar, new_temper])


def rotate_pieces(fields, offsets):
    width = fields.shape[2]
    count = (SMAX + width - 1) // width
    pieces = [fields]
    for blocks in range(1, count + 1):
        pieces.append(passed_along(fields, "azi", blocks))
    extended = jnp.concatenate(pieces[::-1], axis=2)
    nbits = SMAX.bit_length()
    reach = (1 << nbits) - 1
    anchor = count * width
    front = jnp.zeros(fields.shape[:2] + (reach - anchor,) + fields.shape[3:], fields.dtype)
    window = jnp.concatenate([front, extended], axis=2)
    for bit in range(nbits):
        amount = 1 << bit
        length = window.shape[2] - amount
        chosen = offsets // amount % 2 == 1
        window = jnp.where(
            chosen[None, None, None, :], window[:, :, :length], window[:, :, amount:]
        )
    return window


def by_blocks(fields, shifts):
    rows = fields.shape[3]
    total_rows = rows * lax.axis_size("rad")
    row_index = lax.axis_index("rad") * rows + jnp.arange(rows, dtype=jnp.int32)
    radius = 1.0 + (row_index.astype(jnp.float32) + 0.5) / jnp.float32(total_rows)
    inverse = 1.0 / radius
    for step in range(STEPS):
        radial_pad = padded_2(fields, (("rad", 3),), 1, False)
        padded = padded_2(radial_pad, (("azi", 2),), 1, True)
        fields = update(padded, inverse)
        fields = rotate_pieces(fields, shifts[step])
    return fields


def local(fields, shifts):
    n, nr = lax.axis_size("azi"), lax.axis_size("rad")
    count, planes, width, rows = fields.shape
    fits = (count, planes, width, rows) == (FIELDS, 1, HALF, LANES)
    if fits and rows == n * 2 * SUB and n * width > SMAX + LANES:
        return by_cycles(n, nr, fields, shifts)
    return by_blocks(fields, shifts)


def solution(mesh):
    placed = (P(None, None, "azi", "rad"), P(None, "rad"))
    return jax.shard_map(
        local, mesh=mesh, in_specs=placed, out_specs=P(None, None, "azi", "rad"), check_vma=False
    )
```

```python
import functools

import jax
import jax.numpy as jnp
from jax import lax
from jax.experimental import pallas as pl
from jax.experimental.pallas import tpu as pltpu
from jax.sharding import PartitionSpec as P

STEPS = 3
SMAX = 192
FIELDS = 5
LANES = 128
SUB = 8
HALF = 64

courant = 0.2
viscous = 0.1


def halves(a, b, low):
    first = jnp.where(low, a, pltpu.roll(b, HALF, b.ndim - 1))
    second = jnp.where(low, pltpu.roll(a, HALF, a.ndim - 1), b)
    return first, second


def step_update(f, inverse):
    inner = [pltpu.roll(u, 1, 0) for u in f]
    outer = [pltpu.roll(u, u.shape[0] - 1, 0) for u in f]
    behind = [pltpu.roll(u, 1, 1) for u in f]
    ahead = [pltpu.roll(u, u.shape[1] - 1, 1) for u in f]
    log_rho, vr, vp, _, temper = f
    r_pos = courant * jnp.maximum(vr, 0.0)
    r_neg = courant * jnp.minimum(vr, 0.0)
    cg = courant * inverse
    p_pos = cg * jnp.maximum(vp, 0.0)
    p_neg = cg * jnp.minimum(vp, 0.0)
    vg2 = viscous * inverse * inverse

    def moved(i):
        u = f[i]
        d_in, d_out = u - inner[i], outer[i] - u
        d_back, d_fwd = u - behind[i], ahead[i] - u
        base = u - (r_pos * d_in + r_neg * d_out + p_pos * d_back + p_neg * d_fwd)
        if i == 0:
            return base
        polar = (u + u) - 2.0 * u
        return base + (viscous * ((d_out - d_in) + polar) + vg2 * (d_fwd - d_back))

    def dr(i):
        return (outer[i] - inner[i]) * 0.5

    def dp(i):
        return (ahead[i] - behind[i]) * 0.5

    diverge = dr(1) + inverse * dp(2)
    new_log = moved(0) - courant * diverge
    new_vr = moved(1) - courant * (temper * dr(0) + dr(4)) + (0.5 * cg) * vp * vp
    new_vp = moved(2) - cg * (temper * dp(0) + dp(4)) - (0.5 * cg) * vr * vp
    new_vz = moved(3)
    new_t = moved(4) - (courant * 0.4) * temper * diverge
    return [new_log, new_vr, new_vp, new_vz, new_t]


def rotate(u, index, lag):
    tiles = u.shape[1] // LANES
    g = [
        jnp.take_along_axis(u[:, q * LANES : (q + 1) * LANES], index, axis=1)
        for q in range(tiles)
    ]
    out = []
    for q in range(tiles):
        value = g[(q - (SMAX // LANES + 1)) % tiles]
        for back in range(SMAX // LANES, -1, -1):
            value = jnp.where(lag == back, g[(q - back) % tiles], value)
        out.append(value)
    return jnp.concatenate(out, axis=1)


def kernel(
    n, nr, f_hbm, s_hbm, o_ref, f_ref, s_ref, z, send, recv, edge, send2, recv2,
    ssem, rsem, esend, erecv, ssem2, rsem2, isem,
):
    f_in = pltpu.make_async_copy(f_hbm, f_ref, isem.at[0])
    s_in = pltpu.make_async_copy(s_hbm, s_ref, isem.at[1])
    f_in.start()
    s_in.start()
    r = lax.axis_index("rad")
    t = lax.axis_index("azi")
    tiles = f_ref.shape[3] // SUB
    peers = [lax.rem(t + d, n) for d in range(1, n)]
    top_edge = (t == 0) & (r > 0)
    bottom_edge = (t == n - 1) & (r < nr - 1)

    barrier = pltpu.get_barrier_semaphore()
    for peer in peers:
        pl.semaphore_signal(barrier, inc=1, device_id={"azi": peer})

    @pl.when(top_edge)
    def _():
        for b in range(n):
            pl.semaphore_signal(barrier, inc=1, device_id={"rad": r - 1, "azi": b})

    @pl.when(bottom_edge)
    def _():
        for b in range(n):
            pl.semaphore_signal(barrier, inc=1, device_id={"rad": r + 1, "azi": b})

    sub = lax.broadcasted_iota(jnp.int32, (SUB, LANES), 0)
    lane = lax.broadcasted_iota(jnp.int32, (SUB, LANES), 1)
    low = lane < HALF

    s_in.wait()
    f_in.wait()
    shifts = s_ref[...].astype(jnp.float32)
    rest = jnp.zeros((HALF - STEPS, LANES), jnp.float32)
    stacks = [
        f_ref[0:2, 0].reshape(LANES, LANES),
        f_ref[2:4, 0].reshape(LANES, LANES),
        jnp.concatenate([f_ref[4, 0], shifts, rest], axis=0),
    ]
    for p, stack in enumerate(stacks):
        z[:, p] = stack.T.reshape(tiles, SUB, LANES)

    for k in range(n):
        a, b = 2 * k, 2 * k + 1
        for p in range(2):
            send[k, 2 * p] = z[a, p]
            send[k, 2 * p + 1] = z[b, p]
        send[k, 4] = jnp.where(low, z[a, 2], pltpu.roll(z[b, 2], HALF, 1))
        above, below = max(a - 1, 0), min(b + 1, tiles - 1)
        for p in range(3):
            send[k, 5 + p] = jnp.where(sub >= SUB - STEPS, z[above, p], z[below, p])

    needed = n - 1 + (r > 0).astype(jnp.int32) + (r < nr - 1).astype(jnp.int32)
    pl.semaphore_wait(barrier, needed)

    def edge_copy(which, row, slot, device):
        return pltpu.make_async_remote_copy(
            src_ref=z.at[row], dst_ref=edge.at[slot], send_sem=esend.at[which],
            recv_sem=erecv.at[slot], device_id=device,
        )

    to_inner = edge_copy(0, 0, t, {"rad": r - 1, "azi": n - 1})
    to_outer = edge_copy(1, tiles - 1, t, {"rad": r + 1, "azi": 0})

    @pl.when(r > 0)
    def _():
        to_inner.start()

    @pl.when(r < nr - 1)
    def _():
        to_outer.start()

    copies = []
    for d, peer in enumerate(peers):
        copy = pltpu.make_async_remote_copy(
            src_ref=send.at[peer], dst_ref=recv.at[t], send_sem=ssem.at[d],
            recv_sem=rsem.at[d], device_id={"azi": peer},
        )
        copy.start()
        copies.append(copy)
    recv[t] = send[t]

    rows = 3 * SUB
    width = n * HALF
    row = lax.broadcasted_iota(jnp.int32, (rows, width), 0)
    row = jnp.where(row < 2 * SUB + SUB // 2, row, row - rows)
    row = row + (r * f_ref.shape[3] + t * (2 * SUB))
    total = nr * f_ref.shape[3]
    inside = (row >= 0) & (row < total)
    radius = 1.0 + (row.astype(jnp.float32) + 0.5) / jnp.float32(total)
    inverse = 1.0 / radius

    for copy in copies:
        copy.wait_recv()

    @pl.when(top_edge | bottom_edge)
    def _():
        first = jnp.where(t == 0, SUB - STEPS, 0)
        last = jnp.where(t == 0, SUB, STEPS)
        take = (sub >= first) & (sub < last)
        for b in range(n):
            edge_copy(0, 0, b, {"rad": lax.rem(r + 1, nr), "azi": 0}).wait_recv()
            for p in range(3):
                recv[b, 5 + p] = jnp.where(take, edge[b, p], recv[b, 5 + p])

    fields = [[] for _ in range(FIELDS)]
    for q in range(n // 2):
        got = [halves(recv[2 * q, i], recv[2 * q + 1, i], low) for i in range(8)]
        for p in range(2):
            for h in range(2):
                fields[2 * p + h].append(
                    jnp.concatenate([got[2 * p][h], got[2 * p + 1][h], got[5 + p][h]], axis=0)
                )
        fields[4].append(jnp.concatenate([got[4][0], got[4][1], got[7][0]], axis=0))
    fields = [jnp.where(inside, jnp.concatenate(u, axis=1), 0.0) for u in fields]

    carried = jnp.concatenate([z[2 * t, 2], z[2 * t + 1, 2], recv[0, 7]], axis=0)
    lanes = lax.broadcasted_iota(jnp.int32, (rows, LANES), 1)
    for step in range(STEPS):
        shift = carried[:, HALF + step : HALF + step + 1].astype(jnp.int32)
        shift = jnp.broadcast_to(shift, (rows, LANES))
        whole = jnp.where(shift >= LANES, 1, 0)
        part = shift - whole * LANES
        index = jnp.bitwise_and(lanes - part, LANES - 1)
        lag = whole + jnp.where(lanes < part, 1, 0)
        fields = [jnp.where(inside, u, 0.0) for u in step_update(fields, inverse)]
        fields = [rotate(u, index, lag) for u in fields]

    for q in range(n // 2):
        f = [u[:, q * LANES : (q + 1) * LANES] for u in fields]
        for p in range(2):
            for i in range(2):
                rs = slice(i * SUB, (i + 1) * SUB)
                even, odd = halves(f[2 * p][rs], f[2 * p + 1][rs], low)
                send2[2 * q, 2 * p + i] = even
                send2[2 * q + 1, 2 * p + i] = odd
        even, odd = halves(f[4][:SUB], f[4][SUB : 2 * SUB], low)
        send2[2 * q, 4] = even
        send2[2 * q + 1, 4] = odd

    backs = []
    for d, peer in enumerate(peers):
        copy = pltpu.make_async_remote_copy(
            src_ref=send2.at[peer], dst_ref=recv2.at[t], send_sem=ssem2.at[d],
            recv_sem=rsem2.at[d], device_id={"azi": peer},
        )
        copy.start()
        backs.append(copy)
    recv2[t] = send2[t]

    for copy in copies:
        copy.wait_send()

    @pl.when(r > 0)
    def _():
        to_inner.wait_send()

    @pl.when(r < nr - 1)
    def _():
        to_outer.wait_send()

    for copy in backs:
        copy.wait_recv()

    for p in range(2):
        block = recv2[:, 2 * p : 2 * p + 2].reshape(LANES, LANES)
        o_ref[2 * p : 2 * p + 2, 0] = block.T.reshape(2, HALF, LANES)
    parts = []
    for b in range(n):
        tile = recv2[b, 4]
        parts += [tile, pltpu.roll(tile, HALF, 1)]
    o_ref[4, 0] = jnp.concatenate(parts, axis=0).T[:HALF]

    for copy in backs:
        copy.wait_send()


def by_cycles(n, nr, fields, shifts):
    tiles = fields.shape[3] // SUB
    tile = (SUB, LANES)
    dma = pltpu.SemaphoreType.DMA
    return pl.pallas_call(
        functools.partial(kernel, n, nr),
        out_shape=jax.ShapeDtypeStruct(fields.shape, fields.dtype),
        in_specs=[pl.BlockSpec(memory_space=pltpu.HBM)] * 2,
        out_specs=pl.BlockSpec(memory_space=pltpu.VMEM),
        scratch_shapes=[
            pltpu.VMEM(fields.shape, fields.dtype),
            pltpu.VMEM(shifts.shape, shifts.dtype),
            pltpu.VMEM((tiles, 3) + tile, jnp.float32),
            pltpu.VMEM((n, 8) + tile, jnp.float32),
            pltpu.VMEM((n, 8) + tile, jnp.float32),
            pltpu.VMEM((n, 3) + tile, jnp.float32),
            pltpu.VMEM((n, 5) + tile, jnp.float32),
            pltpu.VMEM((n, 5) + tile, jnp.float32),
            dma((n - 1,)),
            dma((n - 1,)),
            dma((2,)),
            dma((n,)),
            dma((n - 1,)),
            dma((n - 1,)),
            dma((2,)),
        ],
        compiler_params=pltpu.CompilerParams(
            collective_id=0, has_side_effects=True, vmem_limit_bytes=16 * 1024 * 1024
        ),
    )(fields, shifts)


def passed_along(value, axis, steps):
    count = lax.axis_size(axis)
    pairs = [(source, (source + steps) % count) for source in range(count)]
    return lax.ppermute(value, axis, pairs)


def padded_2(value, sides, width, wrap):
    for axis, dim in sides:
        count, length = (lax.axis_size(axis), value.shape[dim])
        up = [(i, (i + 1) % count) for i in range(count if wrap else count - 1)]
        down = [(j, i) for i, j in up]
        last = lax.slice_in_dim(value, length - width, length, axis=dim)
        initial = lax.slice_in_dim(value, 0, width, axis=dim)
        before = lax.ppermute(last, axis, up)
        after = lax.ppermute(initial, axis, down)
        value = jnp.concatenate([before, value, after], axis=dim)
    return value


def update(padded, inverse):
    centre = padded[:, :, 1:-1, 1:-1]
    inner = padded[:, :, 1:-1, :-2]
    outer = padded[:, :, 1:-1, 2:]
    behind = padded[:, :, :-2, 1:-1]
    ahead = padded[:, :, 2:, 1:-1]
    polar_pad = jnp.concatenate([centre, centre, centre], axis=1)
    polar_sum = polar_pad[:, 2:] + polar_pad[:, :-2]
    radial_vel = centre[1]
    azim_vel = centre[2]
    advect = courant * (
        jnp.maximum(radial_vel, 0.0) * (centre - inner)
        + jnp.minimum(radial_vel, 0.0) * (outer - centre)
        + inverse
        * (
            jnp.maximum(azim_vel, 0.0) * (centre - behind)
            + jnp.minimum(azim_vel, 0.0) * (ahead - centre)
        )
    )
    laplace = (
        outer
        + inner
        - 2.0 * centre
        + inverse * inverse * (ahead + behind - 2.0 * centre)
        + (polar_sum - 2.0 * centre)
    )
    radial_diff = (outer - inner) * 0.5
    azim_diff = (ahead - behind) * 0.5
    diverge = radial_diff[1] + inverse * azim_diff[2]
    log_rho = centre[0]
    temper = centre[4]
    new_log = log_rho - advect[0] - courant * diverge
    new_radial = (
        radial_vel
        - advect[1]
        - courant * (temper * radial_diff[0] + radial_diff[4])
        + 0.5 * courant * inverse * azim_vel * azim_vel
        + viscous * laplace[1]
    )
    new_azim = (
        azim_vel
        - advect[2]
        - courant * inverse * (temper * azim_diff[0] + azim_diff[4])
        - 0.5 * courant * inverse * radial_vel * azim_vel
        + viscous * laplace[2]
    )
    new_polar = centre[3] - advect[3] + viscous * laplace[3]
    new_temper = temper - advect[4] - courant * 0.4 * temper * diverge + viscous * laplace[4]
    return jnp.stack([new_log, new_radial, new_azim, new_polar, new_temper])


def rotate_pieces(fields, offsets):
    width = fields.shape[2]
    count = (SMAX + width - 1) // width
    pieces = [fields]
    for blocks in range(1, count + 1):
        pieces.append(passed_along(fields, "azi", blocks))
    extended = jnp.concatenate(pieces[::-1], axis=2)
    nbits = SMAX.bit_length()
    reach = (1 << nbits) - 1
    anchor = count * width
    front = jnp.zeros(fields.shape[:2] + (reach - anchor,) + fields.shape[3:], fields.dtype)
    window = jnp.concatenate([front, extended], axis=2)
    for bit in range(nbits):
        amount = 1 << bit
        length = window.shape[2] - amount
        chosen = offsets // amount % 2 == 1
        window = jnp.where(
            chosen[None, None, None, :], window[:, :, :length], window[:, :, amount:]
        )
    return window


def by_blocks(fields, shifts):
    rows = fields.shape[3]
    total_rows = rows * lax.axis_size("rad")
    row_index = lax.axis_index("rad") * rows + jnp.arange(rows, dtype=jnp.int32)
    radius = 1.0 + (row_index.astype(jnp.float32) + 0.5) / jnp.float32(total_rows)
    inverse = 1.0 / radius
    for step in range(STEPS):
        radial_pad = padded_2(fields, (("rad", 3),), 1, False)
        padded = padded_2(radial_pad, (("azi", 2),), 1, True)
        fields = update(padded, inverse)
        fields = rotate_pieces(fields, shifts[step])
    return fields


def local(fields, shifts):
    n, nr = lax.axis_size("azi"), lax.axis_size("rad")
    count, planes, width, rows = fields.shape
    fits = (count, planes, width, rows) == (FIELDS, 1, HALF, LANES)
    if fits and rows == n * 2 * SUB and n * width > SMAX + LANES:
        return by_cycles(n, nr, fields, shifts)
    return by_blocks(fields, shifts)


def solution(mesh):
    placed = (P(None, None, "azi", "rad"), P(None, "rad"))
    return jax.shard_map(
        local, mesh=mesh, in_specs=placed, out_specs=P(None, None, "azi", "rad"), check_vma=False
    )
```

```python
import functools

import jax
import jax.numpy as jnp
from jax import lax
from jax.experimental import pallas as pl
from jax.experimental.pallas import tpu as pltpu
from jax.sharding import PartitionSpec as P

STEPS = 3
SMAX = 192
FIELDS = 5
LANES = 128
SUB = 8
HALF = 64

courant = 0.2
viscous = 0.1


def halves(a, b, low):
    first = jnp.where(low, a, pltpu.roll(b, HALF, b.ndim - 1))
    second = jnp.where(low, pltpu.roll(a, HALF, a.ndim - 1), b)
    return first, second


def step_update(f, inverse):
    inner = [pltpu.roll(u, 1, 0) for u in f]
    outer = [pltpu.roll(u, u.shape[0] - 1, 0) for u in f]
    behind = [pltpu.roll(u, 1, 1) for u in f]
    ahead = [pltpu.roll(u, u.shape[1] - 1, 1) for u in f]
    log_rho, vr, vp, _, temper = f
    r_pos = courant * jnp.maximum(vr, 0.0)
    r_neg = courant * jnp.minimum(vr, 0.0)
    cg = courant * inverse
    p_pos = cg * jnp.maximum(vp, 0.0)
    p_neg = cg * jnp.minimum(vp, 0.0)
    vg2 = viscous * inverse * inverse

    def moved(i):
        u = f[i]
        d_in, d_out = u - inner[i], outer[i] - u
        d_back, d_fwd = u - behind[i], ahead[i] - u
        base = u - (r_pos * d_in + r_neg * d_out + p_pos * d_back + p_neg * d_fwd)
        if i == 0:
            return base
        polar = (u + u) - 2.0 * u
        return base + (viscous * ((d_out - d_in) + polar) + vg2 * (d_fwd - d_back))

    def dr(i):
        return (outer[i] - inner[i]) * 0.5

    def dp(i):
        return (ahead[i] - behind[i]) * 0.5

    diverge = dr(1) + inverse * dp(2)
    new_log = moved(0) - courant * diverge
    new_vr = moved(1) - courant * (temper * dr(0) + dr(4)) + (0.5 * cg) * vp * vp
    new_vp = moved(2) - cg * (temper * dp(0) + dp(4)) - (0.5 * cg) * vr * vp
    new_vz = moved(3)
    new_t = moved(4) - (courant * 0.4) * temper * diverge
    return [new_log, new_vr, new_vp, new_vz, new_t]


def rotate(u, index, lag):
    tiles = u.shape[1] // LANES
    g = [
        jnp.take_along_axis(u[:, q * LANES : (q + 1) * LANES], index, axis=1)
        for q in range(tiles)
    ]
    out = []
    for q in range(tiles):
        value = g[(q - (SMAX // LANES + 1)) % tiles]
        for back in range(SMAX // LANES, -1, -1):
            value = jnp.where(lag == back, g[(q - back) % tiles], value)
        out.append(value)
    return jnp.concatenate(out, axis=1)


def kernel(
    n, nr, f_hbm, s_hbm, recv2, f_ref, s_ref, z, send, recv, edge, send2,
    ssem, rsem, esend, erecv, ssem2, rsem2, isem,
):
    f_in = pltpu.make_async_copy(f_hbm, f_ref, isem.at[0])
    s_in = pltpu.make_async_copy(s_hbm, s_ref, isem.at[1])
    f_in.start()
    s_in.start()
    r = lax.axis_index("rad")
    t = lax.axis_index("azi")
    tiles = f_ref.shape[3] // SUB
    peers = [lax.rem(t + d, n) for d in range(1, n)]
    top_edge = (t == 0) & (r > 0)
    bottom_edge = (t == n - 1) & (r < nr - 1)

    barrier = pltpu.get_barrier_semaphore()
    for peer in peers:
        pl.semaphore_signal(barrier, inc=1, device_id={"azi": peer})

    @pl.when(top_edge)
    def _():
        for b in range(n):
            pl.semaphore_signal(barrier, inc=1, device_id={"rad": r - 1, "azi": b})

    @pl.when(bottom_edge)
    def _():
        for b in range(n):
            pl.semaphore_signal(barrier, inc=1, device_id={"rad": r + 1, "azi": b})

    sub = lax.broadcasted_iota(jnp.int32, (SUB, LANES), 0)
    lane = lax.broadcasted_iota(jnp.int32, (SUB, LANES), 1)
    low = lane < HALF

    s_in.wait()
    f_in.wait()
    shifts = s_ref[...].astype(jnp.float32)
    rest = jnp.zeros((HALF - STEPS, LANES), jnp.float32)
    stacks = [
        f_ref[0:2, 0].reshape(LANES, LANES),
        f_ref[2:4, 0].reshape(LANES, LANES),
        jnp.concatenate([f_ref[4, 0], shifts, rest], axis=0),
    ]
    for p, stack in enumerate(stacks):
        z[:, p] = stack.T.reshape(tiles, SUB, LANES)

    for k in range(n):
        a, b = 2 * k, 2 * k + 1
        for p in range(2):
            send[k, 2 * p] = z[a, p]
            send[k, 2 * p + 1] = z[b, p]
        send[k, 4] = jnp.where(low, z[a, 2], pltpu.roll(z[b, 2], HALF, 1))
        above, below = max(a - 1, 0), min(b + 1, tiles - 1)
        for p in range(3):
            send[k, 5 + p] = jnp.where(sub >= SUB - STEPS, z[above, p], z[below, p])

    needed = n - 1 + (r > 0).astype(jnp.int32) + (r < nr - 1).astype(jnp.int32)
    pl.semaphore_wait(barrier, needed)

    def edge_copy(which, row, slot, device):
        return pltpu.make_async_remote_copy(
            src_ref=z.at[row], dst_ref=edge.at[slot], send_sem=esend.at[which],
            recv_sem=erecv.at[slot], device_id=device,
        )

    to_inner = edge_copy(0, 0, t, {"rad": r - 1, "azi": n - 1})
    to_outer = edge_copy(1, tiles - 1, t, {"rad": r + 1, "azi": 0})

    @pl.when(r > 0)
    def _():
        to_inner.start()

    @pl.when(r < nr - 1)
    def _():
        to_outer.start()

    copies = []
    for d, peer in enumerate(peers):
        copy = pltpu.make_async_remote_copy(
            src_ref=send.at[peer], dst_ref=recv.at[t], send_sem=ssem.at[d],
            recv_sem=rsem.at[d], device_id={"azi": peer},
        )
        copy.start()
        copies.append(copy)
    recv[t] = send[t]

    rows = 3 * SUB
    width = n * HALF
    row = lax.broadcasted_iota(jnp.int32, (rows, width), 0)
    row = jnp.where(row < 2 * SUB + SUB // 2, row, row - rows)
    row = row + (r * f_ref.shape[3] + t * (2 * SUB))
    total = nr * f_ref.shape[3]
    inside = (row >= 0) & (row < total)
    radius = 1.0 + (row.astype(jnp.float32) + 0.5) / jnp.float32(total)
    inverse = 1.0 / radius

    for copy in copies:
        copy.wait_recv()

    @pl.when(top_edge | bottom_edge)
    def _():
        first = jnp.where(t == 0, SUB - STEPS, 0)
        last = jnp.where(t == 0, SUB, STEPS)
        take = (sub >= first) & (sub < last)
        for b in range(n):
            edge_copy(0, 0, b, {"rad": lax.rem(r + 1, nr), "azi": 0}).wait_recv()
            for p in range(3):
                recv[b, 5 + p] = jnp.where(take, edge[b, p], recv[b, 5 + p])

    fields = [[] for _ in range(FIELDS)]
    for q in range(n // 2):
        got = [halves(recv[2 * q, i], recv[2 * q + 1, i], low) for i in range(8)]
        for p in range(2):
            for h in range(2):
                fields[2 * p + h].append(
                    jnp.concatenate([got[2 * p][h], got[2 * p + 1][h], got[5 + p][h]], axis=0)
                )
        fields[4].append(jnp.concatenate([got[4][0], got[4][1], got[7][0]], axis=0))
    fields = [jnp.where(inside, jnp.concatenate(u, axis=1), 0.0) for u in fields]

    carried = jnp.concatenate([z[2 * t, 2], z[2 * t + 1, 2], recv[0, 7]], axis=0)
    lanes = lax.broadcasted_iota(jnp.int32, (rows, LANES), 1)
    for step in range(STEPS):
        shift = carried[:, HALF + step : HALF + step + 1].astype(jnp.int32)
        shift = jnp.broadcast_to(shift, (rows, LANES))
        whole = jnp.where(shift >= LANES, 1, 0)
        part = shift - whole * LANES
        index = jnp.bitwise_and(lanes - part, LANES - 1)
        lag = whole + jnp.where(lanes < part, 1, 0)
        fields = [jnp.where(inside, u, 0.0) for u in step_update(fields, inverse)]
        fields = [rotate(u, index, lag) for u in fields]

    for q in range(n // 2):
        f = [u[:, q * LANES : (q + 1) * LANES] for u in fields]
        for p in range(2):
            for i in range(2):
                rs = slice(i * SUB, (i + 1) * SUB)
                even, odd = halves(f[2 * p][rs], f[2 * p + 1][rs], low)
                send2[2 * q, 2 * p + i] = even
                send2[2 * q + 1, 2 * p + i] = odd
        even, odd = halves(f[4][:SUB], f[4][SUB : 2 * SUB], low)
        send2[2 * q, 4] = even
        send2[2 * q + 1, 4] = odd

    backs = []
    for d, peer in enumerate(peers):
        copy = pltpu.make_async_remote_copy(
            src_ref=send2.at[peer], dst_ref=recv2.at[t], send_sem=ssem2.at[d],
            recv_sem=rsem2.at[d], device_id={"azi": peer},
        )
        copy.start()
        backs.append(copy)
    recv2[t] = send2[t]

    for copy in copies:
        copy.wait_send()

    @pl.when(r > 0)
    def _():
        to_inner.wait_send()

    @pl.when(r < nr - 1)
    def _():
        to_outer.wait_send()

    for copy in backs:
        copy.wait_recv()

    for copy in backs:
        copy.wait_send()


def to_cells(got, o_hbm, out, sem):
    n = got.shape[0]
    writes = []
    for p in range(3):
        fs = slice(2 * p, min(2 * p + 2, FIELDS))
        if p < 2:
            block = got[:, 2 * p : 2 * p + 2].reshape(LANES, LANES)
            out[fs, 0] = block.T.reshape(2, HALF, LANES)
        else:
            parts = []
            for b in range(n):
                tile = got[b, 4]
                parts += [tile, pltpu.roll(tile, HALF, 1)]
            out[4, 0] = jnp.concatenate(parts, axis=0).T[:HALF]
        write = pltpu.make_async_copy(out.at[fs], o_hbm.at[fs], sem.at[p])
        write.start()
        writes.append(write)
    for write in writes:
        write.wait()


def by_cycles(n, nr, fields, shifts):
    tiles = fields.shape[3] // SUB
    tile = (SUB, LANES)
    dma = pltpu.SemaphoreType.DMA
    got = pl.pallas_call(
        functools.partial(kernel, n, nr),
        out_shape=pltpu.VMEM((n, 5) + tile, jnp.float32),
        in_specs=[pl.BlockSpec(memory_space=pltpu.HBM)] * 2,
        out_specs=pl.BlockSpec(memory_space=pltpu.VMEM),
        scratch_shapes=[
            pltpu.VMEM(fields.shape, fields.dtype),
            pltpu.VMEM(shifts.shape, shifts.dtype),
            pltpu.VMEM((tiles, 3) + tile, jnp.float32),
            pltpu.VMEM((n, 8) + tile, jnp.float32),
            pltpu.VMEM((n, 8) + tile, jnp.float32),
            pltpu.VMEM((n, 3) + tile, jnp.float32),
            pltpu.VMEM((n, 5) + tile, jnp.float32),
            dma((n - 1,)),
            dma((n - 1,)),
            dma((2,)),
            dma((n,)),
            dma((n - 1,)),
            dma((n - 1,)),
            dma((2,)),
        ],
        compiler_params=pltpu.CompilerParams(
            collective_id=0, has_side_effects=True, vmem_limit_bytes=16 * 1024 * 1024
        ),
    )(
        pltpu.with_memory_space_constraint(fields, pltpu.HBM),
        pltpu.with_memory_space_constraint(shifts, pltpu.HBM),
    )
    return pl.pallas_call(
        to_cells,
        out_shape=jax.ShapeDtypeStruct(fields.shape, fields.dtype),
        in_specs=[pl.BlockSpec(memory_space=pltpu.VMEM)],
        out_specs=pl.BlockSpec(memory_space=pltpu.HBM),
        scratch_shapes=[pltpu.VMEM(fields.shape, fields.dtype), dma((3,))],
        compiler_params=pltpu.CompilerParams(vmem_limit_bytes=16 * 1024 * 1024),
    )(got)


def passed_along(value, axis, steps):
    count = lax.axis_size(axis)
    pairs = [(source, (source + steps) % count) for source in range(count)]
    return lax.ppermute(value, axis, pairs)


def padded_2(value, sides, width, wrap):
    for axis, dim in sides:
        count, length = (lax.axis_size(axis), value.shape[dim])
        up = [(i, (i + 1) % count) for i in range(count if wrap else count - 1)]
        down = [(j, i) for i, j in up]
        last = lax.slice_in_dim(value, length - width, length, axis=dim)
        initial = lax.slice_in_dim(value, 0, width, axis=dim)
        before = lax.ppermute(last, axis, up)
        after = lax.ppermute(initial, axis, down)
        value = jnp.concatenate([before, value, after], axis=dim)
    return value


def update(padded, inverse):
    centre = padded[:, :, 1:-1, 1:-1]
    inner = padded[:, :, 1:-1, :-2]
    outer = padded[:, :, 1:-1, 2:]
    behind = padded[:, :, :-2, 1:-1]
    ahead = padded[:, :, 2:, 1:-1]
    polar_pad = jnp.concatenate([centre, centre, centre], axis=1)
    polar_sum = polar_pad[:, 2:] + polar_pad[:, :-2]
    radial_vel = centre[1]
    azim_vel = centre[2]
    advect = courant * (
        jnp.maximum(radial_vel, 0.0) * (centre - inner)
        + jnp.minimum(radial_vel, 0.0) * (outer - centre)
        + inverse
        * (
            jnp.maximum(azim_vel, 0.0) * (centre - behind)
            + jnp.minimum(azim_vel, 0.0) * (ahead - centre)
        )
    )
    laplace = (
        outer
        + inner
        - 2.0 * centre
        + inverse * inverse * (ahead + behind - 2.0 * centre)
        + (polar_sum - 2.0 * centre)
    )
    radial_diff = (outer - inner) * 0.5
    azim_diff = (ahead - behind) * 0.5
    diverge = radial_diff[1] + inverse * azim_diff[2]
    log_rho = centre[0]
    temper = centre[4]
    new_log = log_rho - advect[0] - courant * diverge
    new_radial = (
        radial_vel
        - advect[1]
        - courant * (temper * radial_diff[0] + radial_diff[4])
        + 0.5 * courant * inverse * azim_vel * azim_vel
        + viscous * laplace[1]
    )
    new_azim = (
        azim_vel
        - advect[2]
        - courant * inverse * (temper * azim_diff[0] + azim_diff[4])
        - 0.5 * courant * inverse * radial_vel * azim_vel
        + viscous * laplace[2]
    )
    new_polar = centre[3] - advect[3] + viscous * laplace[3]
    new_temper = temper - advect[4] - courant * 0.4 * temper * diverge + viscous * laplace[4]
    return jnp.stack([new_log, new_radial, new_azim, new_polar, new_temper])


def rotate_pieces(fields, offsets):
    width = fields.shape[2]
    count = (SMAX + width - 1) // width
    pieces = [fields]
    for blocks in range(1, count + 1):
        pieces.append(passed_along(fields, "azi", blocks))
    extended = jnp.concatenate(pieces[::-1], axis=2)
    nbits = SMAX.bit_length()
    reach = (1 << nbits) - 1
    anchor = count * width
    front = jnp.zeros(fields.shape[:2] + (reach - anchor,) + fields.shape[3:], fields.dtype)
    window = jnp.concatenate([front, extended], axis=2)
    for bit in range(nbits):
        amount = 1 << bit
        length = window.shape[2] - amount
        chosen = offsets // amount % 2 == 1
        window = jnp.where(
            chosen[None, None, None, :], window[:, :, :length], window[:, :, amount:]
        )
    return window


def by_blocks(fields, shifts):
    rows = fields.shape[3]
    total_rows = rows * lax.axis_size("rad")
    row_index = lax.axis_index("rad") * rows + jnp.arange(rows, dtype=jnp.int32)
    radius = 1.0 + (row_index.astype(jnp.float32) + 0.5) / jnp.float32(total_rows)
    inverse = 1.0 / radius
    for step in range(STEPS):
        radial_pad = padded_2(fields, (("rad", 3),), 1, False)
        padded = padded_2(radial_pad, (("azi", 2),), 1, True)
        fields = update(padded, inverse)
        fields = rotate_pieces(fields, shifts[step])
    return fields


def local(fields, shifts):
    n, nr = lax.axis_size("azi"), lax.axis_size("rad")
    count, planes, width, rows = fields.shape
    fits = (count, planes, width, rows) == (FIELDS, 1, HALF, LANES)
    if fits and rows == n * 2 * SUB and n * width > SMAX + LANES:
        return by_cycles(n, nr, fields, shifts)
    return by_blocks(fields, shifts)


def solution(mesh):
    placed = (P(None, None, "azi", "rad"), P(None, "rad"))
    return jax.shard_map(
        local, mesh=mesh, in_specs=placed, out_specs=P(None, None, "azi", "rad"), check_vma=False
    )
```

```python
import functools

import jax
import jax.numpy as jnp
from jax import lax
from jax.experimental import pallas as pl
from jax.experimental.pallas import tpu as pltpu
from jax.sharding import PartitionSpec as P

STEPS = 3
SMAX = 192
FIELDS = 5
LANES = 128
SUB = 8
HALF = 64
PAIRS = (slice(0, 2), slice(2, 4), slice(4, 5))
THERE = (slice(0, 3), slice(3, 6), slice(6, 8))
BACK = (slice(0, 2), slice(2, 4), slice(4, 5))

courant = 0.2
viscous = 0.1


def halves(a, b, low):
    first = jnp.where(low, a, pltpu.roll(b, HALF, b.ndim - 1))
    second = jnp.where(low, pltpu.roll(a, HALF, a.ndim - 1), b)
    return first, second


def updates(f, inverse, rows):
    inner = [pltpu.roll(u, 1, 0)[:rows] for u in f]
    outer = [pltpu.roll(u, u.shape[0] - 1, 0)[:rows] for u in f]
    f = [u[:rows] for u in f]
    inverse = inverse[:rows]
    behind = [pltpu.roll(u, 1, 1) for u in f]
    ahead = [pltpu.roll(u, u.shape[1] - 1, 1) for u in f]
    _, vr, vp, _, temper = f
    r_pos = courant * jnp.maximum(vr, 0.0)
    r_neg = courant * jnp.minimum(vr, 0.0)
    cg = courant * inverse
    p_pos = cg * jnp.maximum(vp, 0.0)
    p_neg = cg * jnp.minimum(vp, 0.0)
    vg2 = viscous * inverse * inverse

    def moved(i):
        u = f[i]
        d_in, d_out = u - inner[i], outer[i] - u
        d_back, d_fwd = u - behind[i], ahead[i] - u
        base = u - (r_pos * d_in + r_neg * d_out + p_pos * d_back + p_neg * d_fwd)
        if i == 0:
            return base
        polar = (u + u) - 2.0 * u
        return base + (viscous * ((d_out - d_in) + polar) + vg2 * (d_fwd - d_back))

    def dr(i):
        return (outer[i] - inner[i]) * 0.5

    def dp(i):
        return (ahead[i] - behind[i]) * 0.5

    diverge = dr(1) + inverse * dp(2)
    return [
        lambda: moved(0) - courant * diverge,
        lambda: moved(1) - courant * (temper * dr(0) + dr(4)) + (0.5 * cg) * vp * vp,
        lambda: moved(2) - cg * (temper * dp(0) + dp(4)) - (0.5 * cg) * vr * vp,
        lambda: moved(3),
        lambda: moved(4) - (courant * 0.4) * temper * diverge,
    ]


def rotate(u, index, lag):
    tiles = u.shape[1] // LANES
    g = [
        jnp.take_along_axis(u[:, q * LANES : (q + 1) * LANES], index, axis=1)
        for q in range(tiles)
    ]
    out = []
    for q in range(tiles):
        value = g[(q - (SMAX // LANES + 1)) % tiles]
        for back in range(SMAX // LANES, -1, -1):
            value = jnp.where(lag == back, g[(q - back) % tiles], value)
        out.append(value)
    return jnp.concatenate(out, axis=1)


def kernel(
    n, nr, f_hbm, s_hbm, recv2, f_ref, s_ref, z, send, recv, edge, send2,
    ssem, rsem, esend, erecv, ssem2, rsem2, isem,
):
    loads = [
        pltpu.make_async_copy(f_hbm.at[fs], f_ref.at[fs], isem.at[p])
        for p, fs in enumerate(PAIRS)
    ]
    loads.append(pltpu.make_async_copy(s_hbm, s_ref, isem.at[len(PAIRS)]))
    for load in loads:
        load.start()
    r = lax.axis_index("rad")
    t = lax.axis_index("azi")
    tiles = f_ref.shape[3] // SUB
    peers = [lax.rem(t + d, n) for d in range(1, n)]
    top_edge = (t == 0) & (r > 0)
    bottom_edge = (t == n - 1) & (r < nr - 1)

    barrier = pltpu.get_barrier_semaphore()
    for peer in peers:
        pl.semaphore_signal(barrier, inc=1, device_id={"azi": peer})

    @pl.when(top_edge)
    def _():
        for b in range(n):
            pl.semaphore_signal(barrier, inc=1, device_id={"rad": r - 1, "azi": b})

    @pl.when(bottom_edge)
    def _():
        for b in range(n):
            pl.semaphore_signal(barrier, inc=1, device_id={"rad": r + 1, "azi": b})

    sub = lax.broadcasted_iota(jnp.int32, (SUB, LANES), 0)
    lane = lax.broadcasted_iota(jnp.int32, (SUB, LANES), 1)
    low = lane < HALF

    def edge_copy(which, row, slot, device):
        return pltpu.make_async_remote_copy(
            src_ref=z.at[row], dst_ref=edge.at[slot], send_sem=esend.at[which],
            recv_sem=erecv.at[slot], device_id=device,
        )

    to_inner = edge_copy(0, 0, t, {"rad": r - 1, "azi": n - 1})
    to_outer = edge_copy(1, tiles - 1, t, {"rad": r + 1, "azi": 0})

    copies = []
    for p, fs in enumerate(PAIRS):
        loads[p].wait()
        if p < 2:
            stack = f_ref[fs, 0].reshape(LANES, LANES)
        else:
            loads[3].wait()
            shifts = s_ref[...].astype(jnp.float32)
            rest = jnp.zeros((HALF - STEPS, LANES), jnp.float32)
            stack = jnp.concatenate([f_ref[4, 0], shifts, rest], axis=0)
        z[:, p] = stack.T.reshape(tiles, SUB, LANES)
        for k in range(n):
            a, b = 2 * k, 2 * k + 1
            if p < 2:
                send[k, 3 * p] = z[a, p]
                send[k, 3 * p + 1] = z[b, p]
            else:
                send[k, 6] = jnp.where(low, z[a, p], pltpu.roll(z[b, p], HALF, 1))
            above, below = max(a - 1, 0), min(b + 1, tiles - 1)
            halo = jnp.where(sub >= SUB - STEPS, z[above, p], z[below, p])
            send[k, THERE[p].stop - 1] = halo

        if p == 0:
            needed = n - 1 + (r > 0).astype(jnp.int32) + (r < nr - 1).astype(jnp.int32)
            pl.semaphore_wait(barrier, needed)
        if p == 2:

            @pl.when(r > 0)
            def _():
                to_inner.start()

            @pl.when(r < nr - 1)
            def _():
                to_outer.start()

        for d, peer in enumerate(peers):
            copy = pltpu.make_async_remote_copy(
                src_ref=send.at[peer, THERE[p]], dst_ref=recv.at[t, THERE[p]],
                send_sem=ssem.at[p, d], recv_sem=rsem.at[p, d], device_id={"azi": peer},
            )
            copy.start()
            copies.append(copy)
    recv[t] = send[t]

    rows = 3 * SUB
    width = n * HALF
    row = lax.broadcasted_iota(jnp.int32, (rows, width), 0)
    row = jnp.where(row < 2 * SUB + SUB // 2, row, row - rows)
    row = row + (r * f_ref.shape[3] + t * (2 * SUB))
    total = nr * f_ref.shape[3]
    inside = (row >= 0) & (row < total)
    radius = 1.0 + (row.astype(jnp.float32) + 0.5) / jnp.float32(total)
    inverse = 1.0 / radius

    for copy in copies:
        copy.wait_recv()

    @pl.when(top_edge | bottom_edge)
    def _():
        first = jnp.where(t == 0, SUB - STEPS, 0)
        last = jnp.where(t == 0, SUB, STEPS)
        take = (sub >= first) & (sub < last)
        for b in range(n):
            edge_copy(0, 0, b, {"rad": lax.rem(r + 1, nr), "azi": 0}).wait_recv()
            for p in range(3):
                at = THERE[p].stop - 1
                recv[b, at] = jnp.where(take, edge[b, p], recv[b, at])

    fields = [[] for _ in range(FIELDS)]
    for q in range(n // 2):
        got = [halves(recv[2 * q, i], recv[2 * q + 1, i], low) for i in range(8)]
        for p in range(2):
            for h in range(2):
                fields[2 * p + h].append(
                    jnp.concatenate([got[3 * p + i][h] for i in range(3)], axis=0)
                )
        fields[4].append(jnp.concatenate([got[6][0], got[6][1], got[7][0]], axis=0))
    fields = [jnp.where(inside, jnp.concatenate(u, axis=1), 0.0) for u in fields]

    carried = jnp.concatenate([z[2 * t, 2], z[2 * t + 1, 2], recv[0, 7]], axis=0)
    lanes = lax.broadcasted_iota(jnp.int32, (rows, LANES), 1)
    for step in range(STEPS):
        shift = carried[:, HALF + step : HALF + step + 1].astype(jnp.int32)
        shift = jnp.broadcast_to(shift, (rows, LANES))
        whole = jnp.where(shift >= LANES, 1, 0)
        part = shift - whole * LANES
        index = jnp.bitwise_and(lanes - part, LANES - 1)
        lag = whole + jnp.where(lanes < part, 1, 0)
        if step < STEPS - 1:
            fields = [jnp.where(inside, new(), 0.0) for new in updates(fields, inverse, rows)]
            fields = [rotate(u, index, lag) for u in fields]

    own = 2 * SUB
    news = updates(fields, inverse, own)
    backs = []
    for p, fs in enumerate(PAIRS):
        pair = [rotate(new(), index[:own], lag[:own]) for new in news[fs]]
        for q in range(n // 2):
            f = [u[:, q * LANES : (q + 1) * LANES] for u in pair]
            if p < 2:
                for i in range(2):
                    rs = slice(i * SUB, (i + 1) * SUB)
                    even, odd = halves(f[0][rs], f[1][rs], low)
                    send2[2 * q, 2 * p + i] = even
                    send2[2 * q + 1, 2 * p + i] = odd
            else:
                even, odd = halves(f[0][:SUB], f[0][SUB:], low)
                send2[2 * q, 4] = even
                send2[2 * q + 1, 4] = odd
        for d, peer in enumerate(peers):
            copy = pltpu.make_async_remote_copy(
                src_ref=send2.at[peer, BACK[p]], dst_ref=recv2.at[t, BACK[p]],
                send_sem=ssem2.at[p, d], recv_sem=rsem2.at[p, d], device_id={"azi": peer},
            )
            copy.start()
            backs.append(copy)
    recv2[t] = send2[t]

    for copy in copies:
        copy.wait_send()

    @pl.when(r > 0)
    def _():
        to_inner.wait_send()

    @pl.when(r < nr - 1)
    def _():
        to_outer.wait_send()

    for copy in backs:
        copy.wait_recv()

    for copy in backs:
        copy.wait_send()


def to_cells(got, o_hbm, out, sem):
    n = got.shape[0]
    writes = []
    for p in range(3):
        fs = slice(2 * p, min(2 * p + 2, FIELDS))
        if p < 2:
            block = got[:, 2 * p : 2 * p + 2].reshape(LANES, LANES)
            out[fs, 0] = block.T.reshape(2, HALF, LANES)
        else:
            parts = []
            for b in range(n):
                tile = got[b, 4]
                parts += [tile, pltpu.roll(tile, HALF, 1)]
            out[4, 0] = jnp.concatenate(parts, axis=0).T[:HALF]
        write = pltpu.make_async_copy(out.at[fs], o_hbm.at[fs], sem.at[p])
        write.start()
        writes.append(write)
    for write in writes:
        write.wait()


def by_cycles(n, nr, fields, shifts):
    tiles = fields.shape[3] // SUB
    tile = (SUB, LANES)
    dma = pltpu.SemaphoreType.DMA
    got = pl.pallas_call(
        functools.partial(kernel, n, nr),
        out_shape=pltpu.VMEM((n, 5) + tile, jnp.float32),
        in_specs=[pl.BlockSpec(memory_space=pltpu.HBM)] * 2,
        out_specs=pl.BlockSpec(memory_space=pltpu.VMEM),
        scratch_shapes=[
            pltpu.VMEM(fields.shape, fields.dtype),
            pltpu.VMEM(shifts.shape, shifts.dtype),
            pltpu.VMEM((tiles, 3) + tile, jnp.float32),
            pltpu.VMEM((n, 8) + tile, jnp.float32),
            pltpu.VMEM((n, 8) + tile, jnp.float32),
            pltpu.VMEM((n, 3) + tile, jnp.float32),
            pltpu.VMEM((n, 5) + tile, jnp.float32),
            dma((3, n - 1)),
            dma((3, n - 1)),
            dma((2,)),
            dma((n,)),
            dma((3, n - 1)),
            dma((3, n - 1)),
            dma((4,)),
        ],
        compiler_params=pltpu.CompilerParams(
            collective_id=0, has_side_effects=True, vmem_limit_bytes=16 * 1024 * 1024
        ),
    )(
        pltpu.with_memory_space_constraint(fields, pltpu.HBM),
        pltpu.with_memory_space_constraint(shifts, pltpu.HBM),
    )
    return pl.pallas_call(
        to_cells,
        out_shape=jax.ShapeDtypeStruct(fields.shape, fields.dtype),
        in_specs=[pl.BlockSpec(memory_space=pltpu.VMEM)],
        out_specs=pl.BlockSpec(memory_space=pltpu.HBM),
        scratch_shapes=[pltpu.VMEM(fields.shape, fields.dtype), dma((3,))],
        compiler_params=pltpu.CompilerParams(vmem_limit_bytes=16 * 1024 * 1024),
    )(got)


def passed_along(value, axis, steps):
    count = lax.axis_size(axis)
    pairs = [(source, (source + steps) % count) for source in range(count)]
    return lax.ppermute(value, axis, pairs)


def padded_2(value, sides, width, wrap):
    for axis, dim in sides:
        count, length = (lax.axis_size(axis), value.shape[dim])
        up = [(i, (i + 1) % count) for i in range(count if wrap else count - 1)]
        down = [(j, i) for i, j in up]
        last = lax.slice_in_dim(value, length - width, length, axis=dim)
        initial = lax.slice_in_dim(value, 0, width, axis=dim)
        before = lax.ppermute(last, axis, up)
        after = lax.ppermute(initial, axis, down)
        value = jnp.concatenate([before, value, after], axis=dim)
    return value


def update(padded, inverse):
    centre = padded[:, :, 1:-1, 1:-1]
    inner = padded[:, :, 1:-1, :-2]
    outer = padded[:, :, 1:-1, 2:]
    behind = padded[:, :, :-2, 1:-1]
    ahead = padded[:, :, 2:, 1:-1]
    polar_pad = jnp.concatenate([centre, centre, centre], axis=1)
    polar_sum = polar_pad[:, 2:] + polar_pad[:, :-2]
    radial_vel = centre[1]
    azim_vel = centre[2]
    advect = courant * (
        jnp.maximum(radial_vel, 0.0) * (centre - inner)
        + jnp.minimum(radial_vel, 0.0) * (outer - centre)
        + inverse
        * (
            jnp.maximum(azim_vel, 0.0) * (centre - behind)
            + jnp.minimum(azim_vel, 0.0) * (ahead - centre)
        )
    )
    laplace = (
        outer
        + inner
        - 2.0 * centre
        + inverse * inverse * (ahead + behind - 2.0 * centre)
        + (polar_sum - 2.0 * centre)
    )
    radial_diff = (outer - inner) * 0.5
    azim_diff = (ahead - behind) * 0.5
    diverge = radial_diff[1] + inverse * azim_diff[2]
    log_rho = centre[0]
    temper = centre[4]
    new_log = log_rho - advect[0] - courant * diverge
    new_radial = (
        radial_vel
        - advect[1]
        - courant * (temper * radial_diff[0] + radial_diff[4])
        + 0.5 * courant * inverse * azim_vel * azim_vel
        + viscous * laplace[1]
    )
    new_azim = (
        azim_vel
        - advect[2]
        - courant * inverse * (temper * azim_diff[0] + azim_diff[4])
        - 0.5 * courant * inverse * radial_vel * azim_vel
        + viscous * laplace[2]
    )
    new_polar = centre[3] - advect[3] + viscous * laplace[3]
    new_temper = temper - advect[4] - courant * 0.4 * temper * diverge + viscous * laplace[4]
    return jnp.stack([new_log, new_radial, new_azim, new_polar, new_temper])


def rotate_pieces(fields, offsets):
    width = fields.shape[2]
    count = (SMAX + width - 1) // width
    pieces = [fields]
    for blocks in range(1, count + 1):
        pieces.append(passed_along(fields, "azi", blocks))
    extended = jnp.concatenate(pieces[::-1], axis=2)
    nbits = SMAX.bit_length()
    reach = (1 << nbits) - 1
    anchor = count * width
    front = jnp.zeros(fields.shape[:2] + (reach - anchor,) + fields.shape[3:], fields.dtype)
    window = jnp.concatenate([front, extended], axis=2)
    for bit in range(nbits):
        amount = 1 << bit
        length = window.shape[2] - amount
        chosen = offsets // amount % 2 == 1
        window = jnp.where(
            chosen[None, None, None, :], window[:, :, :length], window[:, :, amount:]
        )
    return window


def by_blocks(fields, shifts):
    rows = fields.shape[3]
    total_rows = rows * lax.axis_size("rad")
    row_index = lax.axis_index("rad") * rows + jnp.arange(rows, dtype=jnp.int32)
    radius = 1.0 + (row_index.astype(jnp.float32) + 0.5) / jnp.float32(total_rows)
    inverse = 1.0 / radius
    for step in range(STEPS):
        radial_pad = padded_2(fields, (("rad", 3),), 1, False)
        padded = padded_2(radial_pad, (("azi", 2),), 1, True)
        fields = update(padded, inverse)
        fields = rotate_pieces(fields, shifts[step])
    return fields


def local(fields, shifts):
    n, nr = lax.axis_size("azi"), lax.axis_size("rad")
    count, planes, width, rows = fields.shape
    fits = (count, planes, width, rows) == (FIELDS, 1, HALF, LANES)
    if fits and rows == n * 2 * SUB and n * width > SMAX + LANES:
        return by_cycles(n, nr, fields, shifts)
    return by_blocks(fields, shifts)


def solution(mesh):
    placed = (P(None, None, "azi", "rad"), P(None, "rad"))
    return jax.shard_map(
        local, mesh=mesh, in_specs=placed, out_specs=P(None, None, "azi", "rad"), check_vma=False
    )
```

```python
import functools

import jax
import jax.numpy as jnp
from jax import lax
from jax.experimental import pallas as pl
from jax.experimental.pallas import tpu as pltpu
from jax.sharding import PartitionSpec as P

STEPS = 3
SMAX = 192
FIELDS = 5
LANES = 128
SUB = 8
HALF = 64
PAIRS = (slice(0, 2), slice(2, 4), slice(4, 5))
THERE = (slice(0, 3), slice(3, 6), slice(6, 8))

courant = 0.2
viscous = 0.1


def halves(a, b, low):
    first = jnp.where(low, a, pltpu.roll(b, HALF, b.ndim - 1))
    second = jnp.where(low, pltpu.roll(a, HALF, a.ndim - 1), b)
    return first, second


def updates(f, inverse, rows):
    inner = [pltpu.roll(u, 1, 0)[:rows] for u in f]
    outer = [pltpu.roll(u, u.shape[0] - 1, 0)[:rows] for u in f]
    f = [u[:rows] for u in f]
    inverse = inverse[:rows]
    behind = [pltpu.roll(u, 1, 1) for u in f]
    ahead = [pltpu.roll(u, u.shape[1] - 1, 1) for u in f]
    _, vr, vp, _, temper = f
    r_pos = courant * jnp.maximum(vr, 0.0)
    r_neg = courant * jnp.minimum(vr, 0.0)
    cg = courant * inverse
    p_pos = cg * jnp.maximum(vp, 0.0)
    p_neg = cg * jnp.minimum(vp, 0.0)
    vg2 = viscous * inverse * inverse

    def moved(i):
        u = f[i]
        d_in, d_out = u - inner[i], outer[i] - u
        d_back, d_fwd = u - behind[i], ahead[i] - u
        base = u - (r_pos * d_in + r_neg * d_out + p_pos * d_back + p_neg * d_fwd)
        if i == 0:
            return base
        polar = (u + u) - 2.0 * u
        return base + (viscous * ((d_out - d_in) + polar) + vg2 * (d_fwd - d_back))

    def dr(i):
        return (outer[i] - inner[i]) * 0.5

    def dp(i):
        return (ahead[i] - behind[i]) * 0.5

    diverge = dr(1) + inverse * dp(2)
    return [
        lambda: moved(0) - courant * diverge,
        lambda: moved(1) - courant * (temper * dr(0) + dr(4)) + (0.5 * cg) * vp * vp,
        lambda: moved(2) - cg * (temper * dp(0) + dp(4)) - (0.5 * cg) * vr * vp,
        lambda: moved(3),
        lambda: moved(4) - (courant * 0.4) * temper * diverge,
    ]


def rotate(u, index, lag):
    tiles = u.shape[1] // LANES
    g = [
        jnp.take_along_axis(u[:, q * LANES : (q + 1) * LANES], index, axis=1)
        for q in range(tiles)
    ]
    out = []
    for q in range(tiles):
        value = g[(q - (SMAX // LANES + 1)) % tiles]
        for back in range(SMAX // LANES, -1, -1):
            value = jnp.where(lag == back, g[(q - back) % tiles], value)
        out.append(value)
    return jnp.concatenate(out, axis=1)


def kernel(
    n, nr, f_hbm, s_hbm, recv2, f_ref, s_ref, z, send, recv, edge, send2,
    ssem, rsem, esend, erecv, ssem2, rsem2, isem,
):
    loads = [
        pltpu.make_async_copy(f_hbm, f_ref, isem.at[0]),
        pltpu.make_async_copy(s_hbm, s_ref, isem.at[1]),
    ]
    for load in loads:
        load.start()
    r = lax.axis_index("rad")
    t = lax.axis_index("azi")
    tiles = f_ref.shape[3] // SUB
    peers = [lax.rem(t + d, n) for d in range(1, n)]
    top_edge = (t == 0) & (r > 0)
    bottom_edge = (t == n - 1) & (r < nr - 1)

    barrier = pltpu.get_barrier_semaphore()
    for peer in peers:
        pl.semaphore_signal(barrier, inc=1, device_id={"azi": peer})

    @pl.when(top_edge)
    def _():
        for b in range(n):
            pl.semaphore_signal(barrier, inc=1, device_id={"rad": r - 1, "azi": b})

    @pl.when(bottom_edge)
    def _():
        for b in range(n):
            pl.semaphore_signal(barrier, inc=1, device_id={"rad": r + 1, "azi": b})

    sub = lax.broadcasted_iota(jnp.int32, (SUB, LANES), 0)
    lane = lax.broadcasted_iota(jnp.int32, (SUB, LANES), 1)
    low = lane < HALF

    def edge_copy(which, row, slot, device):
        return pltpu.make_async_remote_copy(
            src_ref=z.at[row], dst_ref=edge.at[slot], send_sem=esend.at[which],
            recv_sem=erecv, device_id=device,
        )

    to_inner = edge_copy(0, 0, t, {"rad": r - 1, "azi": n - 1})
    to_outer = edge_copy(1, tiles - 1, t, {"rad": r + 1, "azi": 0})

    for load in loads:
        load.wait()
    for p, fs in enumerate(PAIRS):
        if p < 2:
            stack = f_ref[fs, 0].reshape(LANES, LANES)
        else:
            shifts = s_ref[...].astype(jnp.float32)
            rest = jnp.zeros((HALF - STEPS, LANES), jnp.float32)
            stack = jnp.concatenate([f_ref[4, 0], shifts, rest], axis=0)
        z[:, p] = stack.T.reshape(tiles, SUB, LANES)
        for k in range(n):
            a, b = 2 * k, 2 * k + 1
            if p < 2:
                send[k, 3 * p] = z[a, p]
                send[k, 3 * p + 1] = z[b, p]
            else:
                send[k, 6] = jnp.where(low, z[a, p], pltpu.roll(z[b, p], HALF, 1))
            above, below = max(a - 1, 0), min(b + 1, tiles - 1)
            halo = jnp.where(sub >= SUB - STEPS, z[above, p], z[below, p])
            send[k, THERE[p].stop - 1] = halo

    needed = n - 1 + (r > 0).astype(jnp.int32) + (r < nr - 1).astype(jnp.int32)
    pl.semaphore_wait(barrier, needed)

    @pl.when(r > 0)
    def _():
        to_inner.start()

    @pl.when(r < nr - 1)
    def _():
        to_outer.start()

    def to_peer(src, dst, send_sem, recv_sem, peer):
        return pltpu.make_async_remote_copy(
            src_ref=src, dst_ref=dst, send_sem=send_sem, recv_sem=recv_sem,
            device_id={"azi": peer},
        )

    for peer in peers:
        to_peer(send.at[peer], recv.at[t], ssem, rsem, peer).start()
    there = to_peer(send.at[1:], recv.at[1:], ssem, rsem, peers[0])
    recv[t] = send[t]

    rows = 3 * SUB
    width = n * HALF
    row = lax.broadcasted_iota(jnp.int32, (rows, width), 0)
    row = jnp.where(row < 2 * SUB + SUB // 2, row, row - rows)
    row = row + (r * f_ref.shape[3] + t * (2 * SUB))
    total = nr * f_ref.shape[3]
    inside = (row >= 0) & (row < total)
    radius = 1.0 + (row.astype(jnp.float32) + 0.5) / jnp.float32(total)
    inverse = 1.0 / radius

    there.wait_recv()

    @pl.when(top_edge | bottom_edge)
    def _():
        first = jnp.where(t == 0, SUB - STEPS, 0)
        last = jnp.where(t == 0, SUB, STEPS)
        take = (sub >= first) & (sub < last)
        pltpu.make_async_remote_copy(
            src_ref=z.at[:n], dst_ref=edge, send_sem=esend.at[0], recv_sem=erecv,
            device_id={"rad": lax.rem(r + 1, nr)},
        ).wait_recv()
        for b in range(n):
            for p in range(3):
                at = THERE[p].stop - 1
                recv[b, at] = jnp.where(take, edge[b, p], recv[b, at])

    fields = [[] for _ in range(FIELDS)]
    for q in range(n // 2):
        got = [halves(recv[2 * q, i], recv[2 * q + 1, i], low) for i in range(8)]
        for p in range(2):
            for h in range(2):
                fields[2 * p + h].append(
                    jnp.concatenate([got[3 * p + i][h] for i in range(3)], axis=0)
                )
        fields[4].append(jnp.concatenate([got[6][0], got[6][1], got[7][0]], axis=0))
    fields = [jnp.where(inside, jnp.concatenate(u, axis=1), 0.0) for u in fields]

    carried = jnp.concatenate([z[2 * t, 2], z[2 * t + 1, 2], recv[0, 7]], axis=0)
    lanes = lax.broadcasted_iota(jnp.int32, (rows, LANES), 1)
    for step in range(STEPS):
        shift = carried[:, HALF + step : HALF + step + 1].astype(jnp.int32)
        shift = jnp.broadcast_to(shift, (rows, LANES))
        whole = jnp.where(shift >= LANES, 1, 0)
        part = shift - whole * LANES
        index = jnp.bitwise_and(lanes - part, LANES - 1)
        lag = whole + jnp.where(lanes < part, 1, 0)
        if step < STEPS - 1:
            fields = [jnp.where(inside, new(), 0.0) for new in updates(fields, inverse, rows)]
            fields = [rotate(u, index, lag) for u in fields]

    own = 2 * SUB
    news = updates(fields, inverse, own)
    for p, fs in enumerate(PAIRS):
        pair = [rotate(new(), index[:own], lag[:own]) for new in news[fs]]
        for q in range(n // 2):
            f = [u[:, q * LANES : (q + 1) * LANES] for u in pair]
            if p < 2:
                for i in range(2):
                    rs = slice(i * SUB, (i + 1) * SUB)
                    even, odd = halves(f[0][rs], f[1][rs], low)
                    send2[2 * q, 2 * p + i] = even
                    send2[2 * q + 1, 2 * p + i] = odd
            else:
                even, odd = halves(f[0][:SUB], f[0][SUB:], low)
                send2[2 * q, 4] = even
                send2[2 * q + 1, 4] = odd
    for peer in peers:
        to_peer(send2.at[peer], recv2.at[t], ssem2, rsem2, peer).start()
    back = to_peer(send2.at[1:], recv2.at[1:], ssem2, rsem2, peers[0])
    recv2[t] = send2[t]

    there.wait_send()

    @pl.when(r > 0)
    def _():
        to_inner.wait_send()

    @pl.when(r < nr - 1)
    def _():
        to_outer.wait_send()

    back.wait_recv()

    back.wait_send()


def to_cells(got, o_hbm, out, sem):
    n = got.shape[0]
    writes = []
    for p in range(3):
        fs = slice(2 * p, min(2 * p + 2, FIELDS))
        if p < 2:
            block = got[:, 2 * p : 2 * p + 2].reshape(LANES, LANES)
            out[fs, 0] = block.T.reshape(2, HALF, LANES)
        else:
            parts = []
            for b in range(n):
                tile = got[b, 4]
                parts += [tile, pltpu.roll(tile, HALF, 1)]
            out[4, 0] = jnp.concatenate(parts, axis=0).T[:HALF]
        write = pltpu.make_async_copy(out.at[fs], o_hbm.at[fs], sem.at[p])
        write.start()
        writes.append(write)
    for write in writes:
        write.wait()


def by_cycles(n, nr, fields, shifts):
    tiles = fields.shape[3] // SUB
    tile = (SUB, LANES)
    dma = pltpu.SemaphoreType.DMA
    got = pl.pallas_call(
        functools.partial(kernel, n, nr),
        out_shape=pltpu.VMEM((n, 5) + tile, jnp.float32),
        in_specs=[pl.BlockSpec(memory_space=pltpu.HBM)] * 2,
        out_specs=pl.BlockSpec(memory_space=pltpu.VMEM),
        scratch_shapes=[
            pltpu.VMEM(fields.shape, fields.dtype),
            pltpu.VMEM(shifts.shape, shifts.dtype),
            pltpu.VMEM((tiles, 3) + tile, jnp.float32),
            pltpu.VMEM((n, 8) + tile, jnp.float32),
            pltpu.VMEM((n, 8) + tile, jnp.float32),
            pltpu.VMEM((n, 3) + tile, jnp.float32),
            pltpu.VMEM((n, 5) + tile, jnp.float32),
            dma,
            dma,
            dma((2,)),
            dma,
            dma,
            dma,
            dma((2,)),
        ],
        compiler_params=pltpu.CompilerParams(
            collective_id=0, has_side_effects=True, vmem_limit_bytes=16 * 1024 * 1024
        ),
    )(
        pltpu.with_memory_space_constraint(fields, pltpu.HBM),
        pltpu.with_memory_space_constraint(shifts, pltpu.HBM),
    )
    return pl.pallas_call(
        to_cells,
        out_shape=jax.ShapeDtypeStruct(fields.shape, fields.dtype),
        in_specs=[pl.BlockSpec(memory_space=pltpu.VMEM)],
        out_specs=pl.BlockSpec(memory_space=pltpu.HBM),
        scratch_shapes=[pltpu.VMEM(fields.shape, fields.dtype), dma((3,))],
        compiler_params=pltpu.CompilerParams(vmem_limit_bytes=16 * 1024 * 1024),
    )(got)


def passed_along(value, axis, steps):
    count = lax.axis_size(axis)
    pairs = [(source, (source + steps) % count) for source in range(count)]
    return lax.ppermute(value, axis, pairs)


def padded_2(value, sides, width, wrap):
    for axis, dim in sides:
        count, length = (lax.axis_size(axis), value.shape[dim])
        up = [(i, (i + 1) % count) for i in range(count if wrap else count - 1)]
        down = [(j, i) for i, j in up]
        last = lax.slice_in_dim(value, length - width, length, axis=dim)
        initial = lax.slice_in_dim(value, 0, width, axis=dim)
        before = lax.ppermute(last, axis, up)
        after = lax.ppermute(initial, axis, down)
        value = jnp.concatenate([before, value, after], axis=dim)
    return value


def update(padded, inverse):
    centre = padded[:, :, 1:-1, 1:-1]
    inner = padded[:, :, 1:-1, :-2]
    outer = padded[:, :, 1:-1, 2:]
    behind = padded[:, :, :-2, 1:-1]
    ahead = padded[:, :, 2:, 1:-1]
    polar_pad = jnp.concatenate([centre, centre, centre], axis=1)
    polar_sum = polar_pad[:, 2:] + polar_pad[:, :-2]
    radial_vel = centre[1]
    azim_vel = centre[2]
    advect = courant * (
        jnp.maximum(radial_vel, 0.0) * (centre - inner)
        + jnp.minimum(radial_vel, 0.0) * (outer - centre)
        + inverse
        * (
            jnp.maximum(azim_vel, 0.0) * (centre - behind)
            + jnp.minimum(azim_vel, 0.0) * (ahead - centre)
        )
    )
    laplace = (
        outer
        + inner
        - 2.0 * centre
        + inverse * inverse * (ahead + behind - 2.0 * centre)
        + (polar_sum - 2.0 * centre)
    )
    radial_diff = (outer - inner) * 0.5
    azim_diff = (ahead - behind) * 0.5
    diverge = radial_diff[1] + inverse * azim_diff[2]
    log_rho = centre[0]
    temper = centre[4]
    new_log = log_rho - advect[0] - courant * diverge
    new_radial = (
        radial_vel
        - advect[1]
        - courant * (temper * radial_diff[0] + radial_diff[4])
        + 0.5 * courant * inverse * azim_vel * azim_vel
        + viscous * laplace[1]
    )
    new_azim = (
        azim_vel
        - advect[2]
        - courant * inverse * (temper * azim_diff[0] + azim_diff[4])
        - 0.5 * courant * inverse * radial_vel * azim_vel
        + viscous * laplace[2]
    )
    new_polar = centre[3] - advect[3] + viscous * laplace[3]
    new_temper = temper - advect[4] - courant * 0.4 * temper * diverge + viscous * laplace[4]
    return jnp.stack([new_log, new_radial, new_azim, new_polar, new_temper])


def rotate_pieces(fields, offsets):
    width = fields.shape[2]
    count = (SMAX + width - 1) // width
    pieces = [fields]
    for blocks in range(1, count + 1):
        pieces.append(passed_along(fields, "azi", blocks))
    extended = jnp.concatenate(pieces[::-1], axis=2)
    nbits = SMAX.bit_length()
    reach = (1 << nbits) - 1
    anchor = count * width
    front = jnp.zeros(fields.shape[:2] + (reach - anchor,) + fields.shape[3:], fields.dtype)
    window = jnp.concatenate([front, extended], axis=2)
    for bit in range(nbits):
        amount = 1 << bit
        length = window.shape[2] - amount
        chosen = offsets // amount % 2 == 1
        window = jnp.where(
            chosen[None, None, None, :], window[:, :, :length], window[:, :, amount:]
        )
    return window


def by_blocks(fields, shifts):
    rows = fields.shape[3]
    total_rows = rows * lax.axis_size("rad")
    row_index = lax.axis_index("rad") * rows + jnp.arange(rows, dtype=jnp.int32)
    radius = 1.0 + (row_index.astype(jnp.float32) + 0.5) / jnp.float32(total_rows)
    inverse = 1.0 / radius
    for step in range(STEPS):
        radial_pad = padded_2(fields, (("rad", 3),), 1, False)
        padded = padded_2(radial_pad, (("azi", 2),), 1, True)
        fields = update(padded, inverse)
        fields = rotate_pieces(fields, shifts[step])
    return fields


def local(fields, shifts):
    n, nr = lax.axis_size("azi"), lax.axis_size("rad")
    count, planes, width, rows = fields.shape
    fits = (count, planes, width, rows) == (FIELDS, 1, HALF, LANES)
    if fits and rows == n * 2 * SUB and n * width > SMAX + LANES:
        return by_cycles(n, nr, fields, shifts)
    return by_blocks(fields, shifts)


def solution(mesh):
    placed = (P(None, None, "azi", "rad"), P(None, "rad"))
    return jax.shard_map(
        local, mesh=mesh, in_specs=placed, out_specs=P(None, None, "azi", "rad"), check_vma=False
    )
```

```python
import functools

import jax
import jax.numpy as jnp
from jax import lax
from jax.experimental import pallas as pl
from jax.experimental.pallas import tpu as pltpu
from jax.sharding import PartitionSpec as P

STEPS = 3
SMAX = 192
FIELDS = 5
LANES = 128
SUB = 8
HALF = 64
PAIRS = (slice(0, 2), slice(2, 4), slice(4, 5))

courant = 0.2
viscous = 0.1


def halves(a, b, low):
    first = jnp.where(low, a, pltpu.roll(b, HALF, b.ndim - 1))
    second = jnp.where(low, pltpu.roll(a, HALF, a.ndim - 1), b)
    return first, second


def updates(f, inverse, rows):
    inner = [pltpu.roll(u, 1, 0)[:rows] for u in f]
    outer = [pltpu.roll(u, u.shape[0] - 1, 0)[:rows] for u in f]
    f = [u[:rows] for u in f]
    inverse = inverse[:rows]
    behind = [pltpu.roll(u, 1, 1) for u in f]
    ahead = [pltpu.roll(u, u.shape[1] - 1, 1) for u in f]
    _, vr, vp, _, temper = f
    r_pos = courant * jnp.maximum(vr, 0.0)
    r_neg = courant * jnp.minimum(vr, 0.0)
    cg = courant * inverse
    p_pos = cg * jnp.maximum(vp, 0.0)
    p_neg = cg * jnp.minimum(vp, 0.0)
    vg2 = viscous * inverse * inverse

    def moved(i):
        u = f[i]
        d_in, d_out = u - inner[i], outer[i] - u
        d_back, d_fwd = u - behind[i], ahead[i] - u
        base = u - (r_pos * d_in + r_neg * d_out + p_pos * d_back + p_neg * d_fwd)
        if i == 0:
            return base
        polar = (u + u) - 2.0 * u
        return base + (viscous * ((d_out - d_in) + polar) + vg2 * (d_fwd - d_back))

    def dr(i):
        return (outer[i] - inner[i]) * 0.5

    def dp(i):
        return (ahead[i] - behind[i]) * 0.5

    diverge = dr(1) + inverse * dp(2)
    return [
        lambda: moved(0) - courant * diverge,
        lambda: moved(1) - courant * (temper * dr(0) + dr(4)) + (0.5 * cg) * vp * vp,
        lambda: moved(2) - cg * (temper * dp(0) + dp(4)) - (0.5 * cg) * vr * vp,
        lambda: moved(3),
        lambda: moved(4) - (courant * 0.4) * temper * diverge,
    ]


def rotate(u, index, lag):
    tiles = u.shape[1] // LANES
    g = [
        jnp.take_along_axis(u[:, q * LANES : (q + 1) * LANES], index, axis=1)
        for q in range(tiles)
    ]
    out = []
    for q in range(tiles):
        value = g[(q - (SMAX // LANES + 1)) % tiles]
        for back in range(SMAX // LANES, -1, -1):
            value = jnp.where(lag == back, g[(q - back) % tiles], value)
        out.append(value)
    return jnp.concatenate(out, axis=1)


def kernel(
    n, nr, f_hbm, s_hbm, recv2, f_ref, s_ref, z, send, recv, halo, eout, edge, send2,
    ssem, rsem, esend, erecv, ssem2, rsem2, isem,
):
    loads = [
        pltpu.make_async_copy(f_hbm, f_ref, isem.at[0]),
        pltpu.make_async_copy(s_hbm, s_ref, isem.at[1]),
    ]
    for load in loads:
        load.start()
    r = lax.axis_index("rad")
    t = lax.axis_index("azi")
    tiles = f_ref.shape[3] // SUB
    chip, core = lax.div(t, 2), lax.rem(t, 2)
    chips = n // 2
    far = [chips - 1 - chip, lax.rem(chip + 2, chips), chip + 1 - 2 * lax.rem(chip, 2)]
    peers = [2 * c + h for c in far for h in (core, 1 - core)] + [2 * chip + 1 - core]
    top_edge = (t == 0) & (r > 0)
    bottom_edge = (t == n - 1) & (r < nr - 1)

    barrier = pltpu.get_barrier_semaphore()
    for peer in peers:
        pl.semaphore_signal(barrier, inc=1, device_id={"azi": peer})

    @pl.when(top_edge)
    def _():
        for b in range(n):
            pl.semaphore_signal(barrier, inc=1, device_id={"rad": r - 1, "azi": b})

    @pl.when(bottom_edge)
    def _():
        for b in range(n):
            pl.semaphore_signal(barrier, inc=1, device_id={"rad": r + 1, "azi": b})

    sub = lax.broadcasted_iota(jnp.int32, (SUB, LANES), 0)
    lane = lax.broadcasted_iota(jnp.int32, (SUB, LANES), 1)
    low = lane < HALF

    def edge_copy(which, slot, device):
        return pltpu.make_async_remote_copy(
            src_ref=eout.at[which], dst_ref=edge.at[slot], send_sem=esend.at[which],
            recv_sem=erecv, device_id=device,
        )

    to_inner = edge_copy(0, t, {"rad": r - 1, "azi": n - 1})
    to_outer = edge_copy(1, t, {"rad": r + 1, "azi": 0})

    for load in loads:
        load.wait()
    for p, fs in enumerate(PAIRS):
        if p < 2:
            stack = f_ref[fs, 0].reshape(LANES, LANES)
        else:
            shifts = s_ref[...].astype(jnp.float32)
            rest = jnp.zeros((HALF - STEPS, LANES), jnp.float32)
            stack = jnp.concatenate([f_ref[4, 0], shifts, rest], axis=0)
        z[:, p] = stack.T.reshape(tiles, SUB, LANES)

    def halo_tile(p, k):
        above, below = jnp.maximum(2 * k - 1, 0), jnp.minimum(2 * k + 2, tiles - 1)
        return jnp.where(sub >= SUB - STEPS, z[above, p], z[below, p])

    for k in range(n):
        a, b = 2 * k, 2 * k + 1
        for p in range(2):
            send[k, 2 * p] = z[a, p]
            send[k, 2 * p + 1] = z[b, p]
        send[k, 4] = jnp.where(low, z[a, 2], pltpu.roll(z[b, 2], HALF, 1))
        last = halo_tile(2, k)
        free = jnp.where(low, pltpu.roll(last, 3, 0), pltpu.roll(pltpu.roll(last, 6, 0), HALF, 1))
        send[k, 5] = jnp.where((sub == 3) | (sub == 4), free, halo_tile(0, k))
        send[k, 6] = jnp.where(sub == 3, pltpu.roll(free, 6, 0), halo_tile(1, k))
    eout[0, 0] = jnp.where(sub < 4, z[0, 0], pltpu.roll(z[0, 1], 4, 0))
    eout[1, 0] = jnp.where(sub < 4, pltpu.roll(z[tiles - 1, 1], 4, 0), z[tiles - 1, 0])
    eout[0, 1] = z[0, 2]
    eout[1, 1] = z[tiles - 1, 2]

    needed = n - 1 + (r > 0).astype(jnp.int32) + (r < nr - 1).astype(jnp.int32)
    pl.semaphore_wait(barrier, needed)

    @pl.when(r > 0)
    def _():
        to_inner.start()

    @pl.when(r < nr - 1)
    def _():
        to_outer.start()

    def to_peer(src, dst, send_sem, recv_sem, peer):
        return pltpu.make_async_remote_copy(
            src_ref=src, dst_ref=dst, send_sem=send_sem, recv_sem=recv_sem,
            device_id={"azi": peer},
        )

    for peer in peers:
        to_peer(send.at[peer], recv.at[t], ssem, rsem, peer).start()
    there = to_peer(send.at[1:], recv.at[1:], ssem, rsem, peers[0])
    recv[t] = send[t]

    rows = 3 * SUB
    width = n * HALF
    row = lax.broadcasted_iota(jnp.int32, (rows, width), 0)
    row = jnp.where(row < 2 * SUB + SUB // 2, row, row - rows)
    row = row + (r * f_ref.shape[3] + t * (2 * SUB))
    total = nr * f_ref.shape[3]
    inside = (row >= 0) & (row < total)
    radius = 1.0 + (row.astype(jnp.float32) + 0.5) / jnp.float32(total)
    inverse = 1.0 / radius

    there.wait_recv()
    own_shifts = halo_tile(2, t)
    for b in range(n):
        free = jnp.where(sub == 5, pltpu.roll(recv[b, 6], 2, 0), recv[b, 5])
        bottom, top = pltpu.roll(free, 5, 0), pltpu.roll(pltpu.roll(free, 2, 0), HALF, 1)
        halo[b] = jnp.where(low, jnp.where(sub < 4, bottom, top), own_shifts)

    @pl.when(top_edge | bottom_edge)
    def _():
        first = jnp.where(t == 0, SUB - STEPS, 0)
        last = jnp.where(t == 0, SUB, STEPS)
        take = (sub >= first) & (sub < last)
        pltpu.make_async_remote_copy(
            src_ref=recv.at[:, :2], dst_ref=edge, send_sem=esend.at[0], recv_sem=erecv,
            device_id={"rad": lax.rem(r + 1, nr)},
        ).wait_recv()
        for b in range(n):
            recv[b, 5] = jnp.where(take, edge[b, 0], recv[b, 5])
            recv[b, 6] = jnp.where(take, pltpu.roll(edge[b, 0], 4, 0), recv[b, 6])
            halo[b] = jnp.where(take, edge[b, 1], halo[b])

    fields = [[] for _ in range(FIELDS)]
    for q in range(n // 2):
        got = [halves(recv[2 * q, i], recv[2 * q + 1, i], low) for i in range(7)]
        for p in range(2):
            for h in range(2):
                tiles_of = (got[2 * p][h], got[2 * p + 1][h], got[5 + p][h])
                fields[2 * p + h].append(jnp.concatenate(tiles_of, axis=0))
        last = jnp.where(low, halo[2 * q], pltpu.roll(halo[2 * q + 1], HALF, 1))
        fields[4].append(jnp.concatenate([got[4][0], got[4][1], last], axis=0))
    fields = [jnp.where(inside, jnp.concatenate(u, axis=1), 0.0) for u in fields]

    carried = jnp.concatenate([z[2 * t, 2], z[2 * t + 1, 2], halo[0]], axis=0)
    lanes = lax.broadcasted_iota(jnp.int32, (rows, LANES), 1)
    for step in range(STEPS):
        shift = carried[:, HALF + step : HALF + step + 1].astype(jnp.int32)
        shift = jnp.broadcast_to(shift, (rows, LANES))
        whole = jnp.where(shift >= LANES, 1, 0)
        part = shift - whole * LANES
        index = jnp.bitwise_and(lanes - part, LANES - 1)
        lag = whole + jnp.where(lanes < part, 1, 0)
        if step < STEPS - 1:
            fields = [jnp.where(inside, new(), 0.0) for new in updates(fields, inverse, rows)]
            fields = [rotate(u, index, lag) for u in fields]

    own = 2 * SUB
    news = updates(fields, inverse, own)
    for p, fs in enumerate(PAIRS):
        pair = [rotate(new(), index[:own], lag[:own]) for new in news[fs]]
        for q in range(n // 2):
            f = [u[:, q * LANES : (q + 1) * LANES] for u in pair]
            if p < 2:
                for i in range(2):
                    rs = slice(i * SUB, (i + 1) * SUB)
                    even, odd = halves(f[0][rs], f[1][rs], low)
                    send2[2 * q, 2 * p + i] = even
                    send2[2 * q + 1, 2 * p + i] = odd
            else:
                even, odd = halves(f[0][:SUB], f[0][SUB:], low)
                send2[2 * q, 4] = even
                send2[2 * q + 1, 4] = odd
    for peer in peers:
        to_peer(send2.at[peer], recv2.at[t], ssem2, rsem2, peer).start()
    back = to_peer(send2.at[1:], recv2.at[1:], ssem2, rsem2, peers[0])
    recv2[t] = send2[t]

    there.wait_send()

    @pl.when(r > 0)
    def _():
        to_inner.wait_send()

    @pl.when(r < nr - 1)
    def _():
        to_outer.wait_send()

    back.wait_recv()

    back.wait_send()


def to_cells(got, o_hbm, out, sem):
    n = got.shape[0]
    writes = []
    for p in range(3):
        fs = slice(2 * p, min(2 * p + 2, FIELDS))
        if p < 2:
            block = got[:, 2 * p : 2 * p + 2].reshape(LANES, LANES)
            out[fs, 0] = block.T.reshape(2, HALF, LANES)
        else:
            parts = []
            for b in range(n):
                tile = got[b, 4]
                parts += [tile, pltpu.roll(tile, HALF, 1)]
            out[4, 0] = jnp.concatenate(parts, axis=0).T[:HALF]
        write = pltpu.make_async_copy(out.at[fs], o_hbm.at[fs], sem.at[p])
        write.start()
        writes.append(write)
    for write in writes:
        write.wait()


def by_cycles(n, nr, fields, shifts):
    tiles = fields.shape[3] // SUB
    tile = (SUB, LANES)
    dma = pltpu.SemaphoreType.DMA
    got = pl.pallas_call(
        functools.partial(kernel, n, nr),
        out_shape=pltpu.VMEM((n, 5) + tile, jnp.float32),
        in_specs=[pl.BlockSpec(memory_space=pltpu.HBM)] * 2,
        out_specs=pl.BlockSpec(memory_space=pltpu.VMEM),
        scratch_shapes=[
            pltpu.VMEM(fields.shape, fields.dtype),
            pltpu.VMEM(shifts.shape, shifts.dtype),
            pltpu.VMEM((tiles, 3) + tile, jnp.float32),
            pltpu.VMEM((n, 7) + tile, jnp.float32),
            pltpu.VMEM((n, 7) + tile, jnp.float32),
            pltpu.VMEM((n,) + tile, jnp.float32),
            pltpu.VMEM((2, 2) + tile, jnp.float32),
            pltpu.VMEM((n, 2) + tile, jnp.float32),
            pltpu.VMEM((n, 5) + tile, jnp.float32),
            dma,
            dma,
            dma((2,)),
            dma,
            dma,
            dma,
            dma((2,)),
        ],
        compiler_params=pltpu.CompilerParams(
            collective_id=0, has_side_effects=True, vmem_limit_bytes=16 * 1024 * 1024
        ),
    )(
        pltpu.with_memory_space_constraint(fields, pltpu.HBM),
        pltpu.with_memory_space_constraint(shifts, pltpu.HBM),
    )
    return pl.pallas_call(
        to_cells,
        out_shape=jax.ShapeDtypeStruct(fields.shape, fields.dtype),
        in_specs=[pl.BlockSpec(memory_space=pltpu.VMEM)],
        out_specs=pl.BlockSpec(memory_space=pltpu.HBM),
        scratch_shapes=[pltpu.VMEM(fields.shape, fields.dtype), dma((3,))],
        compiler_params=pltpu.CompilerParams(vmem_limit_bytes=16 * 1024 * 1024),
    )(got)


def passed_along(value, axis, steps):
    count = lax.axis_size(axis)
    pairs = [(source, (source + steps) % count) for source in range(count)]
    return lax.ppermute(value, axis, pairs)


def padded_2(value, sides, width, wrap):
    for axis, dim in sides:
        count, length = (lax.axis_size(axis), value.shape[dim])
        up = [(i, (i + 1) % count) for i in range(count if wrap else count - 1)]
        down = [(j, i) for i, j in up]
        last = lax.slice_in_dim(value, length - width, length, axis=dim)
        initial = lax.slice_in_dim(value, 0, width, axis=dim)
        before = lax.ppermute(last, axis, up)
        after = lax.ppermute(initial, axis, down)
        value = jnp.concatenate([before, value, after], axis=dim)
    return value


def update(padded, inverse):
    centre = padded[:, :, 1:-1, 1:-1]
    inner = padded[:, :, 1:-1, :-2]
    outer = padded[:, :, 1:-1, 2:]
    behind = padded[:, :, :-2, 1:-1]
    ahead = padded[:, :, 2:, 1:-1]
    polar_pad = jnp.concatenate([centre, centre, centre], axis=1)
    polar_sum = polar_pad[:, 2:] + polar_pad[:, :-2]
    radial_vel = centre[1]
    azim_vel = centre[2]
    advect = courant * (
        jnp.maximum(radial_vel, 0.0) * (centre - inner)
        + jnp.minimum(radial_vel, 0.0) * (outer - centre)
        + inverse
        * (
            jnp.maximum(azim_vel, 0.0) * (centre - behind)
            + jnp.minimum(azim_vel, 0.0) * (ahead - centre)
        )
    )
    laplace = (
        outer
        + inner
        - 2.0 * centre
        + inverse * inverse * (ahead + behind - 2.0 * centre)
        + (polar_sum - 2.0 * centre)
    )
    radial_diff = (outer - inner) * 0.5
    azim_diff = (ahead - behind) * 0.5
    diverge = radial_diff[1] + inverse * azim_diff[2]
    log_rho = centre[0]
    temper = centre[4]
    new_log = log_rho - advect[0] - courant * diverge
    new_radial = (
        radial_vel
        - advect[1]
        - courant * (temper * radial_diff[0] + radial_diff[4])
        + 0.5 * courant * inverse * azim_vel * azim_vel
        + viscous * laplace[1]
    )
    new_azim = (
        azim_vel
        - advect[2]
        - courant * inverse * (temper * azim_diff[0] + azim_diff[4])
        - 0.5 * courant * inverse * radial_vel * azim_vel
        + viscous * laplace[2]
    )
    new_polar = centre[3] - advect[3] + viscous * laplace[3]
    new_temper = temper - advect[4] - courant * 0.4 * temper * diverge + viscous * laplace[4]
    return jnp.stack([new_log, new_radial, new_azim, new_polar, new_temper])


def rotate_pieces(fields, offsets):
    width = fields.shape[2]
    count = (SMAX + width - 1) // width
    pieces = [fields]
    for blocks in range(1, count + 1):
        pieces.append(passed_along(fields, "azi", blocks))
    extended = jnp.concatenate(pieces[::-1], axis=2)
    nbits = SMAX.bit_length()
    reach = (1 << nbits) - 1
    anchor = count * width
    front = jnp.zeros(fields.shape[:2] + (reach - anchor,) + fields.shape[3:], fields.dtype)
    window = jnp.concatenate([front, extended], axis=2)
    for bit in range(nbits):
        amount = 1 << bit
        length = window.shape[2] - amount
        chosen = offsets // amount % 2 == 1
        window = jnp.where(
            chosen[None, None, None, :], window[:, :, :length], window[:, :, amount:]
        )
    return window


def by_blocks(fields, shifts):
    rows = fields.shape[3]
    total_rows = rows * lax.axis_size("rad")
    row_index = lax.axis_index("rad") * rows + jnp.arange(rows, dtype=jnp.int32)
    radius = 1.0 + (row_index.astype(jnp.float32) + 0.5) / jnp.float32(total_rows)
    inverse = 1.0 / radius
    for step in range(STEPS):
        radial_pad = padded_2(fields, (("rad", 3),), 1, False)
        padded = padded_2(radial_pad, (("azi", 2),), 1, True)
        fields = update(padded, inverse)
        fields = rotate_pieces(fields, shifts[step])
    return fields


def local(fields, shifts):
    n, nr = lax.axis_size("azi"), lax.axis_size("rad")
    count, planes, width, rows = fields.shape
    fits = (count, planes, width, rows) == (FIELDS, 1, HALF, LANES)
    if fits and rows == n * 2 * SUB and n * width > SMAX + LANES:
        return by_cycles(n, nr, fields, shifts)
    return by_blocks(fields, shifts)


def solution(mesh):
    placed = (P(None, None, "azi", "rad"), P(None, "rad"))
    return jax.shard_map(
        local, mesh=mesh, in_specs=placed, out_specs=P(None, None, "azi", "rad"), check_vma=False
    )
```

```python
import functools

import jax
import jax.numpy as jnp
from jax import lax
from jax.experimental import pallas as pl
from jax.experimental.pallas import tpu as pltpu
from jax.sharding import PartitionSpec as P

STEPS = 3
SMAX = 192
FIELDS = 5
LANES = 128
SUB = 8
HALF = 64
PAIRS = (slice(0, 2), slice(2, 4), slice(4, 5))

courant = 0.2
viscous = 0.1


def halves(a, b, low):
    first = jnp.where(low, a, pltpu.roll(b, HALF, b.ndim - 1))
    second = jnp.where(low, pltpu.roll(a, HALF, a.ndim - 1), b)
    return first, second


def updates(f, inverse, rows):
    inner = [pltpu.roll(u, 1, 0)[:rows] for u in f]
    outer = [pltpu.roll(u, u.shape[0] - 1, 0)[:rows] for u in f]
    f = [u[:rows] for u in f]
    inverse = inverse[:rows]
    behind = [pltpu.roll(u, 1, 1) for u in f]
    ahead = [pltpu.roll(u, u.shape[1] - 1, 1) for u in f]
    _, vr, vp, _, temper = f
    cg = courant * inverse
    vg2 = viscous * inverse * inverse
    into, out = courant * jnp.maximum(vr, 0.0), -courant * jnp.minimum(vr, 0.0)
    back, fwd = cg * jnp.maximum(vp, 0.0), -cg * jnp.minimum(vp, 0.0)
    w_in, w_out, w_back, w_fwd = into + viscous, out + viscous, back + vg2, fwd + vg2

    def moved(i):
        u = f[i]
        polar = (u + u) - 2.0 * u
        return (
            u + viscous * polar
            + (w_out * (outer[i] - u) - w_in * (u - inner[i]))
            + (w_fwd * (ahead[i] - u) - w_back * (u - behind[i]))
        )

    def advected(i):
        u = f[i]
        return (
            u
            + (out * (outer[i] - u) - into * (u - inner[i]))
            + (fwd * (ahead[i] - u) - back * (u - behind[i]))
        )

    def dr(i):
        return outer[i] - inner[i]

    def dp(i):
        return ahead[i] - behind[i]

    half = 0.5 * courant
    half_g = 0.5 * cg
    diverge = dr(1) + inverse * dp(2)
    return [
        lambda: advected(0) - half * diverge,
        lambda: moved(1) - half * (temper * dr(0) + dr(4)) + half_g * vp * vp,
        lambda: moved(2) - half_g * (temper * dp(0) + dp(4) + vr * vp),
        lambda: moved(3),
        lambda: moved(4) - (0.4 * half) * temper * diverge,
    ]


def rotate(u, index, lag):
    tiles = u.shape[1] // LANES
    g = [
        jnp.take_along_axis(u[:, q * LANES : (q + 1) * LANES], index, axis=1)
        for q in range(tiles)
    ]
    out = []
    for q in range(tiles):
        value = g[(q - (SMAX // LANES + 1)) % tiles]
        for back in range(SMAX // LANES, -1, -1):
            value = jnp.where(lag == back, g[(q - back) % tiles], value)
        out.append(value)
    return jnp.concatenate(out, axis=1)


def kernel(
    n, nr, f_hbm, s_hbm, recv2, f_ref, s_ref, z, send, recv, halo, eout, edge, send2,
    ssem, rsem, esend, erecv, ssem2, rsem2, isem,
):
    loads = [
        pltpu.make_async_copy(f_hbm.at[fs], f_ref.at[fs], isem.at[p])
        for p, fs in enumerate(PAIRS)
    ]
    loads.append(pltpu.make_async_copy(s_hbm, s_ref, isem.at[3]))
    for load in loads:
        load.start()
    r = lax.axis_index("rad")
    t = lax.axis_index("azi")
    tiles = f_ref.shape[3] // SUB
    chip, core = lax.div(t, 2), lax.rem(t, 2)
    chips = n // 2
    far = [chips - 1 - chip, lax.rem(chip + 2, chips), chip + 1 - 2 * lax.rem(chip, 2)]
    peers = [2 * c + h for c in far for h in (core, 1 - core)] + [2 * chip + 1 - core]
    top_edge = (t == 0) & (r > 0)
    bottom_edge = (t == n - 1) & (r < nr - 1)

    barrier = pltpu.get_barrier_semaphore()
    for peer in peers:
        pl.semaphore_signal(barrier, inc=1, device_id={"azi": peer})

    @pl.when(top_edge)
    def _():
        for b in range(n):
            pl.semaphore_signal(barrier, inc=1, device_id={"rad": r - 1, "azi": b})

    @pl.when(bottom_edge)
    def _():
        for b in range(n):
            pl.semaphore_signal(barrier, inc=1, device_id={"rad": r + 1, "azi": b})

    sub = lax.broadcasted_iota(jnp.int32, (SUB, LANES), 0)
    lane = lax.broadcasted_iota(jnp.int32, (SUB, LANES), 1)
    low = lane < HALF

    def edge_copy(which, slot, device):
        return pltpu.make_async_remote_copy(
            src_ref=eout.at[which], dst_ref=edge.at[slot], send_sem=esend.at[which],
            recv_sem=erecv, device_id=device,
        )

    to_inner = edge_copy(0, t, {"rad": r - 1, "azi": n - 1})
    to_outer = edge_copy(1, t, {"rad": r + 1, "azi": 0})

    for p, fs in enumerate(PAIRS):
        loads[p].wait()
        if p < 2:
            stack = f_ref[fs, 0].reshape(LANES, LANES)
        else:
            loads[3].wait()
            shifts = s_ref[...].astype(jnp.float32)
            rest = jnp.zeros((HALF - STEPS, LANES), jnp.float32)
            stack = jnp.concatenate([f_ref[4, 0], shifts, rest], axis=0)
        z[:, p] = stack.T.reshape(tiles, SUB, LANES)

    def halo_tile(p, k):
        above, below = jnp.maximum(2 * k - 1, 0), jnp.minimum(2 * k + 2, tiles - 1)
        return jnp.where(sub >= SUB - STEPS, z[above, p], z[below, p])

    for k in range(n):
        a, b = 2 * k, 2 * k + 1
        for p in range(2):
            send[k, 2 * p] = z[a, p]
            send[k, 2 * p + 1] = z[b, p]
        send[k, 4] = jnp.where(low, z[a, 2], pltpu.roll(z[b, 2], HALF, 1))
        last = halo_tile(2, k)
        free = jnp.where(low, pltpu.roll(last, 3, 0), pltpu.roll(pltpu.roll(last, 6, 0), HALF, 1))
        send[k, 5] = jnp.where((sub == 3) | (sub == 4), free, halo_tile(0, k))
        send[k, 6] = jnp.where(sub == 3, pltpu.roll(free, 6, 0), halo_tile(1, k))
    eout[0, 0] = jnp.where(sub < 4, z[0, 0], pltpu.roll(z[0, 1], 4, 0))
    eout[1, 0] = jnp.where(sub < 4, pltpu.roll(z[tiles - 1, 1], 4, 0), z[tiles - 1, 0])
    eout[0, 1] = z[0, 2]
    eout[1, 1] = z[tiles - 1, 2]

    needed = n - 1 + (r > 0).astype(jnp.int32) + (r < nr - 1).astype(jnp.int32)
    pl.semaphore_wait(barrier, needed)

    @pl.when(r > 0)
    def _():
        to_inner.start()

    @pl.when(r < nr - 1)
    def _():
        to_outer.start()

    def to_peer(src, dst, send_sem, recv_sem, peer):
        return pltpu.make_async_remote_copy(
            src_ref=src, dst_ref=dst, send_sem=send_sem, recv_sem=recv_sem,
            device_id={"azi": peer},
        )

    for peer in peers:
        to_peer(send.at[peer], recv.at[t], ssem, rsem, peer).start()
    there = to_peer(send.at[1:], recv.at[1:], ssem, rsem, peers[0])
    recv[t] = send[t]

    rows = 3 * SUB
    width = n * HALF
    row = lax.broadcasted_iota(jnp.int32, (rows, width), 0)
    row = jnp.where(row < 2 * SUB + SUB // 2, row, row - rows)
    row = row + (r * f_ref.shape[3] + t * (2 * SUB))
    total = nr * f_ref.shape[3]
    inside = (row >= 0) & (row < total)
    radius = 1.0 + (row.astype(jnp.float32) + 0.5) / jnp.float32(total)
    inverse = 1.0 / radius

    own = 2 * SUB

    def inner_rows(u):
        return jnp.concatenate([u[:own], jnp.where(inside[own:], u[own:], 0.0)], axis=0)

    there.wait_recv()
    own_shifts = halo_tile(2, t)
    for b in range(n):
        free = jnp.where(sub == 5, pltpu.roll(recv[b, 6], 2, 0), recv[b, 5])
        bottom, top = pltpu.roll(free, 5, 0), pltpu.roll(pltpu.roll(free, 2, 0), HALF, 1)
        halo[b] = jnp.where(low, jnp.where(sub < 4, bottom, top), own_shifts)

    @pl.when(top_edge | bottom_edge)
    def _():
        first = jnp.where(t == 0, SUB - STEPS, 0)
        last = jnp.where(t == 0, SUB, STEPS)
        take = (sub >= first) & (sub < last)
        pltpu.make_async_remote_copy(
            src_ref=recv.at[:, :2], dst_ref=edge, send_sem=esend.at[0], recv_sem=erecv,
            device_id={"rad": lax.rem(r + 1, nr)},
        ).wait_recv()
        for b in range(n):
            recv[b, 5] = jnp.where(take, edge[b, 0], recv[b, 5])
            recv[b, 6] = jnp.where(take, pltpu.roll(edge[b, 0], 4, 0), recv[b, 6])
            halo[b] = jnp.where(take, edge[b, 1], halo[b])

    fields = [[] for _ in range(FIELDS)]
    for q in range(n // 2):
        got = [halves(recv[2 * q, i], recv[2 * q + 1, i], low) for i in range(7)]
        for p in range(2):
            for h in range(2):
                tiles_of = (got[2 * p][h], got[2 * p + 1][h], got[5 + p][h])
                fields[2 * p + h].append(jnp.concatenate(tiles_of, axis=0))
        last = jnp.where(low, halo[2 * q], pltpu.roll(halo[2 * q + 1], HALF, 1))
        fields[4].append(jnp.concatenate([got[4][0], got[4][1], last], axis=0))
    fields = [inner_rows(jnp.concatenate(u, axis=1)) for u in fields]

    carried = jnp.concatenate([z[2 * t, 2], z[2 * t + 1, 2], halo[0]], axis=0)
    lanes = lax.broadcasted_iota(jnp.int32, (rows, LANES), 1)
    for step in range(STEPS):
        shift = carried[:, HALF + step : HALF + step + 1].astype(jnp.int32)
        shift = jnp.broadcast_to(shift, (rows, LANES))
        whole = jnp.where(shift >= LANES, 1, 0)
        part = shift - whole * LANES
        index = jnp.bitwise_and(lanes - part, LANES - 1)
        lag = whole + jnp.where(lanes < part, 1, 0)
        if step < STEPS - 1:
            fields = [inner_rows(new()) for new in updates(fields, inverse, rows)]
            fields = [rotate(u, index, lag) for u in fields]

    news = updates(fields, inverse, own)
    for p, fs in enumerate(PAIRS):
        pair = [rotate(new(), index[:own], lag[:own]) for new in news[fs]]
        for q in range(n // 2):
            f = [u[:, q * LANES : (q + 1) * LANES] for u in pair]
            if p < 2:
                for i in range(2):
                    rs = slice(i * SUB, (i + 1) * SUB)
                    even, odd = halves(f[0][rs], f[1][rs], low)
                    send2[2 * q, 2 * p + i] = even
                    send2[2 * q + 1, 2 * p + i] = odd
            else:
                even, odd = halves(f[0][:SUB], f[0][SUB:], low)
                send2[2 * q, 4] = even
                send2[2 * q + 1, 4] = odd
    for peer in peers:
        to_peer(send2.at[peer], recv2.at[t], ssem2, rsem2, peer).start()
    back = to_peer(send2.at[1:], recv2.at[1:], ssem2, rsem2, peers[0])
    recv2[t] = send2[t]

    there.wait_send()

    @pl.when(r > 0)
    def _():
        to_inner.wait_send()

    @pl.when(r < nr - 1)
    def _():
        to_outer.wait_send()

    back.wait_recv()

    back.wait_send()


def to_cells(got, o_hbm, out, sem):
    n = got.shape[0]
    writes = []
    for p in range(3):
        fs = slice(2 * p, min(2 * p + 2, FIELDS))
        if p < 2:
            block = got[:, 2 * p : 2 * p + 2].reshape(LANES, LANES)
            out[fs, 0] = block.T.reshape(2, HALF, LANES)
        else:
            parts = []
            for b in range(n):
                tile = got[b, 4]
                parts += [tile, pltpu.roll(tile, HALF, 1)]
            out[4, 0] = jnp.concatenate(parts, axis=0).T[:HALF]
        write = pltpu.make_async_copy(out.at[fs], o_hbm.at[fs], sem.at[p])
        write.start()
        writes.append(write)
    for write in writes:
        write.wait()


def by_cycles(n, nr, fields, shifts):
    tiles = fields.shape[3] // SUB
    tile = (SUB, LANES)
    dma = pltpu.SemaphoreType.DMA
    got = pl.pallas_call(
        functools.partial(kernel, n, nr),
        out_shape=pltpu.VMEM((n, 5) + tile, jnp.float32),
        in_specs=[pl.BlockSpec(memory_space=pltpu.HBM)] * 2,
        out_specs=pl.BlockSpec(memory_space=pltpu.VMEM),
        scratch_shapes=[
            pltpu.VMEM(fields.shape, fields.dtype),
            pltpu.VMEM(shifts.shape, shifts.dtype),
            pltpu.VMEM((tiles, 3) + tile, jnp.float32),
            pltpu.VMEM((n, 7) + tile, jnp.float32),
            pltpu.VMEM((n, 7) + tile, jnp.float32),
            pltpu.VMEM((n,) + tile, jnp.float32),
            pltpu.VMEM((2, 2) + tile, jnp.float32),
            pltpu.VMEM((n, 2) + tile, jnp.float32),
            pltpu.VMEM((n, 5) + tile, jnp.float32),
            dma,
            dma,
            dma((2,)),
            dma,
            dma,
            dma,
            dma((4,)),
        ],
        compiler_params=pltpu.CompilerParams(
            collective_id=0, has_side_effects=True, vmem_limit_bytes=16 * 1024 * 1024
        ),
    )(
        pltpu.with_memory_space_constraint(fields, pltpu.HBM),
        pltpu.with_memory_space_constraint(shifts, pltpu.HBM),
    )
    return pl.pallas_call(
        to_cells,
        out_shape=jax.ShapeDtypeStruct(fields.shape, fields.dtype),
        in_specs=[pl.BlockSpec(memory_space=pltpu.VMEM)],
        out_specs=pl.BlockSpec(memory_space=pltpu.HBM),
        scratch_shapes=[pltpu.VMEM(fields.shape, fields.dtype), dma((3,))],
        compiler_params=pltpu.CompilerParams(vmem_limit_bytes=16 * 1024 * 1024),
    )(got)


def passed_along(value, axis, steps):
    count = lax.axis_size(axis)
    pairs = [(source, (source + steps) % count) for source in range(count)]
    return lax.ppermute(value, axis, pairs)


def padded_2(value, sides, width, wrap):
    for axis, dim in sides:
        count, length = (lax.axis_size(axis), value.shape[dim])
        up = [(i, (i + 1) % count) for i in range(count if wrap else count - 1)]
        down = [(j, i) for i, j in up]
        last = lax.slice_in_dim(value, length - width, length, axis=dim)
        initial = lax.slice_in_dim(value, 0, width, axis=dim)
        before = lax.ppermute(last, axis, up)
        after = lax.ppermute(initial, axis, down)
        value = jnp.concatenate([before, value, after], axis=dim)
    return value


def update(padded, inverse):
    centre = padded[:, :, 1:-1, 1:-1]
    inner = padded[:, :, 1:-1, :-2]
    outer = padded[:, :, 1:-1, 2:]
    behind = padded[:, :, :-2, 1:-1]
    ahead = padded[:, :, 2:, 1:-1]
    polar_pad = jnp.concatenate([centre, centre, centre], axis=1)
    polar_sum = polar_pad[:, 2:] + polar_pad[:, :-2]
    radial_vel = centre[1]
    azim_vel = centre[2]
    advect = courant * (
        jnp.maximum(radial_vel, 0.0) * (centre - inner)
        + jnp.minimum(radial_vel, 0.0) * (outer - centre)
        + inverse
        * (
            jnp.maximum(azim_vel, 0.0) * (centre - behind)
            + jnp.minimum(azim_vel, 0.0) * (ahead - centre)
        )
    )
    laplace = (
        outer
        + inner
        - 2.0 * centre
        + inverse * inverse * (ahead + behind - 2.0 * centre)
        + (polar_sum - 2.0 * centre)
    )
    radial_diff = (outer - inner) * 0.5
    azim_diff = (ahead - behind) * 0.5
    diverge = radial_diff[1] + inverse * azim_diff[2]
    log_rho = centre[0]
    temper = centre[4]
    new_log = log_rho - advect[0] - courant * diverge
    new_radial = (
        radial_vel
        - advect[1]
        - courant * (temper * radial_diff[0] + radial_diff[4])
        + 0.5 * courant * inverse * azim_vel * azim_vel
        + viscous * laplace[1]
    )
    new_azim = (
        azim_vel
        - advect[2]
        - courant * inverse * (temper * azim_diff[0] + azim_diff[4])
        - 0.5 * courant * inverse * radial_vel * azim_vel
        + viscous * laplace[2]
    )
    new_polar = centre[3] - advect[3] + viscous * laplace[3]
    new_temper = temper - advect[4] - courant * 0.4 * temper * diverge + viscous * laplace[4]
    return jnp.stack([new_log, new_radial, new_azim, new_polar, new_temper])


def rotate_pieces(fields, offsets):
    width = fields.shape[2]
    count = (SMAX + width - 1) // width
    pieces = [fields]
    for blocks in range(1, count + 1):
        pieces.append(passed_along(fields, "azi", blocks))
    extended = jnp.concatenate(pieces[::-1], axis=2)
    nbits = SMAX.bit_length()
    reach = (1 << nbits) - 1
    anchor = count * width
    front = jnp.zeros(fields.shape[:2] + (reach - anchor,) + fields.shape[3:], fields.dtype)
    window = jnp.concatenate([front, extended], axis=2)
    for bit in range(nbits):
        amount = 1 << bit
        length = window.shape[2] - amount
        chosen = offsets // amount % 2 == 1
        window = jnp.where(
            chosen[None, None, None, :], window[:, :, :length], window[:, :, amount:]
        )
    return window


def by_blocks(fields, shifts):
    rows = fields.shape[3]
    total_rows = rows * lax.axis_size("rad")
    row_index = lax.axis_index("rad") * rows + jnp.arange(rows, dtype=jnp.int32)
    radius = 1.0 + (row_index.astype(jnp.float32) + 0.5) / jnp.float32(total_rows)
    inverse = 1.0 / radius
    for step in range(STEPS):
        radial_pad = padded_2(fields, (("rad", 3),), 1, False)
        padded = padded_2(radial_pad, (("azi", 2),), 1, True)
        fields = update(padded, inverse)
        fields = rotate_pieces(fields, shifts[step])
    return fields


def local(fields, shifts):
    n, nr = lax.axis_size("azi"), lax.axis_size("rad")
    count, planes, width, rows = fields.shape
    fits = (count, planes, width, rows) == (FIELDS, 1, HALF, LANES)
    if fits and rows == n * 2 * SUB and n * width > SMAX + LANES:
        return by_cycles(n, nr, fields, shifts)
    return by_blocks(fields, shifts)


def solution(mesh):
    placed = (P(None, None, "azi", "rad"), P(None, "rad"))
    return jax.shard_map(
        local, mesh=mesh, in_specs=placed, out_specs=P(None, None, "azi", "rad"), check_vma=False
    )
```

```python
import functools

import jax
import jax.numpy as jnp
from jax import lax
from jax.experimental import pallas as pl
from jax.experimental.pallas import tpu as pltpu
from jax.sharding import PartitionSpec as P

STEPS = 3
SMAX = 192
FIELDS = 5
LANES = 128
SUB = 8
HALF = 64
PAIRS = (slice(0, 2), slice(2, 4), slice(4, 5))

courant = 0.2
viscous = 0.1


def halves(a, b, low):
    first = jnp.where(low, a, pltpu.roll(b, HALF, b.ndim - 1))
    second = jnp.where(low, pltpu.roll(a, HALF, a.ndim - 1), b)
    return first, second


def updates(f, inverse, rows):
    inner = [pltpu.roll(u, 1, 0)[:rows] for u in f]
    outer = [pltpu.roll(u, u.shape[0] - 1, 0)[:rows] for u in f]
    f = [u[:rows] for u in f]
    inverse = inverse[:rows]
    behind = [pltpu.roll(u, 1, 1) for u in f]
    ahead = [pltpu.roll(u, u.shape[1] - 1, 1) for u in f]
    _, vr, vp, _, temper = f
    cg = courant * inverse
    vg2 = viscous * inverse * inverse
    into, out = courant * jnp.maximum(vr, 0.0), -courant * jnp.minimum(vr, 0.0)
    back, fwd = cg * jnp.maximum(vp, 0.0), -cg * jnp.minimum(vp, 0.0)
    w_in, w_out, w_back, w_fwd = into + viscous, out + viscous, back + vg2, fwd + vg2

    def moved(i):
        u = f[i]
        polar = (u + u) - 2.0 * u
        return (
            u + viscous * polar
            + (w_out * (outer[i] - u) - w_in * (u - inner[i]))
            + (w_fwd * (ahead[i] - u) - w_back * (u - behind[i]))
        )

    def advected(i):
        u = f[i]
        return (
            u
            + (out * (outer[i] - u) - into * (u - inner[i]))
            + (fwd * (ahead[i] - u) - back * (u - behind[i]))
        )

    def dr(i):
        return outer[i] - inner[i]

    def dp(i):
        return ahead[i] - behind[i]

    half = 0.5 * courant
    half_g = 0.5 * cg
    diverge = dr(1) + inverse * dp(2)
    return [
        lambda: advected(0) - half * diverge,
        lambda: moved(1) - half * (temper * dr(0) + dr(4)) + half_g * vp * vp,
        lambda: moved(2) - half_g * (temper * dp(0) + dp(4) + vr * vp),
        lambda: moved(3),
        lambda: moved(4) - (0.4 * half) * temper * diverge,
    ]


def rotate(u, index, lag):
    tiles = u.shape[1] // LANES
    g = [
        jnp.take_along_axis(u[:, q * LANES : (q + 1) * LANES], index, axis=1)
        for q in range(tiles)
    ]
    out = []
    for q in range(tiles):
        value = g[(q - (SMAX // LANES + 1)) % tiles]
        for back in range(SMAX // LANES, -1, -1):
            value = jnp.where(lag == back, g[(q - back) % tiles], value)
        out.append(value)
    return jnp.concatenate(out, axis=1)


def kernel(
    n, nr, f_hbm, s_hbm, recv2, f_ref, s_ref, z, send, recv, halo, eout, edge, send2,
    ssem, rsem, esend, erecv, ssem2, rsem2, isem,
):
    loads = [
        pltpu.make_async_copy(f_hbm, f_ref, isem.at[0]),
        pltpu.make_async_copy(s_hbm, s_ref, isem.at[1]),
    ]
    for load in loads:
        load.start()
    r = lax.axis_index("rad")
    t = lax.axis_index("azi")
    tiles = f_ref.shape[3] // SUB
    chip, core = lax.div(t, 2), lax.rem(t, 2)
    chips = n // 2
    opposite = chips - 1 - chip
    beside, across = chip + 1 - 2 * lax.rem(chip, 2), lax.rem(chip + 2, chips)
    first = jnp.where(core == 0, across, beside)
    second = jnp.where(core == 0, beside, across)
    order = [opposite, first, second]
    peers = [2 * c + h for c in order for h in (core, 1 - core)] + [2 * chip + 1 - core]
    top_edge = (t == 0) & (r > 0)
    bottom_edge = (t == n - 1) & (r < nr - 1)

    barrier = pltpu.get_barrier_semaphore()
    for peer in peers:
        pl.semaphore_signal(barrier, inc=1, device_id={"azi": peer})

    @pl.when(top_edge)
    def _():
        for b in range(n):
            pl.semaphore_signal(barrier, inc=1, device_id={"rad": r - 1, "azi": b})

    @pl.when(bottom_edge)
    def _():
        for b in range(n):
            pl.semaphore_signal(barrier, inc=1, device_id={"rad": r + 1, "azi": b})

    sub = lax.broadcasted_iota(jnp.int32, (SUB, LANES), 0)
    lane = lax.broadcasted_iota(jnp.int32, (SUB, LANES), 1)
    low = lane < HALF

    def edge_copy(which, slot, device):
        return pltpu.make_async_remote_copy(
            src_ref=eout.at[which], dst_ref=edge.at[slot], send_sem=esend.at[which],
            recv_sem=erecv, device_id=device,
        )

    to_inner = edge_copy(0, t, {"rad": r - 1, "azi": n - 1})
    to_outer = edge_copy(1, t, {"rad": r + 1, "azi": 0})

    for load in loads:
        load.wait()
    for p, fs in enumerate(PAIRS):
        if p < 2:
            stack = f_ref[fs, 0].reshape(LANES, LANES)
        else:
            shifts = s_ref[...].astype(jnp.float32)
            rest = jnp.zeros((HALF - STEPS, LANES), jnp.float32)
            stack = jnp.concatenate([f_ref[4, 0], shifts, rest], axis=0)
        z[:, p] = stack.T.reshape(tiles, SUB, LANES)

    def halo_tile(p, k):
        above, below = jnp.maximum(2 * k - 1, 0), jnp.minimum(2 * k + 2, tiles - 1)
        return jnp.where(sub >= SUB - STEPS, z[above, p], z[below, p])

    for k in range(n):
        a, b = 2 * k, 2 * k + 1
        for p in range(2):
            send[k, 2 * p] = z[a, p]
            send[k, 2 * p + 1] = z[b, p]
        send[k, 4] = jnp.where(low, z[a, 2], pltpu.roll(z[b, 2], HALF, 1))
        last = halo_tile(2, k)
        free = jnp.where(low, pltpu.roll(last, 3, 0), pltpu.roll(pltpu.roll(last, 6, 0), HALF, 1))
        send[k, 5] = jnp.where((sub == 3) | (sub == 4), free, halo_tile(0, k))
        send[k, 6] = jnp.where(sub == 3, pltpu.roll(free, 6, 0), halo_tile(1, k))
    eout[0, 0] = jnp.where(sub < 4, z[0, 0], pltpu.roll(z[0, 1], 4, 0))
    eout[1, 0] = jnp.where(sub < 4, pltpu.roll(z[tiles - 1, 1], 4, 0), z[tiles - 1, 0])
    eout[0, 1] = z[0, 2]
    eout[1, 1] = z[tiles - 1, 2]

    needed = n - 1 + (r > 0).astype(jnp.int32) + (r < nr - 1).astype(jnp.int32)
    pl.semaphore_wait(barrier, needed)

    @pl.when(r > 0)
    def _():
        to_inner.start()

    @pl.when(r < nr - 1)
    def _():
        to_outer.start()

    def to_peer(src, dst, send_sem, recv_sem, peer):
        return pltpu.make_async_remote_copy(
            src_ref=src, dst_ref=dst, send_sem=send_sem, recv_sem=recv_sem,
            device_id={"azi": peer},
        )

    for peer in peers:
        to_peer(send.at[peer], recv.at[t], ssem, rsem, peer).start()
    there = to_peer(send.at[1:], recv.at[1:], ssem, rsem, peers[0])
    recv[t] = send[t]

    rows = 3 * SUB
    width = n * HALF
    row = lax.broadcasted_iota(jnp.int32, (rows, width), 0)
    row = jnp.where(row < 2 * SUB + SUB // 2, row, row - rows)
    row = row + (r * f_ref.shape[3] + t * (2 * SUB))
    total = nr * f_ref.shape[3]
    inside = (row >= 0) & (row < total)
    radius = 1.0 + (row.astype(jnp.float32) + 0.5) / jnp.float32(total)
    inverse = 1.0 / radius

    own = 2 * SUB

    def inner_rows(u):
        return jnp.concatenate([u[:own], jnp.where(inside[own:], u[own:], 0.0)], axis=0)

    there.wait_recv()
    own_shifts = halo_tile(2, t)
    for b in range(n):
        free = jnp.where(sub == 5, pltpu.roll(recv[b, 6], 2, 0), recv[b, 5])
        bottom, top = pltpu.roll(free, 5, 0), pltpu.roll(pltpu.roll(free, 2, 0), HALF, 1)
        halo[b] = jnp.where(low, jnp.where(sub < 4, bottom, top), own_shifts)

    @pl.when(top_edge | bottom_edge)
    def _():
        first = jnp.where(t == 0, SUB - STEPS, 0)
        last = jnp.where(t == 0, SUB, STEPS)
        take = (sub >= first) & (sub < last)
        pltpu.make_async_remote_copy(
            src_ref=recv.at[:, :2], dst_ref=edge, send_sem=esend.at[0], recv_sem=erecv,
            device_id={"rad": lax.rem(r + 1, nr)},
        ).wait_recv()
        for b in range(n):
            recv[b, 5] = jnp.where(take, edge[b, 0], recv[b, 5])
            recv[b, 6] = jnp.where(take, pltpu.roll(edge[b, 0], 4, 0), recv[b, 6])
            halo[b] = jnp.where(take, edge[b, 1], halo[b])

    fields = [[] for _ in range(FIELDS)]
    for q in range(n // 2):
        got = [halves(recv[2 * q, i], recv[2 * q + 1, i], low) for i in range(7)]
        for p in range(2):
            for h in range(2):
                tiles_of = (got[2 * p][h], got[2 * p + 1][h], got[5 + p][h])
                fields[2 * p + h].append(jnp.concatenate(tiles_of, axis=0))
        last = jnp.where(low, halo[2 * q], pltpu.roll(halo[2 * q + 1], HALF, 1))
        fields[4].append(jnp.concatenate([got[4][0], got[4][1], last], axis=0))
    fields = [inner_rows(jnp.concatenate(u, axis=1)) for u in fields]

    carried = jnp.concatenate([z[2 * t, 2], z[2 * t + 1, 2], halo[0]], axis=0)
    lanes = lax.broadcasted_iota(jnp.int32, (rows, LANES), 1)
    for step in range(STEPS):
        shift = carried[:, HALF + step : HALF + step + 1].astype(jnp.int32)
        shift = jnp.broadcast_to(shift, (rows, LANES))
        whole = jnp.where(shift >= LANES, 1, 0)
        part = shift - whole * LANES
        index = jnp.bitwise_and(lanes - part, LANES - 1)
        lag = whole + jnp.where(lanes < part, 1, 0)
        if step < STEPS - 1:
            fields = [inner_rows(new()) for new in updates(fields, inverse, rows)]
            fields = [rotate(u, index, lag) for u in fields]

    news = updates(fields, inverse, own)
    for p, fs in enumerate(PAIRS):
        pair = [rotate(new(), index[:own], lag[:own]) for new in news[fs]]
        for q in range(n // 2):
            f = [u[:, q * LANES : (q + 1) * LANES] for u in pair]
            if p < 2:
                for i in range(2):
                    rs = slice(i * SUB, (i + 1) * SUB)
                    even, odd = halves(f[0][rs], f[1][rs], low)
                    send2[2 * q, 2 * p + i] = even
                    send2[2 * q + 1, 2 * p + i] = odd
            else:
                even, odd = halves(f[0][:SUB], f[0][SUB:], low)
                send2[2 * q, 4] = even
                send2[2 * q + 1, 4] = odd
    for peer in peers:
        to_peer(send2.at[peer], recv2.at[t], ssem2, rsem2, peer).start()
    back = to_peer(send2.at[1:], recv2.at[1:], ssem2, rsem2, peers[0])
    recv2[t] = send2[t]

    there.wait_send()

    @pl.when(r > 0)
    def _():
        to_inner.wait_send()

    @pl.when(r < nr - 1)
    def _():
        to_outer.wait_send()

    back.wait_recv()

    back.wait_send()


def to_cells(got, o_hbm, out, sem):
    n = got.shape[0]
    writes = []
    for p in range(3):
        fs = slice(2 * p, min(2 * p + 2, FIELDS))
        if p < 2:
            block = got[:, 2 * p : 2 * p + 2].reshape(LANES, LANES)
            out[fs, 0] = block.T.reshape(2, HALF, LANES)
        else:
            parts = []
            for b in range(n):
                tile = got[b, 4]
                parts += [tile, pltpu.roll(tile, HALF, 1)]
            out[4, 0] = jnp.concatenate(parts, axis=0).T[:HALF]
        write = pltpu.make_async_copy(out.at[fs], o_hbm.at[fs], sem.at[p])
        write.start()
        writes.append(write)
    for write in writes:
        write.wait()


def by_cycles(n, nr, fields, shifts):
    tiles = fields.shape[3] // SUB
    tile = (SUB, LANES)
    dma = pltpu.SemaphoreType.DMA
    got = pl.pallas_call(
        functools.partial(kernel, n, nr),
        out_shape=pltpu.VMEM((n, 5) + tile, jnp.float32),
        in_specs=[pl.BlockSpec(memory_space=pltpu.HBM)] * 2,
        out_specs=pl.BlockSpec(memory_space=pltpu.VMEM),
        scratch_shapes=[
            pltpu.VMEM(fields.shape, fields.dtype),
            pltpu.VMEM(shifts.shape, shifts.dtype),
            pltpu.VMEM((tiles, 3) + tile, jnp.float32),
            pltpu.VMEM((n, 7) + tile, jnp.float32),
            pltpu.VMEM((n, 7) + tile, jnp.float32),
            pltpu.VMEM((n,) + tile, jnp.float32),
            pltpu.VMEM((2, 2) + tile, jnp.float32),
            pltpu.VMEM((n, 2) + tile, jnp.float32),
            pltpu.VMEM((n, 5) + tile, jnp.float32),
            dma,
            dma,
            dma((2,)),
            dma,
            dma,
            dma,
            dma((2,)),
        ],
        compiler_params=pltpu.CompilerParams(
            collective_id=0, has_side_effects=True, vmem_limit_bytes=16 * 1024 * 1024
        ),
    )(
        pltpu.with_memory_space_constraint(fields, pltpu.HBM),
        pltpu.with_memory_space_constraint(shifts, pltpu.HBM),
    )
    return pl.pallas_call(
        to_cells,
        out_shape=jax.ShapeDtypeStruct(fields.shape, fields.dtype),
        in_specs=[pl.BlockSpec(memory_space=pltpu.VMEM)],
        out_specs=pl.BlockSpec(memory_space=pltpu.HBM),
        scratch_shapes=[pltpu.VMEM(fields.shape, fields.dtype), dma((3,))],
        compiler_params=pltpu.CompilerParams(vmem_limit_bytes=16 * 1024 * 1024),
    )(got)


def passed_along(value, axis, steps):
    count = lax.axis_size(axis)
    pairs = [(source, (source + steps) % count) for source in range(count)]
    return lax.ppermute(value, axis, pairs)


def padded_2(value, sides, width, wrap):
    for axis, dim in sides:
        count, length = (lax.axis_size(axis), value.shape[dim])
        up = [(i, (i + 1) % count) for i in range(count if wrap else count - 1)]
        down = [(j, i) for i, j in up]
        last = lax.slice_in_dim(value, length - width, length, axis=dim)
        initial = lax.slice_in_dim(value, 0, width, axis=dim)
        before = lax.ppermute(last, axis, up)
        after = lax.ppermute(initial, axis, down)
        value = jnp.concatenate([before, value, after], axis=dim)
    return value


def update(padded, inverse):
    centre = padded[:, :, 1:-1, 1:-1]
    inner = padded[:, :, 1:-1, :-2]
    outer = padded[:, :, 1:-1, 2:]
    behind = padded[:, :, :-2, 1:-1]
    ahead = padded[:, :, 2:, 1:-1]
    polar_pad = jnp.concatenate([centre, centre, centre], axis=1)
    polar_sum = polar_pad[:, 2:] + polar_pad[:, :-2]
    radial_vel = centre[1]
    azim_vel = centre[2]
    advect = courant * (
        jnp.maximum(radial_vel, 0.0) * (centre - inner)
        + jnp.minimum(radial_vel, 0.0) * (outer - centre)
        + inverse
        * (
            jnp.maximum(azim_vel, 0.0) * (centre - behind)
            + jnp.minimum(azim_vel, 0.0) * (ahead - centre)
        )
    )
    laplace = (
        outer
        + inner
        - 2.0 * centre
        + inverse * inverse * (ahead + behind - 2.0 * centre)
        + (polar_sum - 2.0 * centre)
    )
    radial_diff = (outer - inner) * 0.5
    azim_diff = (ahead - behind) * 0.5
    diverge = radial_diff[1] + inverse * azim_diff[2]
    log_rho = centre[0]
    temper = centre[4]
    new_log = log_rho - advect[0] - courant * diverge
    new_radial = (
        radial_vel
        - advect[1]
        - courant * (temper * radial_diff[0] + radial_diff[4])
        + 0.5 * courant * inverse * azim_vel * azim_vel
        + viscous * laplace[1]
    )
    new_azim = (
        azim_vel
        - advect[2]
        - courant * inverse * (temper * azim_diff[0] + azim_diff[4])
        - 0.5 * courant * inverse * radial_vel * azim_vel
        + viscous * laplace[2]
    )
    new_polar = centre[3] - advect[3] + viscous * laplace[3]
    new_temper = temper - advect[4] - courant * 0.4 * temper * diverge + viscous * laplace[4]
    return jnp.stack([new_log, new_radial, new_azim, new_polar, new_temper])


def rotate_pieces(fields, offsets):
    width = fields.shape[2]
    count = (SMAX + width - 1) // width
    pieces = [fields]
    for blocks in range(1, count + 1):
        pieces.append(passed_along(fields, "azi", blocks))
    extended = jnp.concatenate(pieces[::-1], axis=2)
    nbits = SMAX.bit_length()
    reach = (1 << nbits) - 1
    anchor = count * width
    front = jnp.zeros(fields.shape[:2] + (reach - anchor,) + fields.shape[3:], fields.dtype)
    window = jnp.concatenate([front, extended], axis=2)
    for bit in range(nbits):
        amount = 1 << bit
        length = window.shape[2] - amount
        chosen = offsets // amount % 2 == 1
        window = jnp.where(
            chosen[None, None, None, :], window[:, :, :length], window[:, :, amount:]
        )
    return window


def by_blocks(fields, shifts):
    rows = fields.shape[3]
    total_rows = rows * lax.axis_size("rad")
    row_index = lax.axis_index("rad") * rows + jnp.arange(rows, dtype=jnp.int32)
    radius = 1.0 + (row_index.astype(jnp.float32) + 0.5) / jnp.float32(total_rows)
    inverse = 1.0 / radius
    for step in range(STEPS):
        radial_pad = padded_2(fields, (("rad", 3),), 1, False)
        padded = padded_2(radial_pad, (("azi", 2),), 1, True)
        fields = update(padded, inverse)
        fields = rotate_pieces(fields, shifts[step])
    return fields


def local(fields, shifts):
    n, nr = lax.axis_size("azi"), lax.axis_size("rad")
    count, planes, width, rows = fields.shape
    fits = (count, planes, width, rows) == (FIELDS, 1, HALF, LANES)
    if fits and rows == n * 2 * SUB and n * width > SMAX + LANES:
        return by_cycles(n, nr, fields, shifts)
    return by_blocks(fields, shifts)


def solution(mesh):
    placed = (P(None, None, "azi", "rad"), P(None, "rad"))
    return jax.shard_map(
        local, mesh=mesh, in_specs=placed, out_specs=P(None, None, "azi", "rad"), check_vma=False
    )
```

```python
import functools

import jax
import jax.numpy as jnp
from jax import lax
from jax.experimental import pallas as pl
from jax.experimental.pallas import tpu as pltpu
from jax.sharding import PartitionSpec as P

STEPS = 3
SMAX = 192
FIELDS = 5
LANES = 128
SUB = 8
HALF = 64
PAIRS = (slice(0, 2), slice(2, 4), slice(4, 5))

courant = 0.2
viscous = 0.1


def halves(a, b, low):
    first = jnp.where(low, a, pltpu.roll(b, HALF, b.ndim - 1))
    second = jnp.where(low, pltpu.roll(a, HALF, a.ndim - 1), b)
    return first, second


def updates(f, inverse, rows):
    inner = [pltpu.roll(u, 1, 0)[:rows] for u in f]
    outer = [pltpu.roll(u, u.shape[0] - 1, 0)[:rows] for u in f]
    f = [u[:rows] for u in f]
    inverse = inverse[:rows]
    behind = [pltpu.roll(u, 1, 1) for u in f]
    ahead = [pltpu.roll(u, u.shape[1] - 1, 1) for u in f]
    _, vr, vp, _, temper = f
    cg = courant * inverse
    vg2 = viscous * inverse * inverse
    into, out = courant * jnp.maximum(vr, 0.0), -courant * jnp.minimum(vr, 0.0)
    back, fwd = cg * jnp.maximum(vp, 0.0), -cg * jnp.minimum(vp, 0.0)
    w_in, w_out, w_back, w_fwd = into + viscous, out + viscous, back + vg2, fwd + vg2

    def moved(i):
        u = f[i]
        polar = (u + u) - 2.0 * u
        return (
            u + viscous * polar
            + (w_out * (outer[i] - u) - w_in * (u - inner[i]))
            + (w_fwd * (ahead[i] - u) - w_back * (u - behind[i]))
        )

    def advected(i):
        u = f[i]
        return (
            u
            + (out * (outer[i] - u) - into * (u - inner[i]))
            + (fwd * (ahead[i] - u) - back * (u - behind[i]))
        )

    def dr(i):
        return outer[i] - inner[i]

    def dp(i):
        return ahead[i] - behind[i]

    half = 0.5 * courant
    half_g = 0.5 * cg
    diverge = dr(1) + inverse * dp(2)
    return [
        lambda: advected(0) - half * diverge,
        lambda: moved(1) - half * (temper * dr(0) + dr(4)) + half_g * vp * vp,
        lambda: moved(2) - half_g * (temper * dp(0) + dp(4) + vr * vp),
        lambda: moved(3),
        lambda: moved(4) - (0.4 * half) * temper * diverge,
    ]


def rotate(u, index, lag):
    tiles = u.shape[1] // LANES
    g = [
        jnp.take_along_axis(u[:, q * LANES : (q + 1) * LANES], index, axis=1)
        for q in range(tiles)
    ]
    out = []
    for q in range(tiles):
        value = g[(q - (SMAX // LANES + 1)) % tiles]
        for back in range(SMAX // LANES, -1, -1):
            value = jnp.where(lag == back, g[(q - back) % tiles], value)
        out.append(value)
    return jnp.concatenate(out, axis=1)


def kernel(
    n, nr, f_hbm, s_hbm, recv2, f_ref, s_ref, z, send, recv, halo, eout, edge, send2,
    ssem, rsem, esend, erecv, ssem2, rsem2, isem,
):
    loads = [
        pltpu.make_async_copy(f_hbm, f_ref, isem.at[0]),
        pltpu.make_async_copy(s_hbm, s_ref, isem.at[1]),
    ]
    for load in loads:
        load.start()
    r = lax.axis_index("rad")
    t = lax.axis_index("azi")
    tiles = f_ref.shape[3] // SUB
    chip, core = lax.div(t, 2), lax.rem(t, 2)
    chips = n // 2
    opposite = chips - 1 - chip
    beside, across = chip + 1 - 2 * lax.rem(chip, 2), lax.rem(chip + 2, chips)
    first = jnp.where(core == 0, across, beside)
    second = jnp.where(core == 0, beside, across)
    order = [opposite, first, second]
    peers = [2 * c + h for c in order for h in (core, 1 - core)] + [2 * chip + 1 - core]
    top_edge = (t == 0) & (r > 0)
    bottom_edge = (t == n - 1) & (r < nr - 1)

    barrier = pltpu.get_barrier_semaphore()
    for peer in peers:
        pl.semaphore_signal(barrier, inc=1, device_id={"azi": peer})

    @pl.when(top_edge)
    def _():
        for b in range(n):
            pl.semaphore_signal(barrier, inc=1, device_id={"rad": r - 1, "azi": b})

    @pl.when(bottom_edge)
    def _():
        for b in range(n):
            pl.semaphore_signal(barrier, inc=1, device_id={"rad": r + 1, "azi": b})

    sub = lax.broadcasted_iota(jnp.int32, (SUB, LANES), 0)
    lane = lax.broadcasted_iota(jnp.int32, (SUB, LANES), 1)
    low = lane < HALF

    def edge_copy(which, slot, device):
        return pltpu.make_async_remote_copy(
            src_ref=eout.at[which], dst_ref=edge.at[slot], send_sem=esend.at[which],
            recv_sem=erecv, device_id=device,
        )

    to_inner = edge_copy(0, t, {"rad": r - 1, "azi": n - 1})
    to_outer = edge_copy(1, t, {"rad": r + 1, "azi": 0})

    for load in loads:
        load.wait()
    for p, fs in enumerate(PAIRS):
        if p < 2:
            stack = f_ref[fs, 0].reshape(LANES, LANES)
        else:
            shifts = s_ref[...].astype(jnp.float32)
            rest = jnp.zeros((HALF - STEPS, LANES), jnp.float32)
            stack = jnp.concatenate([f_ref[4, 0], shifts, rest], axis=0)
        z[:, p] = stack.T.reshape(tiles, SUB, LANES)

    def halo_tile(p, k):
        above, below = jnp.maximum(2 * k - 1, 0), jnp.minimum(2 * k + 2, tiles - 1)
        return jnp.where(sub >= SUB - STEPS, z[above, p], z[below, p])

    def build(k):
        a, b = 2 * k, 2 * k + 1
        for p in range(2):
            send[k, 2 * p] = z[a, p]
            send[k, 2 * p + 1] = z[b, p]
        send[k, 4] = jnp.where(low, z[a, 2], pltpu.roll(z[b, 2], HALF, 1))
        last = halo_tile(2, k)
        free = jnp.where(low, pltpu.roll(last, 3, 0), pltpu.roll(pltpu.roll(last, 6, 0), HALF, 1))
        send[k, 5] = jnp.where((sub == 3) | (sub == 4), free, halo_tile(0, k))
        send[k, 6] = jnp.where(sub == 3, pltpu.roll(free, 6, 0), halo_tile(1, k))

    build(peers[0])
    eout[0, 0] = jnp.where(sub < 4, z[0, 0], pltpu.roll(z[0, 1], 4, 0))
    eout[1, 0] = jnp.where(sub < 4, pltpu.roll(z[tiles - 1, 1], 4, 0), z[tiles - 1, 0])
    eout[0, 1] = z[0, 2]
    eout[1, 1] = z[tiles - 1, 2]

    needed = n - 1 + (r > 0).astype(jnp.int32) + (r < nr - 1).astype(jnp.int32)
    pl.semaphore_wait(barrier, needed)

    def to_peer(src, dst, send_sem, recv_sem, peer):
        return pltpu.make_async_remote_copy(
            src_ref=src, dst_ref=dst, send_sem=send_sem, recv_sem=recv_sem,
            device_id={"azi": peer},
        )

    for i, peer in enumerate(peers):
        to_peer(send.at[peer], recv.at[t], ssem, rsem, peer).start()
        build(peers[i + 1] if i < n - 2 else t)
        if i == 1:

            @pl.when(r > 0)
            def _():
                to_inner.start()

            @pl.when(r < nr - 1)
            def _():
                to_outer.start()

    there = to_peer(send.at[1:], recv.at[1:], ssem, rsem, peers[0])
    recv[t] = send[t]

    rows = 3 * SUB
    width = n * HALF
    row = lax.broadcasted_iota(jnp.int32, (rows, width), 0)
    row = jnp.where(row < 2 * SUB + SUB // 2, row, row - rows)
    row = row + (r * f_ref.shape[3] + t * (2 * SUB))
    total = nr * f_ref.shape[3]
    inside = (row >= 0) & (row < total)
    radius = 1.0 + (row.astype(jnp.float32) + 0.5) / jnp.float32(total)
    inverse = 1.0 / radius

    own = 2 * SUB

    def inner_rows(u):
        return jnp.concatenate([u[:own], jnp.where(inside[own:], u[own:], 0.0)], axis=0)

    there.wait_recv()
    own_shifts = halo_tile(2, t)
    for b in range(n):
        free = jnp.where(sub == 5, pltpu.roll(recv[b, 6], 2, 0), recv[b, 5])
        bottom, top = pltpu.roll(free, 5, 0), pltpu.roll(pltpu.roll(free, 2, 0), HALF, 1)
        halo[b] = jnp.where(low, jnp.where(sub < 4, bottom, top), own_shifts)

    @pl.when(top_edge | bottom_edge)
    def _():
        first = jnp.where(t == 0, SUB - STEPS, 0)
        last = jnp.where(t == 0, SUB, STEPS)
        take = (sub >= first) & (sub < last)
        pltpu.make_async_remote_copy(
            src_ref=recv.at[:, :2], dst_ref=edge, send_sem=esend.at[0], recv_sem=erecv,
            device_id={"rad": lax.rem(r + 1, nr)},
        ).wait_recv()
        for b in range(n):
            recv[b, 5] = jnp.where(take, edge[b, 0], recv[b, 5])
            recv[b, 6] = jnp.where(take, pltpu.roll(edge[b, 0], 4, 0), recv[b, 6])
            halo[b] = jnp.where(take, edge[b, 1], halo[b])

    fields = [[] for _ in range(FIELDS)]
    for q in range(n // 2):
        got = [halves(recv[2 * q, i], recv[2 * q + 1, i], low) for i in range(7)]
        for p in range(2):
            for h in range(2):
                tiles_of = (got[2 * p][h], got[2 * p + 1][h], got[5 + p][h])
                fields[2 * p + h].append(jnp.concatenate(tiles_of, axis=0))
        last = jnp.where(low, halo[2 * q], pltpu.roll(halo[2 * q + 1], HALF, 1))
        fields[4].append(jnp.concatenate([got[4][0], got[4][1], last], axis=0))
    fields = [inner_rows(jnp.concatenate(u, axis=1)) for u in fields]

    carried = jnp.concatenate([z[2 * t, 2], z[2 * t + 1, 2], halo[0]], axis=0)
    lanes = lax.broadcasted_iota(jnp.int32, (rows, LANES), 1)
    for step in range(STEPS):
        shift = carried[:, HALF + step : HALF + step + 1].astype(jnp.int32)
        shift = jnp.broadcast_to(shift, (rows, LANES))
        whole = jnp.where(shift >= LANES, 1, 0)
        part = shift - whole * LANES
        index = jnp.bitwise_and(lanes - part, LANES - 1)
        lag = whole + jnp.where(lanes < part, 1, 0)
        if step < STEPS - 1:
            fields = [inner_rows(new()) for new in updates(fields, inverse, rows)]
            fields = [rotate(u, index, lag) for u in fields]

    news = updates(fields, inverse, own)
    for p, fs in enumerate(PAIRS):
        pair = [rotate(new(), index[:own], lag[:own]) for new in news[fs]]
        for q in range(n // 2):
            f = [u[:, q * LANES : (q + 1) * LANES] for u in pair]
            if p < 2:
                for i in range(2):
                    rs = slice(i * SUB, (i + 1) * SUB)
                    even, odd = halves(f[0][rs], f[1][rs], low)
                    send2[2 * q, 2 * p + i] = even
                    send2[2 * q + 1, 2 * p + i] = odd
            else:
                even, odd = halves(f[0][:SUB], f[0][SUB:], low)
                send2[2 * q, 4] = even
                send2[2 * q + 1, 4] = odd
    others = [jnp.where(j < chip, j, j + 1) for j in range(chips - 1)]
    for peer in [2 * c + h for c in others for h in (core, 1 - core)] + peers[-1:]:
        to_peer(send2.at[peer], recv2.at[t], ssem2, rsem2, peer).start()
    back = to_peer(send2.at[1:], recv2.at[1:], ssem2, rsem2, peers[0])
    recv2[t] = send2[t]

    there.wait_send()

    @pl.when(r > 0)
    def _():
        to_inner.wait_send()

    @pl.when(r < nr - 1)
    def _():
        to_outer.wait_send()

    back.wait_recv()

    back.wait_send()


def to_cells(got, o_hbm, out, sem):
    n = got.shape[0]
    writes = []
    for p in range(3):
        fs = slice(2 * p, min(2 * p + 2, FIELDS))
        if p < 2:
            block = got[:, 2 * p : 2 * p + 2].reshape(LANES, LANES)
            out[fs, 0] = block.T.reshape(2, HALF, LANES)
        else:
            parts = []
            for b in range(n):
                tile = got[b, 4]
                parts += [tile, pltpu.roll(tile, HALF, 1)]
            out[4, 0] = jnp.concatenate(parts, axis=0).T[:HALF]
        write = pltpu.make_async_copy(out.at[fs], o_hbm.at[fs], sem.at[p])
        write.start()
        writes.append(write)
    for write in writes:
        write.wait()


def by_cycles(n, nr, fields, shifts):
    tiles = fields.shape[3] // SUB
    tile = (SUB, LANES)
    dma = pltpu.SemaphoreType.DMA
    got = pl.pallas_call(
        functools.partial(kernel, n, nr),
        out_shape=pltpu.VMEM((n, 5) + tile, jnp.float32),
        in_specs=[pl.BlockSpec(memory_space=pltpu.HBM)] * 2,
        out_specs=pl.BlockSpec(memory_space=pltpu.VMEM),
        scratch_shapes=[
            pltpu.VMEM(fields.shape, fields.dtype),
            pltpu.VMEM(shifts.shape, shifts.dtype),
            pltpu.VMEM((tiles, 3) + tile, jnp.float32),
            pltpu.VMEM((n, 7) + tile, jnp.float32),
            pltpu.VMEM((n, 7) + tile, jnp.float32),
            pltpu.VMEM((n,) + tile, jnp.float32),
            pltpu.VMEM((2, 2) + tile, jnp.float32),
            pltpu.VMEM((n, 2) + tile, jnp.float32),
            pltpu.VMEM((n, 5) + tile, jnp.float32),
            dma,
            dma,
            dma((2,)),
            dma,
            dma,
            dma,
            dma((2,)),
        ],
        compiler_params=pltpu.CompilerParams(
            collective_id=0, has_side_effects=True, vmem_limit_bytes=16 * 1024 * 1024
        ),
    )(
        pltpu.with_memory_space_constraint(fields, pltpu.HBM),
        pltpu.with_memory_space_constraint(shifts, pltpu.HBM),
    )
    return pl.pallas_call(
        to_cells,
        out_shape=jax.ShapeDtypeStruct(fields.shape, fields.dtype),
        in_specs=[pl.BlockSpec(memory_space=pltpu.VMEM)],
        out_specs=pl.BlockSpec(memory_space=pltpu.HBM),
        scratch_shapes=[pltpu.VMEM(fields.shape, fields.dtype), dma((3,))],
        compiler_params=pltpu.CompilerParams(vmem_limit_bytes=16 * 1024 * 1024),
    )(got)


def passed_along(value, axis, steps):
    count = lax.axis_size(axis)
    pairs = [(source, (source + steps) % count) for source in range(count)]
    return lax.ppermute(value, axis, pairs)


def padded_2(value, sides, width, wrap):
    for axis, dim in sides:
        count, length = (lax.axis_size(axis), value.shape[dim])
        up = [(i, (i + 1) % count) for i in range(count if wrap else count - 1)]
        down = [(j, i) for i, j in up]
        last = lax.slice_in_dim(value, length - width, length, axis=dim)
        initial = lax.slice_in_dim(value, 0, width, axis=dim)
        before = lax.ppermute(last, axis, up)
        after = lax.ppermute(initial, axis, down)
        value = jnp.concatenate([before, value, after], axis=dim)
    return value


def update(padded, inverse):
    centre = padded[:, :, 1:-1, 1:-1]
    inner = padded[:, :, 1:-1, :-2]
    outer = padded[:, :, 1:-1, 2:]
    behind = padded[:, :, :-2, 1:-1]
    ahead = padded[:, :, 2:, 1:-1]
    polar_pad = jnp.concatenate([centre, centre, centre], axis=1)
    polar_sum = polar_pad[:, 2:] + polar_pad[:, :-2]
    radial_vel = centre[1]
    azim_vel = centre[2]
    advect = courant * (
        jnp.maximum(radial_vel, 0.0) * (centre - inner)
        + jnp.minimum(radial_vel, 0.0) * (outer - centre)
        + inverse
        * (
            jnp.maximum(azim_vel, 0.0) * (centre - behind)
            + jnp.minimum(azim_vel, 0.0) * (ahead - centre)
        )
    )
    laplace = (
        outer
        + inner
        - 2.0 * centre
        + inverse * inverse * (ahead + behind - 2.0 * centre)
        + (polar_sum - 2.0 * centre)
    )
    radial_diff = (outer - inner) * 0.5
    azim_diff = (ahead - behind) * 0.5
    diverge = radial_diff[1] + inverse * azim_diff[2]
    log_rho = centre[0]
    temper = centre[4]
    new_log = log_rho - advect[0] - courant * diverge
    new_radial = (
        radial_vel
        - advect[1]
        - courant * (temper * radial_diff[0] + radial_diff[4])
        + 0.5 * courant * inverse * azim_vel * azim_vel
        + viscous * laplace[1]
    )
    new_azim = (
        azim_vel
        - advect[2]
        - courant * inverse * (temper * azim_diff[0] + azim_diff[4])
        - 0.5 * courant * inverse * radial_vel * azim_vel
        + viscous * laplace[2]
    )
    new_polar = centre[3] - advect[3] + viscous * laplace[3]
    new_temper = temper - advect[4] - courant * 0.4 * temper * diverge + viscous * laplace[4]
    return jnp.stack([new_log, new_radial, new_azim, new_polar, new_temper])


def rotate_pieces(fields, offsets):
    width = fields.shape[2]
    count = (SMAX + width - 1) // width
    pieces = [fields]
    for blocks in range(1, count + 1):
        pieces.append(passed_along(fields, "azi", blocks))
    extended = jnp.concatenate(pieces[::-1], axis=2)
    nbits = SMAX.bit_length()
    reach = (1 << nbits) - 1
    anchor = count * width
    front = jnp.zeros(fields.shape[:2] + (reach - anchor,) + fields.shape[3:], fields.dtype)
    window = jnp.concatenate([front, extended], axis=2)
    for bit in range(nbits):
        amount = 1 << bit
        length = window.shape[2] - amount
        chosen = offsets // amount % 2 == 1
        window = jnp.where(
            chosen[None, None, None, :], window[:, :, :length], window[:, :, amount:]
        )
    return window


def by_blocks(fields, shifts):
    rows = fields.shape[3]
    total_rows = rows * lax.axis_size("rad")
    row_index = lax.axis_index("rad") * rows + jnp.arange(rows, dtype=jnp.int32)
    radius = 1.0 + (row_index.astype(jnp.float32) + 0.5) / jnp.float32(total_rows)
    inverse = 1.0 / radius
    for step in range(STEPS):
        radial_pad = padded_2(fields, (("rad", 3),), 1, False)
        padded = padded_2(radial_pad, (("azi", 2),), 1, True)
        fields = update(padded, inverse)
        fields = rotate_pieces(fields, shifts[step])
    return fields


def local(fields, shifts):
    n, nr = lax.axis_size("azi"), lax.axis_size("rad")
    count, planes, width, rows = fields.shape
    fits = (count, planes, width, rows) == (FIELDS, 1, HALF, LANES)
    if fits and rows == n * 2 * SUB and n * width > SMAX + LANES:
        return by_cycles(n, nr, fields, shifts)
    return by_blocks(fields, shifts)


def solution(mesh):
    placed = (P(None, None, "azi", "rad"), P(None, "rad"))
    return jax.shard_map(
        local, mesh=mesh, in_specs=placed, out_specs=P(None, None, "azi", "rad"), check_vma=False
    )
```

```python
import functools

import jax
import jax.numpy as jnp
from jax import lax
from jax.experimental import pallas as pl
from jax.experimental.pallas import tpu as pltpu
from jax.sharding import PartitionSpec as P

STEPS = 3
SMAX = 192
FIELDS = 5
LANES = 128
SUB = 8
HALF = 64
PAIRS = (slice(0, 2), slice(2, 4), slice(4, 5))

courant = 0.2
viscous = 0.1


def halves(a, b, low):
    first = jnp.where(low, a, pltpu.roll(b, HALF, b.ndim - 1))
    second = jnp.where(low, pltpu.roll(a, HALF, a.ndim - 1), b)
    return first, second


def around(ref, f):
    for i, u in enumerate(f):
        ref[i, :SUB] = u[2 * SUB :]
        ref[i, SUB : 4 * SUB] = u
        ref[i, 4 * SUB :] = u[:SUB]


def updates(ref, inverse, rows):
    inner = [ref[i, SUB - 1 : SUB - 1 + rows] for i in range(FIELDS)]
    outer = [ref[i, SUB + 1 : SUB + 1 + rows] for i in range(FIELDS)]
    f = [ref[i, SUB : SUB + rows] for i in range(FIELDS)]
    inverse = inverse[:rows]
    behind = [pltpu.roll(u, 1, 1) for u in f]
    ahead = [pltpu.roll(u, u.shape[1] - 1, 1) for u in f]
    _, vr, vp, _, temper = f
    cg = courant * inverse
    vg2 = viscous * inverse * inverse
    into, out = courant * jnp.maximum(vr, 0.0), -courant * jnp.minimum(vr, 0.0)
    back, fwd = cg * jnp.maximum(vp, 0.0), -cg * jnp.minimum(vp, 0.0)
    w_in, w_out, w_back, w_fwd = into + viscous, out + viscous, back + vg2, fwd + vg2

    def moved(i):
        u = f[i]
        polar = (u + u) - 2.0 * u
        return (
            u + viscous * polar
            + (w_out * (outer[i] - u) - w_in * (u - inner[i]))
            + (w_fwd * (ahead[i] - u) - w_back * (u - behind[i]))
        )

    def advected(i):
        u = f[i]
        return (
            u
            + (out * (outer[i] - u) - into * (u - inner[i]))
            + (fwd * (ahead[i] - u) - back * (u - behind[i]))
        )

    def dr(i):
        return outer[i] - inner[i]

    def dp(i):
        return ahead[i] - behind[i]

    half = 0.5 * courant
    half_g = 0.5 * cg
    diverge = dr(1) + inverse * dp(2)
    return [
        lambda: advected(0) - half * diverge,
        lambda: moved(1) - half * (temper * dr(0) + dr(4)) + half_g * vp * vp,
        lambda: moved(2) - half_g * (temper * dp(0) + dp(4) + vr * vp),
        lambda: moved(3),
        lambda: moved(4) - (0.4 * half) * temper * diverge,
    ]


def rotate(u, index, lag):
    tiles = u.shape[1] // LANES
    g = [
        jnp.take_along_axis(u[:, q * LANES : (q + 1) * LANES], index, axis=1, mode="promise_in_bounds")
        for q in range(tiles)
    ]
    out = []
    for q in range(tiles):
        value = g[(q - (SMAX // LANES + 1)) % tiles]
        for back in range(SMAX // LANES, -1, -1):
            value = jnp.where(lag == back, g[(q - back) % tiles], value)
        out.append(value)
    return jnp.concatenate(out, axis=1)


def kernel(
    n, nr, f_hbm, s_hbm, recv2, f_ref, s_ref, z, send, recv, halo, eout, edge, send2, ring,
    ssem, rsem, esend, erecv, ssem2, rsem2, isem,
):
    loads = [
        pltpu.make_async_copy(f_hbm, f_ref, isem.at[0]),
        pltpu.make_async_copy(s_hbm, s_ref, isem.at[1]),
    ]
    for load in loads:
        load.start()
    r = lax.axis_index("rad")
    t = lax.axis_index("azi")
    tiles = f_ref.shape[3] // SUB
    chip, core = lax.div(t, 2), lax.rem(t, 2)
    chips = n // 2
    opposite = chips - 1 - chip
    beside, across = chip + 1 - 2 * lax.rem(chip, 2), lax.rem(chip + 2, chips)
    first = jnp.where(core == 0, across, beside)
    second = jnp.where(core == 0, beside, across)
    order = [opposite, first, second]
    peers = [2 * c + h for c in order for h in (core, 1 - core)] + [2 * chip + 1 - core]
    top_edge = (t == 0) & (r > 0)
    bottom_edge = (t == n - 1) & (r < nr - 1)

    barrier = pltpu.get_barrier_semaphore()
    for peer in peers:
        pl.semaphore_signal(barrier, inc=1, device_id={"azi": peer})

    @pl.when(top_edge)
    def _():
        for b in range(n):
            pl.semaphore_signal(barrier, inc=1, device_id={"rad": r - 1, "azi": b})

    @pl.when(bottom_edge)
    def _():
        for b in range(n):
            pl.semaphore_signal(barrier, inc=1, device_id={"rad": r + 1, "azi": b})

    sub = lax.broadcasted_iota(jnp.int32, (SUB, LANES), 0)
    lane = lax.broadcasted_iota(jnp.int32, (SUB, LANES), 1)
    low = lane < HALF

    def edge_copy(which, slot, device):
        return pltpu.make_async_remote_copy(
            src_ref=eout.at[which], dst_ref=edge.at[slot], send_sem=esend.at[which],
            recv_sem=erecv, device_id=device,
        )

    to_inner = edge_copy(0, t, {"rad": r - 1, "azi": n - 1})
    to_outer = edge_copy(1, t, {"rad": r + 1, "azi": 0})

    for load in loads:
        load.wait()
    for p, fs in enumerate(PAIRS):
        if p < 2:
            stack = f_ref[fs, 0].reshape(LANES, LANES)
        else:
            shifts = s_ref[...].astype(jnp.float32)
            rest = jnp.zeros((HALF - STEPS, LANES), jnp.float32)
            stack = jnp.concatenate([f_ref[4, 0], shifts, rest], axis=0)
        z[:, p] = stack.T.reshape(tiles, SUB, LANES)

    def halo_tile(p, k):
        above, below = jnp.maximum(2 * k - 1, 0), jnp.minimum(2 * k + 2, tiles - 1)
        return jnp.where(sub >= SUB - STEPS, z[above, p], z[below, p])

    def build(k):
        a, b = 2 * k, 2 * k + 1
        for p in range(2):
            send[k, 2 * p] = z[a, p]
            send[k, 2 * p + 1] = z[b, p]
        send[k, 4] = jnp.where(low, z[a, 2], pltpu.roll(z[b, 2], HALF, 1))
        last = halo_tile(2, k)
        free = jnp.where(low, pltpu.roll(last, 3, 0), pltpu.roll(pltpu.roll(last, 6, 0), HALF, 1))
        send[k, 5] = jnp.where((sub == 3) | (sub == 4), free, halo_tile(0, k))
        send[k, 6] = jnp.where(sub == 3, pltpu.roll(free, 6, 0), halo_tile(1, k))

    build(peers[0])
    eout[0, 0] = jnp.where(sub < 4, z[0, 0], pltpu.roll(z[0, 1], 4, 0))
    eout[1, 0] = jnp.where(sub < 4, pltpu.roll(z[tiles - 1, 1], 4, 0), z[tiles - 1, 0])
    eout[0, 1] = z[0, 2]
    eout[1, 1] = z[tiles - 1, 2]

    needed = n - 1 + (r > 0).astype(jnp.int32) + (r < nr - 1).astype(jnp.int32)
    pl.semaphore_wait(barrier, needed)

    def to_peer(src, dst, send_sem, recv_sem, peer):
        return pltpu.make_async_remote_copy(
            src_ref=src, dst_ref=dst, send_sem=send_sem, recv_sem=recv_sem,
            device_id={"azi": peer},
        )

    for i, peer in enumerate(peers):
        to_peer(send.at[peer], recv.at[t], ssem, rsem, peer).start()
        build(peers[i + 1] if i < n - 2 else t)
        if i == 1:

            @pl.when(r > 0)
            def _():
                to_inner.start()

            @pl.when(r < nr - 1)
            def _():
                to_outer.start()

    there = to_peer(send.at[1:], recv.at[1:], ssem, rsem, peers[0])
    recv[t] = send[t]

    rows = 3 * SUB
    width = n * HALF
    row = lax.broadcasted_iota(jnp.int32, (rows, width), 0)
    row = jnp.where(row < 2 * SUB + SUB // 2, row, row - rows)
    row = row + (r * f_ref.shape[3] + t * (2 * SUB))
    total = nr * f_ref.shape[3]
    inside = (row >= 0) & (row < total)
    radius = 1.0 + (row.astype(jnp.float32) + 0.5) / jnp.float32(total)
    inverse = 1.0 / radius

    own = 2 * SUB

    def inner_rows(u):
        return jnp.concatenate([u[:own], jnp.where(inside[own:], u[own:], 0.0)], axis=0)

    there.wait_recv()
    own_shifts = halo_tile(2, t)
    for b in range(n):
        free = jnp.where(sub == 5, pltpu.roll(recv[b, 6], 2, 0), recv[b, 5])
        bottom, top = pltpu.roll(free, 5, 0), pltpu.roll(pltpu.roll(free, 2, 0), HALF, 1)
        halo[b] = jnp.where(low, jnp.where(sub < 4, bottom, top), own_shifts)

    @pl.when(top_edge | bottom_edge)
    def _():
        first = jnp.where(t == 0, SUB - STEPS, 0)
        last = jnp.where(t == 0, SUB, STEPS)
        take = (sub >= first) & (sub < last)
        pltpu.make_async_remote_copy(
            src_ref=recv.at[:, :2], dst_ref=edge, send_sem=esend.at[0], recv_sem=erecv,
            device_id={"rad": lax.rem(r + 1, nr)},
        ).wait_recv()
        for b in range(n):
            recv[b, 5] = jnp.where(take, edge[b, 0], recv[b, 5])
            recv[b, 6] = jnp.where(take, pltpu.roll(edge[b, 0], 4, 0), recv[b, 6])
            halo[b] = jnp.where(take, edge[b, 1], halo[b])

    fields = [[] for _ in range(FIELDS)]
    for q in range(n // 2):
        got = [halves(recv[2 * q, i], recv[2 * q + 1, i], low) for i in range(7)]
        for p in range(2):
            for h in range(2):
                tiles_of = (got[2 * p][h], got[2 * p + 1][h], got[5 + p][h])
                fields[2 * p + h].append(jnp.concatenate(tiles_of, axis=0))
        last = jnp.where(low, halo[2 * q], pltpu.roll(halo[2 * q + 1], HALF, 1))
        fields[4].append(jnp.concatenate([got[4][0], got[4][1], last], axis=0))
    fields = [inner_rows(jnp.concatenate(u, axis=1)) for u in fields]

    carried = jnp.concatenate([z[2 * t, 2], z[2 * t + 1, 2], halo[0]], axis=0)
    lanes = lax.broadcasted_iota(jnp.int32, (rows, LANES), 1)
    for step in range(STEPS):
        shift = carried[:, HALF + step : HALF + step + 1].astype(jnp.int32)
        shift = jnp.broadcast_to(shift, (rows, LANES))
        whole = jnp.where(shift >= LANES, 1, 0)
        part = shift - whole * LANES
        index = jnp.bitwise_and(lanes - part, LANES - 1)
        lag = whole + jnp.where(lanes < part, 1, 0)
        if step < STEPS - 1:
            around(ring.at[step % 2], fields)
            news = updates(ring.at[step % 2], inverse, rows)
            fields = [inner_rows(new()) for new in news]
            fields = [rotate(u, index, lag) for u in fields]

    around(ring.at[(STEPS - 1) % 2], fields)
    news = updates(ring.at[(STEPS - 1) % 2], inverse, own)
    for p, fs in enumerate(PAIRS):
        pair = [rotate(new(), index[:own], lag[:own]) for new in news[fs]]
        for q in range(n // 2):
            f = [u[:, q * LANES : (q + 1) * LANES] for u in pair]
            if p < 2:
                for i in range(2):
                    rs = slice(i * SUB, (i + 1) * SUB)
                    even, odd = halves(f[0][rs], f[1][rs], low)
                    send2[2 * q, 2 * p + i] = even
                    send2[2 * q + 1, 2 * p + i] = odd
            else:
                even, odd = halves(f[0][:SUB], f[0][SUB:], low)
                send2[2 * q, 4] = even
                send2[2 * q + 1, 4] = odd
    others = [jnp.where(j < chip, j, j + 1) for j in range(chips - 1)]
    for peer in [2 * c + h for c in others for h in (core, 1 - core)] + peers[-1:]:
        to_peer(send2.at[peer], recv2.at[t], ssem2, rsem2, peer).start()
    back = to_peer(send2.at[1:], recv2.at[1:], ssem2, rsem2, peers[0])
    recv2[t] = send2[t]

    there.wait_send()

    @pl.when(r > 0)
    def _():
        to_inner.wait_send()

    @pl.when(r < nr - 1)
    def _():
        to_outer.wait_send()

    back.wait_recv()

    back.wait_send()


def to_cells(got, o_hbm, out, sem):
    n = got.shape[0]
    writes = []
    for p in range(3):
        fs = slice(2 * p, min(2 * p + 2, FIELDS))
        if p < 2:
            block = got[:, 2 * p : 2 * p + 2].reshape(LANES, LANES)
            out[fs, 0] = block.T.reshape(2, HALF, LANES)
        else:
            parts = []
            for b in range(n):
                tile = got[b, 4]
                parts += [tile, pltpu.roll(tile, HALF, 1)]
            out[4, 0] = jnp.concatenate(parts, axis=0).T[:HALF]
        write = pltpu.make_async_copy(out.at[fs], o_hbm.at[fs], sem.at[p])
        write.start()
        writes.append(write)
    for write in writes:
        write.wait()


def by_cycles(n, nr, fields, shifts):
    tiles = fields.shape[3] // SUB
    tile = (SUB, LANES)
    dma = pltpu.SemaphoreType.DMA
    got = pl.pallas_call(
        functools.partial(kernel, n, nr),
        out_shape=pltpu.VMEM((n, 5) + tile, jnp.float32),
        in_specs=[pl.BlockSpec(memory_space=pltpu.HBM)] * 2,
        out_specs=pl.BlockSpec(memory_space=pltpu.VMEM),
        scratch_shapes=[
            pltpu.VMEM(fields.shape, fields.dtype),
            pltpu.VMEM(shifts.shape, shifts.dtype),
            pltpu.VMEM((tiles, 3) + tile, jnp.float32),
            pltpu.VMEM((n, 7) + tile, jnp.float32),
            pltpu.VMEM((n, 7) + tile, jnp.float32),
            pltpu.VMEM((n,) + tile, jnp.float32),
            pltpu.VMEM((2, 2) + tile, jnp.float32),
            pltpu.VMEM((n, 2) + tile, jnp.float32),
            pltpu.VMEM((n, 5) + tile, jnp.float32),
            pltpu.VMEM((2, FIELDS, 5 * SUB, n * HALF), jnp.float32),
            dma,
            dma,
            dma((2,)),
            dma,
            dma,
            dma,
            dma((2,)),
        ],
        compiler_params=pltpu.CompilerParams(
            collective_id=0, has_side_effects=True, vmem_limit_bytes=16 * 1024 * 1024
        ),
    )(
        pltpu.with_memory_space_constraint(fields, pltpu.HBM),
        pltpu.with_memory_space_constraint(shifts, pltpu.HBM),
    )
    return pl.pallas_call(
        to_cells,
        out_shape=jax.ShapeDtypeStruct(fields.shape, fields.dtype),
        in_specs=[pl.BlockSpec(memory_space=pltpu.VMEM)],
        out_specs=pl.BlockSpec(memory_space=pltpu.HBM),
        scratch_shapes=[pltpu.VMEM(fields.shape, fields.dtype), dma((3,))],
        compiler_params=pltpu.CompilerParams(vmem_limit_bytes=16 * 1024 * 1024),
    )(got)


def passed_along(value, axis, steps):
    count = lax.axis_size(axis)
    pairs = [(source, (source + steps) % count) for source in range(count)]
    return lax.ppermute(value, axis, pairs)


def padded_2(value, sides, width, wrap):
    for axis, dim in sides:
        count, length = (lax.axis_size(axis), value.shape[dim])
        up = [(i, (i + 1) % count) for i in range(count if wrap else count - 1)]
        down = [(j, i) for i, j in up]
        last = lax.slice_in_dim(value, length - width, length, axis=dim)
        initial = lax.slice_in_dim(value, 0, width, axis=dim)
        before = lax.ppermute(last, axis, up)
        after = lax.ppermute(initial, axis, down)
        value = jnp.concatenate([before, value, after], axis=dim)
    return value


def update(padded, inverse):
    centre = padded[:, :, 1:-1, 1:-1]
    inner = padded[:, :, 1:-1, :-2]
    outer = padded[:, :, 1:-1, 2:]
    behind = padded[:, :, :-2, 1:-1]
    ahead = padded[:, :, 2:, 1:-1]
    polar_pad = jnp.concatenate([centre, centre, centre], axis=1)
    polar_sum = polar_pad[:, 2:] + polar_pad[:, :-2]
    radial_vel = centre[1]
    azim_vel = centre[2]
    advect = courant * (
        jnp.maximum(radial_vel, 0.0) * (centre - inner)
        + jnp.minimum(radial_vel, 0.0) * (outer - centre)
        + inverse
        * (
            jnp.maximum(azim_vel, 0.0) * (centre - behind)
            + jnp.minimum(azim_vel, 0.0) * (ahead - centre)
        )
    )
    laplace = (
        outer
        + inner
        - 2.0 * centre
        + inverse * inverse * (ahead + behind - 2.0 * centre)
        + (polar_sum - 2.0 * centre)
    )
    radial_diff = (outer - inner) * 0.5
    azim_diff = (ahead - behind) * 0.5
    diverge = radial_diff[1] + inverse * azim_diff[2]
    log_rho = centre[0]
    temper = centre[4]
    new_log = log_rho - advect[0] - courant * diverge
    new_radial = (
        radial_vel
        - advect[1]
        - courant * (temper * radial_diff[0] + radial_diff[4])
        + 0.5 * courant * inverse * azim_vel * azim_vel
        + viscous * laplace[1]
    )
    new_azim = (
        azim_vel
        - advect[2]
        - courant * inverse * (temper * azim_diff[0] + azim_diff[4])
        - 0.5 * courant * inverse * radial_vel * azim_vel
        + viscous * laplace[2]
    )
    new_polar = centre[3] - advect[3] + viscous * laplace[3]
    new_temper = temper - advect[4] - courant * 0.4 * temper * diverge + viscous * laplace[4]
    return jnp.stack([new_log, new_radial, new_azim, new_polar, new_temper])


def rotate_pieces(fields, offsets):
    width = fields.shape[2]
    count = (SMAX + width - 1) // width
    pieces = [fields]
    for blocks in range(1, count + 1):
        pieces.append(passed_along(fields, "azi", blocks))
    extended = jnp.concatenate(pieces[::-1], axis=2)
    nbits = SMAX.bit_length()
    reach = (1 << nbits) - 1
    anchor = count * width
    front = jnp.zeros(fields.shape[:2] + (reach - anchor,) + fields.shape[3:], fields.dtype)
    window = jnp.concatenate([front, extended], axis=2)
    for bit in range(nbits):
        amount = 1 << bit
        length = window.shape[2] - amount
        chosen = offsets // amount % 2 == 1
        window = jnp.where(
            chosen[None, None, None, :], window[:, :, :length], window[:, :, amount:]
        )
    return window


def by_blocks(fields, shifts):
    rows = fields.shape[3]
    total_rows = rows * lax.axis_size("rad")
    row_index = lax.axis_index("rad") * rows + jnp.arange(rows, dtype=jnp.int32)
    radius = 1.0 + (row_index.astype(jnp.float32) + 0.5) / jnp.float32(total_rows)
    inverse = 1.0 / radius
    for step in range(STEPS):
        radial_pad = padded_2(fields, (("rad", 3),), 1, False)
        padded = padded_2(radial_pad, (("azi", 2),), 1, True)
        fields = update(padded, inverse)
        fields = rotate_pieces(fields, shifts[step])
    return fields


def local(fields, shifts):
    n, nr = lax.axis_size("azi"), lax.axis_size("rad")
    count, planes, width, rows = fields.shape
    fits = (count, planes, width, rows) == (FIELDS, 1, HALF, LANES)
    if fits and rows == n * 2 * SUB and n * width > SMAX + LANES:
        return by_cycles(n, nr, fields, shifts)
    return by_blocks(fields, shifts)


def solution(mesh):
    placed = (P(None, None, "azi", "rad"), P(None, "rad"))
    return jax.shard_map(
        local, mesh=mesh, in_specs=placed, out_specs=P(None, None, "azi", "rad"), check_vma=False
    )
```

```python
import functools

import jax
import jax.numpy as jnp
from jax import lax
from jax.experimental import pallas as pl
from jax.experimental.pallas import tpu as pltpu
from jax.sharding import PartitionSpec as P

STEPS = 3
SMAX = 192
FIELDS = 5
LANES = 128
SUB = 8
HALF = 64
PAIRS = (slice(0, 2), slice(2, 4), slice(4, 5))

courant = 0.2
viscous = 0.1


def halves(a, b, low):
    first = jnp.where(low, a, pltpu.roll(b, HALF, b.ndim - 1))
    second = jnp.where(low, pltpu.roll(a, HALF, a.ndim - 1), b)
    return first, second


def updates(f, inverse, rows):
    inner = [pltpu.roll(u, 1, 0)[:rows] for u in f]
    outer = [pltpu.roll(u, u.shape[0] - 1, 0)[:rows] for u in f]
    f = [u[:rows] for u in f]
    inverse = inverse[:rows]
    behind = [pltpu.roll(u, 1, 1) for u in f]
    ahead = [pltpu.roll(u, u.shape[1] - 1, 1) for u in f]
    _, vr, vp, _, temper = f
    cg = courant * inverse
    vg2 = viscous * inverse * inverse
    into, out = courant * jnp.maximum(vr, 0.0), -courant * jnp.minimum(vr, 0.0)
    back, fwd = cg * jnp.maximum(vp, 0.0), -cg * jnp.minimum(vp, 0.0)
    w_in, w_out, w_back, w_fwd = into + viscous, out + viscous, back + vg2, fwd + vg2

    def moved(i):
        u = f[i]
        polar = (u + u) - 2.0 * u
        return (
            u + viscous * polar
            + (w_out * (outer[i] - u) - w_in * (u - inner[i]))
            + (w_fwd * (ahead[i] - u) - w_back * (u - behind[i]))
        )

    def advected(i):
        u = f[i]
        return (
            u
            + (out * (outer[i] - u) - into * (u - inner[i]))
            + (fwd * (ahead[i] - u) - back * (u - behind[i]))
        )

    def dr(i):
        return outer[i] - inner[i]

    def dp(i):
        return ahead[i] - behind[i]

    half = 0.5 * courant
    half_g = 0.5 * cg
    diverge = dr(1) + inverse * dp(2)
    return [
        lambda: advected(0) - half * diverge,
        lambda: moved(1) - half * (temper * dr(0) + dr(4)) + half_g * vp * vp,
        lambda: moved(2) - half_g * (temper * dp(0) + dp(4) + vr * vp),
        lambda: moved(3),
        lambda: moved(4) - (0.4 * half) * temper * diverge,
    ]


def rotate(u, index, lag):
    tiles = u.shape[1] // LANES
    g = [
        jnp.take_along_axis(u[:, q * LANES : (q + 1) * LANES], index, axis=1, mode="promise_in_bounds")
        for q in range(tiles)
    ]
    out = []
    for q in range(tiles):
        value = g[(q - (SMAX // LANES + 1)) % tiles]
        for back in range(SMAX // LANES, -1, -1):
            value = jnp.where(lag == back, g[(q - back) % tiles], value)
        out.append(value)
    return jnp.concatenate(out, axis=1)


def kernel(
    n, nr, f_hbm, s_hbm, recv2, f_ref, s_ref, z, send, recv, halo, eout, edge, send2,
    ssem, rsem, esend, erecv, ssem2, rsem2, isem,
):
    loads = [
        pltpu.make_async_copy(f_hbm, f_ref, isem.at[0]),
        pltpu.make_async_copy(s_hbm, s_ref, isem.at[1]),
    ]
    loads[0].start()
    r = lax.axis_index("rad")
    t = lax.axis_index("azi")
    tiles = f_ref.shape[3] // SUB
    chip, core = lax.div(t, 2), lax.rem(t, 2)
    chips = n // 2
    opposite = chips - 1 - chip
    beside, across = chip + 1 - 2 * lax.rem(chip, 2), lax.rem(chip + 2, chips)
    first = jnp.where(core == 0, across, beside)
    second = jnp.where(core == 0, beside, across)
    order = [opposite, first, second]
    peers = [2 * c + h for c in order for h in (core, 1 - core)] + [2 * chip + 1 - core]
    top_edge = (t == 0) & (r > 0)
    bottom_edge = (t == n - 1) & (r < nr - 1)

    barrier = pltpu.get_barrier_semaphore()
    for peer in peers:
        pl.semaphore_signal(barrier, inc=1, device_id={"azi": peer})

    @pl.when(top_edge)
    def _():
        for b in range(n):
            pl.semaphore_signal(barrier, inc=1, device_id={"rad": r - 1, "azi": b})

    @pl.when(bottom_edge)
    def _():
        for b in range(n):
            pl.semaphore_signal(barrier, inc=1, device_id={"rad": r + 1, "azi": b})

    loads[1].start()
    sub = lax.broadcasted_iota(jnp.int32, (SUB, LANES), 0)
    lane = lax.broadcasted_iota(jnp.int32, (SUB, LANES), 1)
    low = lane < HALF

    def edge_copy(which, slot, device):
        return pltpu.make_async_remote_copy(
            src_ref=eout.at[which], dst_ref=edge.at[slot], send_sem=esend.at[which],
            recv_sem=erecv, device_id=device,
        )

    to_inner = edge_copy(0, t, {"rad": r - 1, "azi": n - 1})
    to_outer = edge_copy(1, t, {"rad": r + 1, "azi": 0})

    loads[0].wait()
    for p, fs in enumerate(PAIRS):
        if p < 2:
            stack = f_ref[fs, 0].reshape(LANES, LANES)
        else:
            loads[1].wait()
            shifts = s_ref[...].astype(jnp.float32)
            rest = jnp.zeros((HALF - STEPS, LANES), jnp.float32)
            stack = jnp.concatenate([f_ref[4, 0], shifts, rest], axis=0)
        z[:, p] = stack.T.reshape(tiles, SUB, LANES)

    def halo_tile(p, k):
        above, below = jnp.maximum(2 * k - 1, 0), jnp.minimum(2 * k + 2, tiles - 1)
        return jnp.where(sub >= SUB - STEPS, z[above, p], z[below, p])

    def build(k):
        a, b = 2 * k, 2 * k + 1
        for p in range(2):
            send[k, 2 * p] = z[a, p]
            send[k, 2 * p + 1] = z[b, p]
        send[k, 4] = jnp.where(low, z[a, 2], pltpu.roll(z[b, 2], HALF, 1))
        last = halo_tile(2, k)
        free = jnp.where(low, pltpu.roll(last, 3, 0), pltpu.roll(pltpu.roll(last, 6, 0), HALF, 1))
        send[k, 5] = jnp.where((sub == 3) | (sub == 4), free, halo_tile(0, k))
        send[k, 6] = jnp.where(sub == 3, pltpu.roll(free, 6, 0), halo_tile(1, k))

    build(peers[0])
    eout[0, 0] = jnp.where(sub < 4, z[0, 0], pltpu.roll(z[0, 1], 4, 0))
    eout[1, 0] = jnp.where(sub < 4, pltpu.roll(z[tiles - 1, 1], 4, 0), z[tiles - 1, 0])
    eout[0, 1] = z[0, 2]
    eout[1, 1] = z[tiles - 1, 2]

    needed = n - 1 + (r > 0).astype(jnp.int32) + (r < nr - 1).astype(jnp.int32)
    pl.semaphore_wait(barrier, needed)

    def to_peer(src, dst, send_sem, recv_sem, peer):
        return pltpu.make_async_remote_copy(
            src_ref=src, dst_ref=dst, send_sem=send_sem, recv_sem=recv_sem,
            device_id={"azi": peer},
        )

    for i, peer in enumerate(peers):
        to_peer(send.at[peer], recv.at[t], ssem, rsem, peer).start()
        build(peers[i + 1] if i < n - 2 else t)
        if i == 1:

            @pl.when(r > 0)
            def _():
                to_inner.start()

            @pl.when(r < nr - 1)
            def _():
                to_outer.start()

    there = to_peer(send.at[1:], recv.at[1:], ssem, rsem, peers[0])
    recv[t] = send[t]

    rows = 3 * SUB
    width = n * HALF
    row = lax.broadcasted_iota(jnp.int32, (rows, width), 0)
    row = jnp.where(row < 2 * SUB + SUB // 2, row, row - rows)
    row = row + (r * f_ref.shape[3] + t * (2 * SUB))
    total = nr * f_ref.shape[3]
    inside = (row >= 0) & (row < total)
    radius = 1.0 + (row.astype(jnp.float32) + 0.5) / jnp.float32(total)
    inverse = 1.0 / radius

    own = 2 * SUB

    def inner_rows(u):
        return jnp.concatenate([u[:own], jnp.where(inside[own:], u[own:], 0.0)], axis=0)

    there.wait_recv()
    own_shifts = halo_tile(2, t)
    for b in range(n):
        free = jnp.where(sub == 5, pltpu.roll(recv[b, 6], 2, 0), recv[b, 5])
        bottom, top = pltpu.roll(free, 5, 0), pltpu.roll(pltpu.roll(free, 2, 0), HALF, 1)
        halo[b] = jnp.where(low, jnp.where(sub < 4, bottom, top), own_shifts)

    @pl.when(top_edge | bottom_edge)
    def _():
        first = jnp.where(t == 0, SUB - STEPS, 0)
        last = jnp.where(t == 0, SUB, STEPS)
        take = (sub >= first) & (sub < last)
        pltpu.make_async_remote_copy(
            src_ref=recv.at[:, :2], dst_ref=edge, send_sem=esend.at[0], recv_sem=erecv,
            device_id={"rad": lax.rem(r + 1, nr)},
        ).wait_recv()
        for b in range(n):
            recv[b, 5] = jnp.where(take, edge[b, 0], recv[b, 5])
            recv[b, 6] = jnp.where(take, pltpu.roll(edge[b, 0], 4, 0), recv[b, 6])
            halo[b] = jnp.where(take, edge[b, 1], halo[b])

    fields = [[] for _ in range(FIELDS)]
    for q in range(n // 2):
        got = [halves(recv[2 * q, i], recv[2 * q + 1, i], low) for i in range(7)]
        for p in range(2):
            for h in range(2):
                tiles_of = (got[2 * p][h], got[2 * p + 1][h], got[5 + p][h])
                fields[2 * p + h].append(jnp.concatenate(tiles_of, axis=0))
        last = jnp.where(low, halo[2 * q], pltpu.roll(halo[2 * q + 1], HALF, 1))
        fields[4].append(jnp.concatenate([got[4][0], got[4][1], last], axis=0))
    fields = [inner_rows(jnp.concatenate(u, axis=1)) for u in fields]

    carried = jnp.concatenate([z[2 * t, 2], z[2 * t + 1, 2], halo[0]], axis=0)
    lanes = lax.broadcasted_iota(jnp.int32, (rows, LANES), 1)
    for step in range(STEPS):
        shift = carried[:, HALF + step : HALF + step + 1].astype(jnp.int32)
        shift = jnp.broadcast_to(shift, (rows, LANES))
        whole = jnp.where(shift >= LANES, 1, 0)
        part = shift - whole * LANES
        index = jnp.bitwise_and(lanes - part, LANES - 1)
        lag = whole + jnp.where(lanes < part, 1, 0)
        if step < STEPS - 1:
            fields = [inner_rows(new()) for new in updates(fields, inverse, rows)]
            fields = [rotate(u, index, lag) for u in fields]

    news = updates(fields, inverse, own)
    for p, fs in enumerate(PAIRS):
        pair = [rotate(new(), index[:own], lag[:own]) for new in news[fs]]
        for q in range(n // 2):
            f = [u[:, q * LANES : (q + 1) * LANES] for u in pair]
            if p < 2:
                for i in range(2):
                    rs = slice(i * SUB, (i + 1) * SUB)
                    even, odd = halves(f[0][rs], f[1][rs], low)
                    send2[2 * q, 2 * p + i] = even
                    send2[2 * q + 1, 2 * p + i] = odd
            else:
                even, odd = halves(f[0][:SUB], f[0][SUB:], low)
                send2[2 * q, 4] = even
                send2[2 * q + 1, 4] = odd
    others = [jnp.where(j < chip, j, j + 1) for j in range(chips - 1)]
    for peer in [2 * c + h for c in others for h in (core, 1 - core)] + peers[-1:]:
        to_peer(send2.at[peer], recv2.at[t], ssem2, rsem2, peer).start()
    back = to_peer(send2.at[1:], recv2.at[1:], ssem2, rsem2, peers[0])
    recv2[t] = send2[t]

    there.wait_send()

    @pl.when(r > 0)
    def _():
        to_inner.wait_send()

    @pl.when(r < nr - 1)
    def _():
        to_outer.wait_send()

    back.wait_recv()

    back.wait_send()


def to_cells(got, o_hbm, out, sem):
    n = got.shape[0]
    writes = []
    for p in range(3):
        fs = slice(2 * p, min(2 * p + 2, FIELDS))
        if p < 2:
            block = got[:, 2 * p : 2 * p + 2].reshape(LANES, LANES)
            out[fs, 0] = block.T.reshape(2, HALF, LANES)
        else:
            parts = []
            for b in range(n):
                tile = got[b, 4]
                parts += [tile, pltpu.roll(tile, HALF, 1)]
            out[4, 0] = jnp.concatenate(parts, axis=0).T[:HALF]
        write = pltpu.make_async_copy(out.at[fs], o_hbm.at[fs], sem.at[p])
        write.start()
        writes.append(write)
    for write in writes:
        write.wait()


def by_cycles(n, nr, fields, shifts):
    tiles = fields.shape[3] // SUB
    tile = (SUB, LANES)
    dma = pltpu.SemaphoreType.DMA
    got = pl.pallas_call(
        functools.partial(kernel, n, nr),
        out_shape=pltpu.VMEM((n, 5) + tile, jnp.float32),
        in_specs=[pl.BlockSpec(memory_space=pltpu.HBM)] * 2,
        out_specs=pl.BlockSpec(memory_space=pltpu.VMEM),
        scratch_shapes=[
            pltpu.VMEM(fields.shape, fields.dtype),
            pltpu.VMEM(shifts.shape, shifts.dtype),
            pltpu.VMEM((tiles, 3) + tile, jnp.float32),
            pltpu.VMEM((n, 7) + tile, jnp.float32),
            pltpu.VMEM((n, 7) + tile, jnp.float32),
            pltpu.VMEM((n,) + tile, jnp.float32),
            pltpu.VMEM((2, 2) + tile, jnp.float32),
            pltpu.VMEM((n, 2) + tile, jnp.float32),
            pltpu.VMEM((n, 5) + tile, jnp.float32),
            dma,
            dma,
            dma((2,)),
            dma,
            dma,
            dma,
            dma((2,)),
        ],
        compiler_params=pltpu.CompilerParams(
            collective_id=0, has_side_effects=True, vmem_limit_bytes=16 * 1024 * 1024
        ),
    )(
        pltpu.with_memory_space_constraint(fields, pltpu.HBM),
        pltpu.with_memory_space_constraint(shifts, pltpu.HBM),
    )
    return pl.pallas_call(
        to_cells,
        out_shape=jax.ShapeDtypeStruct(fields.shape, fields.dtype),
        in_specs=[pl.BlockSpec(memory_space=pltpu.VMEM)],
        out_specs=pl.BlockSpec(memory_space=pltpu.HBM),
        scratch_shapes=[pltpu.VMEM(fields.shape, fields.dtype), dma((3,))],
        compiler_params=pltpu.CompilerParams(vmem_limit_bytes=16 * 1024 * 1024),
    )(got)


def passed_along(value, axis, steps):
    count = lax.axis_size(axis)
    pairs = [(source, (source + steps) % count) for source in range(count)]
    return lax.ppermute(value, axis, pairs)


def padded_2(value, sides, width, wrap):
    for axis, dim in sides:
        count, length = (lax.axis_size(axis), value.shape[dim])
        up = [(i, (i + 1) % count) for i in range(count if wrap else count - 1)]
        down = [(j, i) for i, j in up]
        last = lax.slice_in_dim(value, length - width, length, axis=dim)
        initial = lax.slice_in_dim(value, 0, width, axis=dim)
        before = lax.ppermute(last, axis, up)
        after = lax.ppermute(initial, axis, down)
        value = jnp.concatenate([before, value, after], axis=dim)
    return value


def update(padded, inverse):
    centre = padded[:, :, 1:-1, 1:-1]
    inner = padded[:, :, 1:-1, :-2]
    outer = padded[:, :, 1:-1, 2:]
    behind = padded[:, :, :-2, 1:-1]
    ahead = padded[:, :, 2:, 1:-1]
    polar_pad = jnp.concatenate([centre, centre, centre], axis=1)
    polar_sum = polar_pad[:, 2:] + polar_pad[:, :-2]
    radial_vel = centre[1]
    azim_vel = centre[2]
    advect = courant * (
        jnp.maximum(radial_vel, 0.0) * (centre - inner)
        + jnp.minimum(radial_vel, 0.0) * (outer - centre)
        + inverse
        * (
            jnp.maximum(azim_vel, 0.0) * (centre - behind)
            + jnp.minimum(azim_vel, 0.0) * (ahead - centre)
        )
    )
    laplace = (
        outer
        + inner
        - 2.0 * centre
        + inverse * inverse * (ahead + behind - 2.0 * centre)
        + (polar_sum - 2.0 * centre)
    )
    radial_diff = (outer - inner) * 0.5
    azim_diff = (ahead - behind) * 0.5
    diverge = radial_diff[1] + inverse * azim_diff[2]
    log_rho = centre[0]
    temper = centre[4]
    new_log = log_rho - advect[0] - courant * diverge
    new_radial = (
        radial_vel
        - advect[1]
        - courant * (temper * radial_diff[0] + radial_diff[4])
        + 0.5 * courant * inverse * azim_vel * azim_vel
        + viscous * laplace[1]
    )
    new_azim = (
        azim_vel
        - advect[2]
        - courant * inverse * (temper * azim_diff[0] + azim_diff[4])
        - 0.5 * courant * inverse * radial_vel * azim_vel
        + viscous * laplace[2]
    )
    new_polar = centre[3] - advect[3] + viscous * laplace[3]
    new_temper = temper - advect[4] - courant * 0.4 * temper * diverge + viscous * laplace[4]
    return jnp.stack([new_log, new_radial, new_azim, new_polar, new_temper])


def rotate_pieces(fields, offsets):
    width = fields.shape[2]
    count = (SMAX + width - 1) // width
    pieces = [fields]
    for blocks in range(1, count + 1):
        pieces.append(passed_along(fields, "azi", blocks))
    extended = jnp.concatenate(pieces[::-1], axis=2)
    nbits = SMAX.bit_length()
    reach = (1 << nbits) - 1
    anchor = count * width
    front = jnp.zeros(fields.shape[:2] + (reach - anchor,) + fields.shape[3:], fields.dtype)
    window = jnp.concatenate([front, extended], axis=2)
    for bit in range(nbits):
        amount = 1 << bit
        length = window.shape[2] - amount
        chosen = offsets // amount % 2 == 1
        window = jnp.where(
            chosen[None, None, None, :], window[:, :, :length], window[:, :, amount:]
        )
    return window


def by_blocks(fields, shifts):
    rows = fields.shape[3]
    total_rows = rows * lax.axis_size("rad")
    row_index = lax.axis_index("rad") * rows + jnp.arange(rows, dtype=jnp.int32)
    radius = 1.0 + (row_index.astype(jnp.float32) + 0.5) / jnp.float32(total_rows)
    inverse = 1.0 / radius
    for step in range(STEPS):
        radial_pad = padded_2(fields, (("rad", 3),), 1, False)
        padded = padded_2(radial_pad, (("azi", 2),), 1, True)
        fields = update(padded, inverse)
        fields = rotate_pieces(fields, shifts[step])
    return fields


def local(fields, shifts):
    n, nr = lax.axis_size("azi"), lax.axis_size("rad")
    count, planes, width, rows = fields.shape
    fits = (count, planes, width, rows) == (FIELDS, 1, HALF, LANES)
    if fits and rows == n * 2 * SUB and n * width > SMAX + LANES:
        return by_cycles(n, nr, fields, shifts)
    return by_blocks(fields, shifts)


def solution(mesh):
    placed = (P(None, None, "azi", "rad"), P(None, "rad"))
    return jax.shard_map(
        local, mesh=mesh, in_specs=placed, out_specs=P(None, None, "azi", "rad"), check_vma=False
    )
```

```python
import functools

import jax
import jax.numpy as jnp
from jax import lax
from jax.experimental import pallas as pl
from jax.experimental.pallas import tpu as pltpu
from jax.sharding import PartitionSpec as P

STEPS = 3
SMAX = 192
FIELDS = 5
LANES = 128
SUB = 8
HALF = 64
PAIRS = (slice(0, 2), slice(2, 4), slice(4, 5))

courant = 0.2
viscous = 0.1


def halves(a, b, low):
    first = jnp.where(low, a, pltpu.roll(b, HALF, b.ndim - 1))
    second = jnp.where(low, pltpu.roll(a, HALF, a.ndim - 1), b)
    return first, second


def updates(f, inverse, rows):
    inner = [pltpu.roll(u, 1, 0)[:rows] for u in f]
    outer = [pltpu.roll(u, u.shape[0] - 1, 0)[:rows] for u in f]
    f = [u[:rows] for u in f]
    inverse = inverse[:rows]
    behind = [pltpu.roll(u, 1, 1) for u in f]
    ahead = [pltpu.roll(u, u.shape[1] - 1, 1) for u in f]
    _, vr, vp, _, temper = f
    cg = courant * inverse
    vg2 = viscous * inverse * inverse
    into, out = courant * jnp.maximum(vr, 0.0), -courant * jnp.minimum(vr, 0.0)
    back, fwd = cg * jnp.maximum(vp, 0.0), -cg * jnp.minimum(vp, 0.0)
    w_in, w_out, w_back, w_fwd = into + viscous, out + viscous, back + vg2, fwd + vg2

    def moved(i):
        u = f[i]
        polar = (u + u) - 2.0 * u
        return (
            u + viscous * polar
            + (w_out * (outer[i] - u) - w_in * (u - inner[i]))
            + (w_fwd * (ahead[i] - u) - w_back * (u - behind[i]))
        )

    def advected(i):
        u = f[i]
        return (
            u
            + (out * (outer[i] - u) - into * (u - inner[i]))
            + (fwd * (ahead[i] - u) - back * (u - behind[i]))
        )

    def dr(i):
        return outer[i] - inner[i]

    def dp(i):
        return ahead[i] - behind[i]

    half = 0.5 * courant
    half_g = 0.5 * cg
    diverge = dr(1) + inverse * dp(2)
    return [
        lambda: advected(0) - half * diverge,
        lambda: moved(1) - half * (temper * dr(0) + dr(4)) + half_g * vp * vp,
        lambda: moved(2) - half_g * (temper * dp(0) + dp(4) + vr * vp),
        lambda: moved(3),
        lambda: moved(4) - (0.4 * half) * temper * diverge,
    ]


def rotate(u, index, lag):
    tiles = u.shape[1] // LANES
    g = [
        jnp.take_along_axis(u[:, q * LANES : (q + 1) * LANES], index, axis=1)
        for q in range(tiles)
    ]
    out = []
    for q in range(tiles):
        value = g[(q - (SMAX // LANES + 1)) % tiles]
        for back in range(SMAX // LANES, -1, -1):
            value = jnp.where(lag == back, g[(q - back) % tiles], value)
        out.append(value)
    return jnp.concatenate(out, axis=1)


def kernel(
    n, nr, f_hbm, s_hbm, recv2, f_ref, s_ref, z, send, recv, halo, eout, edge, send2,
    ssem, rsem, esend, erecv, ssem2, rsem2, isem,
):
    loads = [
        pltpu.make_async_copy(f_hbm, f_ref, isem.at[0]),
        pltpu.make_async_copy(s_hbm, s_ref, isem.at[1]),
    ]
    for load in loads:
        load.start()
    r = lax.axis_index("rad")
    t = lax.axis_index("azi")
    tiles = f_ref.shape[3] // SUB
    chip, core = lax.div(t, 2), lax.rem(t, 2)
    chips = n // 2
    opposite = chips - 1 - chip
    beside, across = chip + 1 - 2 * lax.rem(chip, 2), lax.rem(chip + 2, chips)
    first = jnp.where(core == 0, across, beside)
    second = jnp.where(core == 0, beside, across)
    order = [opposite, first, second]
    peers = [2 * c + h for c in order for h in (core, 1 - core)] + [2 * chip + 1 - core]
    top_edge = (t == 0) & (r > 0)
    bottom_edge = (t == n - 1) & (r < nr - 1)

    barrier = pltpu.get_barrier_semaphore()
    for peer in peers:
        pl.semaphore_signal(barrier, inc=1, device_id={"azi": peer})

    @pl.when(top_edge)
    def _():
        for b in range(n):
            pl.semaphore_signal(barrier, inc=1, device_id={"rad": r - 1, "azi": b})

    @pl.when(bottom_edge)
    def _():
        for b in range(n):
            pl.semaphore_signal(barrier, inc=1, device_id={"rad": r + 1, "azi": b})

    sub = lax.broadcasted_iota(jnp.int32, (SUB, LANES), 0)
    lane = lax.broadcasted_iota(jnp.int32, (SUB, LANES), 1)
    low = lane < HALF

    def edge_copy(which, slot, device):
        return pltpu.make_async_remote_copy(
            src_ref=eout.at[which], dst_ref=edge.at[slot], send_sem=esend.at[which],
            recv_sem=erecv, device_id=device,
        )

    to_inner = edge_copy(0, t, {"rad": r - 1, "azi": n - 1})
    to_outer = edge_copy(1, t, {"rad": r + 1, "azi": 0})

    for load in loads:
        load.wait()
    for p, fs in enumerate(PAIRS):
        if p < 2:
            stack = f_ref[fs, 0].reshape(LANES, LANES)
        else:
            shifts = s_ref[...].astype(jnp.float32)
            rest = jnp.zeros((HALF - STEPS, LANES), jnp.float32)
            stack = jnp.concatenate([f_ref[4, 0], shifts, rest], axis=0)
        z[:, p] = stack.T.reshape(tiles, SUB, LANES)

    def halo_tile(p, k):
        above, below = jnp.maximum(2 * k - 1, 0), jnp.minimum(2 * k + 2, tiles - 1)
        return jnp.where(sub >= SUB - STEPS, z[above, p], z[below, p])

    for k in range(n):
        a, b = 2 * k, 2 * k + 1
        for p in range(2):
            send[k, 2 * p] = z[a, p]
            send[k, 2 * p + 1] = z[b, p]
        send[k, 4] = jnp.where(low, z[a, 2], pltpu.roll(z[b, 2], HALF, 1))
        last = halo_tile(2, k)
        free = jnp.where(low, pltpu.roll(last, 3, 0), pltpu.roll(pltpu.roll(last, 6, 0), HALF, 1))
        send[k, 5] = jnp.where((sub == 3) | (sub == 4), free, halo_tile(0, k))
        send[k, 6] = jnp.where(sub == 3, pltpu.roll(free, 6, 0), halo_tile(1, k))
    eout[0, 0] = jnp.where(sub < 4, z[0, 0], pltpu.roll(z[0, 1], 4, 0))
    eout[1, 0] = jnp.where(sub < 4, pltpu.roll(z[tiles - 1, 1], 4, 0), z[tiles - 1, 0])
    eout[0, 1] = z[0, 2]
    eout[1, 1] = z[tiles - 1, 2]

    needed = n - 1 + (r > 0).astype(jnp.int32) + (r < nr - 1).astype(jnp.int32)
    pl.semaphore_wait(barrier, needed)

    @pl.when(r > 0)
    def _():
        to_inner.start()

    @pl.when(r < nr - 1)
    def _():
        to_outer.start()

    def to_peer(src, dst, send_sem, recv_sem, peer):
        return pltpu.make_async_remote_copy(
            src_ref=src, dst_ref=dst, send_sem=send_sem, recv_sem=recv_sem,
            device_id={"azi": peer},
        )

    for peer in peers:
        to_peer(send.at[peer], recv.at[t], ssem, rsem, peer).start()
    there = to_peer(send.at[1:], recv.at[1:], ssem, rsem, peers[0])
    recv[t] = send[t]

    rows = 3 * SUB
    width = n * HALF
    row = lax.broadcasted_iota(jnp.int32, (rows, width), 0)
    row = jnp.where(row < 2 * SUB + SUB // 2, row, row - rows)
    row = row + (r * f_ref.shape[3] + t * (2 * SUB))
    total = nr * f_ref.shape[3]
    inside = (row >= 0) & (row < total)
    radius = 1.0 + (row.astype(jnp.float32) + 0.5) / jnp.float32(total)
    inverse = 1.0 / radius

    own = 2 * SUB

    def inner_rows(u):
        return jnp.concatenate([u[:own], jnp.where(inside[own:], u[own:], 0.0)], axis=0)

    there.wait_recv()
    own_shifts = halo_tile(2, t)
    for b in range(n):
        free = jnp.where(sub == 5, pltpu.roll(recv[b, 6], 2, 0), recv[b, 5])
        bottom, top = pltpu.roll(free, 5, 0), pltpu.roll(pltpu.roll(free, 2, 0), HALF, 1)
        halo[b] = jnp.where(low, jnp.where(sub < 4, bottom, top), own_shifts)

    @pl.when(top_edge | bottom_edge)
    def _():
        first = jnp.where(t == 0, SUB - STEPS, 0)
        last = jnp.where(t == 0, SUB, STEPS)
        take = (sub >= first) & (sub < last)
        pltpu.make_async_remote_copy(
            src_ref=recv.at[:, :2], dst_ref=edge, send_sem=esend.at[0], recv_sem=erecv,
            device_id={"rad": lax.rem(r + 1, nr)},
        ).wait_recv()
        for b in range(n):
            recv[b, 5] = jnp.where(take, edge[b, 0], recv[b, 5])
            recv[b, 6] = jnp.where(take, pltpu.roll(edge[b, 0], 4, 0), recv[b, 6])
            halo[b] = jnp.where(take, edge[b, 1], halo[b])

    fields = [[] for _ in range(FIELDS)]
    for q in range(n // 2):
        got = [halves(recv[2 * q, i], recv[2 * q + 1, i], low) for i in range(7)]
        for p in range(2):
            for h in range(2):
                tiles_of = (got[2 * p][h], got[2 * p + 1][h], got[5 + p][h])
                fields[2 * p + h].append(jnp.concatenate(tiles_of, axis=0))
        last = jnp.where(low, halo[2 * q], pltpu.roll(halo[2 * q + 1], HALF, 1))
        fields[4].append(jnp.concatenate([got[4][0], got[4][1], last], axis=0))
    fields = [inner_rows(jnp.concatenate(u, axis=1)) for u in fields]

    carried = jnp.concatenate([z[2 * t, 2], z[2 * t + 1, 2], halo[0]], axis=0)
    lanes = lax.broadcasted_iota(jnp.int32, (rows, LANES), 1)
    for step in range(STEPS):
        shift = carried[:, HALF + step : HALF + step + 1].astype(jnp.int32)
        shift = jnp.broadcast_to(shift, (rows, LANES))
        whole = jnp.where(shift >= LANES, 1, 0)
        part = shift - whole * LANES
        index = jnp.bitwise_and(lanes - part, LANES - 1)
        lag = whole + jnp.where(lanes < part, 1, 0)
        if step < STEPS - 1:
            fields = [inner_rows(new()) for new in updates(fields, inverse, rows)]
            fields = [rotate(u, index, lag) for u in fields]

    news = updates(fields, inverse, own)
    for p, fs in enumerate(PAIRS):
        pair = [rotate(new(), index[:own], lag[:own]) for new in news[fs]]
        for q in range(n // 2):
            f = [u[:, q * LANES : (q + 1) * LANES] for u in pair]
            if p < 2:
                for i in range(2):
                    rs = slice(i * SUB, (i + 1) * SUB)
                    even, odd = halves(f[0][rs], f[1][rs], low)
                    send2[2 * q, 2 * p + i] = even
                    send2[2 * q + 1, 2 * p + i] = odd
            else:
                even, odd = halves(f[0][:SUB], f[0][SUB:], low)
                send2[2 * q, 4] = even
                send2[2 * q + 1, 4] = odd
    others = [jnp.where(j < chip, j, j + 1) for j in range(chips - 1)]
    for peer in [2 * c + h for c in others for h in (core, 1 - core)] + peers[-1:]:
        to_peer(send2.at[peer], recv2.at[t], ssem2, rsem2, peer).start()
    back = to_peer(send2.at[1:], recv2.at[1:], ssem2, rsem2, peers[0])
    recv2[t] = send2[t]

    there.wait_send()

    @pl.when(r > 0)
    def _():
        to_inner.wait_send()

    @pl.when(r < nr - 1)
    def _():
        to_outer.wait_send()

    back.wait_recv()

    back.wait_send()


def to_cells(got, o_hbm, out, sem):
    n = got.shape[0]
    writes = []
    for p in range(3):
        fs = slice(2 * p, min(2 * p + 2, FIELDS))
        if p < 2:
            block = got[:, 2 * p : 2 * p + 2].reshape(LANES, LANES)
            out[fs, 0] = block.T.reshape(2, HALF, LANES)
        else:
            parts = []
            for b in range(n):
                tile = got[b, 4]
                parts += [tile, pltpu.roll(tile, HALF, 1)]
            out[4, 0] = jnp.concatenate(parts, axis=0).T[:HALF]
        write = pltpu.make_async_copy(out.at[fs], o_hbm.at[fs], sem.at[p])
        write.start()
        writes.append(write)
    for write in writes:
        write.wait()


def by_cycles(n, nr, fields, shifts):
    tiles = fields.shape[3] // SUB
    tile = (SUB, LANES)
    dma = pltpu.SemaphoreType.DMA
    got = pl.pallas_call(
        functools.partial(kernel, n, nr),
        out_shape=pltpu.VMEM((n, 5) + tile, jnp.float32),
        in_specs=[pl.BlockSpec(memory_space=pltpu.HBM)] * 2,
        out_specs=pl.BlockSpec(memory_space=pltpu.VMEM),
        scratch_shapes=[
            pltpu.VMEM(fields.shape, fields.dtype),
            pltpu.VMEM(shifts.shape, shifts.dtype),
            pltpu.VMEM((tiles, 3) + tile, jnp.float32),
            pltpu.VMEM((n, 7) + tile, jnp.float32),
            pltpu.VMEM((n, 7) + tile, jnp.float32),
            pltpu.VMEM((n,) + tile, jnp.float32),
            pltpu.VMEM((2, 2) + tile, jnp.float32),
            pltpu.VMEM((n, 2) + tile, jnp.float32),
            pltpu.VMEM((n, 5) + tile, jnp.float32),
            dma,
            dma,
            dma((2,)),
            dma,
            dma,
            dma,
            dma((2,)),
        ],
        compiler_params=pltpu.CompilerParams(
            collective_id=0, has_side_effects=True, vmem_limit_bytes=16 * 1024 * 1024
        ),
    )(
        pltpu.with_memory_space_constraint(fields, pltpu.HBM),
        pltpu.with_memory_space_constraint(shifts, pltpu.HBM),
    )
    return pl.pallas_call(
        to_cells,
        out_shape=jax.ShapeDtypeStruct(fields.shape, fields.dtype),
        in_specs=[pl.BlockSpec(memory_space=pltpu.VMEM)],
        out_specs=pl.BlockSpec(memory_space=pltpu.HBM),
        scratch_shapes=[pltpu.VMEM(fields.shape, fields.dtype), dma((3,))],
        compiler_params=pltpu.CompilerParams(vmem_limit_bytes=16 * 1024 * 1024),
    )(got)


def passed_along(value, axis, steps):
    count = lax.axis_size(axis)
    pairs = [(source, (source + steps) % count) for source in range(count)]
    return lax.ppermute(value, axis, pairs)


def padded_2(value, sides, width, wrap):
    for axis, dim in sides:
        count, length = (lax.axis_size(axis), value.shape[dim])
        up = [(i, (i + 1) % count) for i in range(count if wrap else count - 1)]
        down = [(j, i) for i, j in up]
        last = lax.slice_in_dim(value, length - width, length, axis=dim)
        initial = lax.slice_in_dim(value, 0, width, axis=dim)
        before = lax.ppermute(last, axis, up)
        after = lax.ppermute(initial, axis, down)
        value = jnp.concatenate([before, value, after], axis=dim)
    return value


def update(padded, inverse):
    centre = padded[:, :, 1:-1, 1:-1]
    inner = padded[:, :, 1:-1, :-2]
    outer = padded[:, :, 1:-1, 2:]
    behind = padded[:, :, :-2, 1:-1]
    ahead = padded[:, :, 2:, 1:-1]
    polar_pad = jnp.concatenate([centre, centre, centre], axis=1)
    polar_sum = polar_pad[:, 2:] + polar_pad[:, :-2]
    radial_vel = centre[1]
    azim_vel = centre[2]
    advect = courant * (
        jnp.maximum(radial_vel, 0.0) * (centre - inner)
        + jnp.minimum(radial_vel, 0.0) * (outer - centre)
        + inverse
        * (
            jnp.maximum(azim_vel, 0.0) * (centre - behind)
            + jnp.minimum(azim_vel, 0.0) * (ahead - centre)
        )
    )
    laplace = (
        outer
        + inner
        - 2.0 * centre
        + inverse * inverse * (ahead + behind - 2.0 * centre)
        + (polar_sum - 2.0 * centre)
    )
    radial_diff = (outer - inner) * 0.5
    azim_diff = (ahead - behind) * 0.5
    diverge = radial_diff[1] + inverse * azim_diff[2]
    log_rho = centre[0]
    temper = centre[4]
    new_log = log_rho - advect[0] - courant * diverge
    new_radial = (
        radial_vel
        - advect[1]
        - courant * (temper * radial_diff[0] + radial_diff[4])
        + 0.5 * courant * inverse * azim_vel * azim_vel
        + viscous * laplace[1]
    )
    new_azim = (
        azim_vel
        - advect[2]
        - courant * inverse * (temper * azim_diff[0] + azim_diff[4])
        - 0.5 * courant * inverse * radial_vel * azim_vel
        + viscous * laplace[2]
    )
    new_polar = centre[3] - advect[3] + viscous * laplace[3]
    new_temper = temper - advect[4] - courant * 0.4 * temper * diverge + viscous * laplace[4]
    return jnp.stack([new_log, new_radial, new_azim, new_polar, new_temper])


def rotate_pieces(fields, offsets):
    width = fields.shape[2]
    count = (SMAX + width - 1) // width
    pieces = [fields]
    for blocks in range(1, count + 1):
        pieces.append(passed_along(fields, "azi", blocks))
    extended = jnp.concatenate(pieces[::-1], axis=2)
    nbits = SMAX.bit_length()
    reach = (1 << nbits) - 1
    anchor = count * width
    front = jnp.zeros(fields.shape[:2] + (reach - anchor,) + fields.shape[3:], fields.dtype)
    window = jnp.concatenate([front, extended], axis=2)
    for bit in range(nbits):
        amount = 1 << bit
        length = window.shape[2] - amount
        chosen = offsets // amount % 2 == 1
        window = jnp.where(
            chosen[None, None, None, :], window[:, :, :length], window[:, :, amount:]
        )
    return window


def by_blocks(fields, shifts):
    rows = fields.shape[3]
    total_rows = rows * lax.axis_size("rad")
    row_index = lax.axis_index("rad") * rows + jnp.arange(rows, dtype=jnp.int32)
    radius = 1.0 + (row_index.astype(jnp.float32) + 0.5) / jnp.float32(total_rows)
    inverse = 1.0 / radius
    for step in range(STEPS):
        radial_pad = padded_2(fields, (("rad", 3),), 1, False)
        padded = padded_2(radial_pad, (("azi", 2),), 1, True)
        fields = update(padded, inverse)
        fields = rotate_pieces(fields, shifts[step])
    return fields


def local(fields, shifts):
    n, nr = lax.axis_size("azi"), lax.axis_size("rad")
    count, planes, width, rows = fields.shape
    fits = (count, planes, width, rows) == (FIELDS, 1, HALF, LANES)
    if fits and rows == n * 2 * SUB and n * width > SMAX + LANES:
        return by_cycles(n, nr, fields, shifts)
    return by_blocks(fields, shifts)


def solution(mesh):
    placed = (P(None, None, "azi", "rad"), P(None, "rad"))
    return jax.shard_map(
        local, mesh=mesh, in_specs=placed, out_specs=P(None, None, "azi", "rad"), check_vma=False
    )
```

```python
import functools

import jax
import jax.numpy as jnp
from jax import lax
from jax.experimental import pallas as pl
from jax.experimental.pallas import tpu as pltpu
from jax.sharding import PartitionSpec as P

STEPS = 3
SMAX = 192
FIELDS = 5
LANES = 128
SUB = 8
HALF = 64
PAIRS = (slice(0, 2), slice(2, 4), slice(4, 5))

courant = 0.2
viscous = 0.1


def halves(a, b, low):
    first = jnp.where(low, a, pltpu.roll(b, HALF, b.ndim - 1))
    second = jnp.where(low, pltpu.roll(a, HALF, a.ndim - 1), b)
    return first, second


def updates(f, inverse, rows):
    inner = [pltpu.roll(u, 1, 0)[:rows] for u in f]
    outer = [pltpu.roll(u, u.shape[0] - 1, 0)[:rows] for u in f]
    f = [u[:rows] for u in f]
    inverse = inverse[:rows]
    behind = [pltpu.roll(u, 1, 1) for u in f]
    ahead = [pltpu.roll(u, u.shape[1] - 1, 1) for u in f]
    _, vr, vp, _, temper = f
    cg = courant * inverse
    vg2 = viscous * inverse * inverse
    into, out = courant * jnp.maximum(vr, 0.0), -courant * jnp.minimum(vr, 0.0)
    back, fwd = cg * jnp.maximum(vp, 0.0), -cg * jnp.minimum(vp, 0.0)
    w_in, w_out, w_back, w_fwd = into + viscous, out + viscous, back + vg2, fwd + vg2

    def moved(i):
        u = f[i]
        polar = (u + u) - 2.0 * u
        return (
            u + viscous * polar
            + (w_out * (outer[i] - u) - w_in * (u - inner[i]))
            + (w_fwd * (ahead[i] - u) - w_back * (u - behind[i]))
        )

    def advected(i):
        u = f[i]
        return (
            u
            + (out * (outer[i] - u) - into * (u - inner[i]))
            + (fwd * (ahead[i] - u) - back * (u - behind[i]))
        )

    def dr(i):
        return outer[i] - inner[i]

    def dp(i):
        return ahead[i] - behind[i]

    half = 0.5 * courant
    half_g = 0.5 * cg
    diverge = dr(1) + inverse * dp(2)
    return [
        lambda: advected(0) - half * diverge,
        lambda: moved(1) - half * (temper * dr(0) + dr(4)) + half_g * vp * vp,
        lambda: moved(2) - half_g * (temper * dp(0) + dp(4) + vr * vp),
        lambda: moved(3),
        lambda: moved(4) - (0.4 * half) * temper * diverge,
    ]


def rotate(u, index, lag):
    tiles = u.shape[1] // LANES
    g = [
        jnp.take_along_axis(u[:, q * LANES : (q + 1) * LANES], index, axis=1)
        for q in range(tiles)
    ]
    out = []
    for q in range(tiles):
        value = g[(q - (SMAX // LANES + 1)) % tiles]
        for back in range(SMAX // LANES, -1, -1):
            value = jnp.where(lag == back, g[(q - back) % tiles], value)
        out.append(value)
    return jnp.concatenate(out, axis=1)


def kernel(
    n, nr, f_hbm, s_hbm, recv2, f_ref, s_ref, z, send, recv, halo, eout, edge, send2,
    ssem, rsem, esend, erecv, ssem2, rsem2, isem,
):
    loads = [
        pltpu.make_async_copy(f_hbm, f_ref, isem.at[0]),
        pltpu.make_async_copy(s_hbm, s_ref, isem.at[1]),
    ]
    for load in loads:
        load.start()
    r = lax.axis_index("rad")
    t = lax.axis_index("azi")
    tiles = f_ref.shape[3] // SUB
    chip, core = lax.div(t, 2), lax.rem(t, 2)
    chips = n // 2
    opposite = chips - 1 - chip
    beside, across = chip + 1 - 2 * lax.rem(chip, 2), lax.rem(chip + 2, chips)
    first = jnp.where(core == 0, across, beside)
    second = jnp.where(core == 0, beside, across)
    order = [opposite, first, second]
    peers = [2 * c + h for c in order for h in (core, 1 - core)] + [2 * chip + 1 - core]
    top_edge = (t == 0) & (r > 0)
    bottom_edge = (t == n - 1) & (r < nr - 1)

    barrier = pltpu.get_barrier_semaphore()
    for peer in peers:
        pl.semaphore_signal(barrier, inc=1, device_id={"azi": peer})

    @pl.when(top_edge)
    def _():
        for b in range(n):
            pl.semaphore_signal(barrier, inc=1, device_id={"rad": r - 1, "azi": b})

    @pl.when(bottom_edge)
    def _():
        for b in range(n):
            pl.semaphore_signal(barrier, inc=1, device_id={"rad": r + 1, "azi": b})

    sub = lax.broadcasted_iota(jnp.int32, (SUB, LANES), 0)
    lane = lax.broadcasted_iota(jnp.int32, (SUB, LANES), 1)
    low = lane < HALF

    def edge_copy(which, slot, device):
        return pltpu.make_async_remote_copy(
            src_ref=eout.at[which], dst_ref=edge.at[slot], send_sem=esend.at[which],
            recv_sem=erecv, device_id=device,
        )

    to_inner = edge_copy(0, t, {"rad": r - 1, "azi": n - 1})
    to_outer = edge_copy(1, t, {"rad": r + 1, "azi": 0})

    for load in loads:
        load.wait()
    for p, fs in enumerate(PAIRS):
        if p < 2:
            stack = f_ref[fs, 0].reshape(LANES, LANES)
        else:
            shifts = s_ref[...].astype(jnp.float32)
            rest = jnp.zeros((HALF - STEPS, LANES), jnp.float32)
            stack = jnp.concatenate([f_ref[4, 0], shifts, rest], axis=0)
        z[:, p] = stack.T.reshape(tiles, SUB, LANES)

    def halo_tile(p, k):
        above, below = jnp.maximum(2 * k - 1, 0), jnp.minimum(2 * k + 2, tiles - 1)
        return jnp.where(sub >= SUB - STEPS, z[above, p], z[below, p])

    def build(k):
        a, b = 2 * k, 2 * k + 1
        for p in range(2):
            send[k, 2 * p] = z[a, p]
            send[k, 2 * p + 1] = z[b, p]
        send[k, 4] = jnp.where(low, z[a, 2], pltpu.roll(z[b, 2], HALF, 1))
        last = halo_tile(2, k)
        free = jnp.where(low, pltpu.roll(last, 3, 0), pltpu.roll(pltpu.roll(last, 6, 0), HALF, 1))
        send[k, 5] = jnp.where((sub == 3) | (sub == 4), free, halo_tile(0, k))
        send[k, 6] = jnp.where(sub == 3, pltpu.roll(free, 6, 0), halo_tile(1, k))

    build(peers[0])
    eout[0, 0] = jnp.where(sub < 4, z[0, 0], pltpu.roll(z[0, 1], 4, 0))
    eout[1, 0] = jnp.where(sub < 4, pltpu.roll(z[tiles - 1, 1], 4, 0), z[tiles - 1, 0])
    eout[0, 1] = z[0, 2]
    eout[1, 1] = z[tiles - 1, 2]

    needed = n - 1 + (r > 0).astype(jnp.int32) + (r < nr - 1).astype(jnp.int32)
    pl.semaphore_wait(barrier, needed)

    def to_peer(src, dst, send_sem, recv_sem, peer):
        return pltpu.make_async_remote_copy(
            src_ref=src, dst_ref=dst, send_sem=send_sem, recv_sem=recv_sem,
            device_id={"azi": peer},
        )

    for i, peer in enumerate(peers):
        to_peer(send.at[peer], recv.at[t], ssem, rsem, peer).start()
        build(peers[i + 1] if i < n - 2 else t)
        if i == 1:

            @pl.when(r > 0)
            def _():
                to_inner.start()

            @pl.when(r < nr - 1)
            def _():
                to_outer.start()

    there = to_peer(send.at[1:], recv.at[1:], ssem, rsem, peers[0])
    recv[t] = send[t]

    rows = 3 * SUB
    width = n * HALF
    row = lax.broadcasted_iota(jnp.int32, (rows, width), 0)
    row = jnp.where(row < 2 * SUB + SUB // 2, row, row - rows)
    row = row + (r * f_ref.shape[3] + t * (2 * SUB))
    total = nr * f_ref.shape[3]
    inside = (row >= 0) & (row < total)
    radius = 1.0 + (row.astype(jnp.float32) + 0.5) / jnp.float32(total)
    inverse = 1.0 / radius

    own = 2 * SUB

    def inner_rows(u):
        return jnp.concatenate([u[:own], jnp.where(inside[own:], u[own:], 0.0)], axis=0)

    there.wait_recv()
    own_shifts = halo_tile(2, t)
    for b in range(n):
        free = jnp.where(sub == 5, pltpu.roll(recv[b, 6], 2, 0), recv[b, 5])
        bottom, top = pltpu.roll(free, 5, 0), pltpu.roll(pltpu.roll(free, 2, 0), HALF, 1)
        halo[b] = jnp.where(low, jnp.where(sub < 4, bottom, top), own_shifts)

    @pl.when(top_edge | bottom_edge)
    def _():
        first = jnp.where(t == 0, SUB - STEPS, 0)
        last = jnp.where(t == 0, SUB, STEPS)
        take = (sub >= first) & (sub < last)
        pltpu.make_async_remote_copy(
            src_ref=recv.at[:, :2], dst_ref=edge, send_sem=esend.at[0], recv_sem=erecv,
            device_id={"rad": lax.rem(r + 1, nr)},
        ).wait_recv()
        for b in range(n):
            recv[b, 5] = jnp.where(take, edge[b, 0], recv[b, 5])
            recv[b, 6] = jnp.where(take, pltpu.roll(edge[b, 0], 4, 0), recv[b, 6])
            halo[b] = jnp.where(take, edge[b, 1], halo[b])

    fields = [[] for _ in range(FIELDS)]
    for q in range(n // 2):
        got = [halves(recv[2 * q, i], recv[2 * q + 1, i], low) for i in range(7)]
        for p in range(2):
            for h in range(2):
                tiles_of = (got[2 * p][h], got[2 * p + 1][h], got[5 + p][h])
                fields[2 * p + h].append(jnp.concatenate(tiles_of, axis=0))
        last = jnp.where(low, halo[2 * q], pltpu.roll(halo[2 * q + 1], HALF, 1))
        fields[4].append(jnp.concatenate([got[4][0], got[4][1], last], axis=0))
    fields = [inner_rows(jnp.concatenate(u, axis=1)) for u in fields]

    carried = jnp.concatenate([z[2 * t, 2], z[2 * t + 1, 2], halo[0]], axis=0)
    lanes = lax.broadcasted_iota(jnp.int32, (rows, LANES), 1)
    for step in range(STEPS):
        shift = carried[:, HALF + step : HALF + step + 1].astype(jnp.int32)
        shift = jnp.broadcast_to(shift, (rows, LANES))
        whole = jnp.where(shift >= LANES, 1, 0)
        part = shift - whole * LANES
        index = jnp.bitwise_and(lanes - part, LANES - 1)
        lag = whole + jnp.where(lanes < part, 1, 0)
        if step < STEPS - 1:
            fields = [inner_rows(new()) for new in updates(fields, inverse, rows)]
            fields = [rotate(u, index, lag) for u in fields]

    news = updates(fields, inverse, own)
    for p, fs in enumerate(PAIRS):
        pair = [rotate(new(), index[:own], lag[:own]) for new in news[fs]]
        for q in range(n // 2):
            f = [u[:, q * LANES : (q + 1) * LANES] for u in pair]
            if p < 2:
                for i in range(2):
                    rs = slice(i * SUB, (i + 1) * SUB)
                    even, odd = halves(f[0][rs], f[1][rs], low)
                    send2[2 * q, 2 * p + i] = even
                    send2[2 * q + 1, 2 * p + i] = odd
            else:
                even, odd = halves(f[0][:SUB], f[0][SUB:], low)
                send2[2 * q, 4] = even
                send2[2 * q + 1, 4] = odd
    for peer in peers:
        to_peer(send2.at[peer], recv2.at[t], ssem2, rsem2, peer).start()
    back = to_peer(send2.at[1:], recv2.at[1:], ssem2, rsem2, peers[0])
    recv2[t] = send2[t]

    there.wait_send()

    @pl.when(r > 0)
    def _():
        to_inner.wait_send()

    @pl.when(r < nr - 1)
    def _():
        to_outer.wait_send()

    back.wait_recv()

    back.wait_send()


def to_cells(got, o_hbm, out, sem):
    n = got.shape[0]
    writes = []
    for p in range(3):
        fs = slice(2 * p, min(2 * p + 2, FIELDS))
        if p < 2:
            block = got[:, 2 * p : 2 * p + 2].reshape(LANES, LANES)
            out[fs, 0] = block.T.reshape(2, HALF, LANES)
        else:
            parts = []
            for b in range(n):
                tile = got[b, 4]
                parts += [tile, pltpu.roll(tile, HALF, 1)]
            out[4, 0] = jnp.concatenate(parts, axis=0).T[:HALF]
        write = pltpu.make_async_copy(out.at[fs], o_hbm.at[fs], sem.at[p])
        write.start()
        writes.append(write)
    for write in writes:
        write.wait()


def by_cycles(n, nr, fields, shifts):
    tiles = fields.shape[3] // SUB
    tile = (SUB, LANES)
    dma = pltpu.SemaphoreType.DMA
    got = pl.pallas_call(
        functools.partial(kernel, n, nr),
        out_shape=pltpu.VMEM((n, 5) + tile, jnp.float32),
        in_specs=[pl.BlockSpec(memory_space=pltpu.HBM)] * 2,
        out_specs=pl.BlockSpec(memory_space=pltpu.VMEM),
        scratch_shapes=[
            pltpu.VMEM(fields.shape, fields.dtype),
            pltpu.VMEM(shifts.shape, shifts.dtype),
            pltpu.VMEM((tiles, 3) + tile, jnp.float32),
            pltpu.VMEM((n, 7) + tile, jnp.float32),
            pltpu.VMEM((n, 7) + tile, jnp.float32),
            pltpu.VMEM((n,) + tile, jnp.float32),
            pltpu.VMEM((2, 2) + tile, jnp.float32),
            pltpu.VMEM((n, 2) + tile, jnp.float32),
            pltpu.VMEM((n, 5) + tile, jnp.float32),
            dma,
            dma,
            dma((2,)),
            dma,
            dma,
            dma,
            dma((2,)),
        ],
        compiler_params=pltpu.CompilerParams(
            collective_id=0, has_side_effects=True, vmem_limit_bytes=16 * 1024 * 1024
        ),
    )(
        pltpu.with_memory_space_constraint(fields, pltpu.HBM),
        pltpu.with_memory_space_constraint(shifts, pltpu.HBM),
    )
    return pl.pallas_call(
        to_cells,
        out_shape=jax.ShapeDtypeStruct(fields.shape, fields.dtype),
        in_specs=[pl.BlockSpec(memory_space=pltpu.VMEM)],
        out_specs=pl.BlockSpec(memory_space=pltpu.HBM),
        scratch_shapes=[pltpu.VMEM(fields.shape, fields.dtype), dma((3,))],
        compiler_params=pltpu.CompilerParams(vmem_limit_bytes=16 * 1024 * 1024),
    )(got)


def passed_along(value, axis, steps):
    count = lax.axis_size(axis)
    pairs = [(source, (source + steps) % count) for source in range(count)]
    return lax.ppermute(value, axis, pairs)


def padded_2(value, sides, width, wrap):
    for axis, dim in sides:
        count, length = (lax.axis_size(axis), value.shape[dim])
        up = [(i, (i + 1) % count) for i in range(count if wrap else count - 1)]
        down = [(j, i) for i, j in up]
        last = lax.slice_in_dim(value, length - width, length, axis=dim)
        initial = lax.slice_in_dim(value, 0, width, axis=dim)
        before = lax.ppermute(last, axis, up)
        after = lax.ppermute(initial, axis, down)
        value = jnp.concatenate([before, value, after], axis=dim)
    return value


def update(padded, inverse):
    centre = padded[:, :, 1:-1, 1:-1]
    inner = padded[:, :, 1:-1, :-2]
    outer = padded[:, :, 1:-1, 2:]
    behind = padded[:, :, :-2, 1:-1]
    ahead = padded[:, :, 2:, 1:-1]
    polar_pad = jnp.concatenate([centre, centre, centre], axis=1)
    polar_sum = polar_pad[:, 2:] + polar_pad[:, :-2]
    radial_vel = centre[1]
    azim_vel = centre[2]
    advect = courant * (
        jnp.maximum(radial_vel, 0.0) * (centre - inner)
        + jnp.minimum(radial_vel, 0.0) * (outer - centre)
        + inverse
        * (
            jnp.maximum(azim_vel, 0.0) * (centre - behind)
            + jnp.minimum(azim_vel, 0.0) * (ahead - centre)
        )
    )
    laplace = (
        outer
        + inner
        - 2.0 * centre
        + inverse * inverse * (ahead + behind - 2.0 * centre)
        + (polar_sum - 2.0 * centre)
    )
    radial_diff = (outer - inner) * 0.5
    azim_diff = (ahead - behind) * 0.5
    diverge = radial_diff[1] + inverse * azim_diff[2]
    log_rho = centre[0]
    temper = centre[4]
    new_log = log_rho - advect[0] - courant * diverge
    new_radial = (
        radial_vel
        - advect[1]
        - courant * (temper * radial_diff[0] + radial_diff[4])
        + 0.5 * courant * inverse * azim_vel * azim_vel
        + viscous * laplace[1]
    )
    new_azim = (
        azim_vel
        - advect[2]
        - courant * inverse * (temper * azim_diff[0] + azim_diff[4])
        - 0.5 * courant * inverse * radial_vel * azim_vel
        + viscous * laplace[2]
    )
    new_polar = centre[3] - advect[3] + viscous * laplace[3]
    new_temper = temper - advect[4] - courant * 0.4 * temper * diverge + viscous * laplace[4]
    return jnp.stack([new_log, new_radial, new_azim, new_polar, new_temper])


def rotate_pieces(fields, offsets):
    width = fields.shape[2]
    count = (SMAX + width - 1) // width
    pieces = [fields]
    for blocks in range(1, count + 1):
        pieces.append(passed_along(fields, "azi", blocks))
    extended = jnp.concatenate(pieces[::-1], axis=2)
    nbits = SMAX.bit_length()
    reach = (1 << nbits) - 1
    anchor = count * width
    front = jnp.zeros(fields.shape[:2] + (reach - anchor,) + fields.shape[3:], fields.dtype)
    window = jnp.concatenate([front, extended], axis=2)
    for bit in range(nbits):
        amount = 1 << bit
        length = window.shape[2] - amount
        chosen = offsets // amount % 2 == 1
        window = jnp.where(
            chosen[None, None, None, :], window[:, :, :length], window[:, :, amount:]
        )
    return window


def by_blocks(fields, shifts):
    rows = fields.shape[3]
    total_rows = rows * lax.axis_size("rad")
    row_index = lax.axis_index("rad") * rows + jnp.arange(rows, dtype=jnp.int32)
    radius = 1.0 + (row_index.astype(jnp.float32) + 0.5) / jnp.float32(total_rows)
    inverse = 1.0 / radius
    for step in range(STEPS):
        radial_pad = padded_2(fields, (("rad", 3),), 1, False)
        padded = padded_2(radial_pad, (("azi", 2),), 1, True)
        fields = update(padded, inverse)
        fields = rotate_pieces(fields, shifts[step])
    return fields


def local(fields, shifts):
    n, nr = lax.axis_size("azi"), lax.axis_size("rad")
    count, planes, width, rows = fields.shape
    fits = (count, planes, width, rows) == (FIELDS, 1, HALF, LANES)
    if fits and rows == n * 2 * SUB and n * width > SMAX + LANES:
        return by_cycles(n, nr, fields, shifts)
    return by_blocks(fields, shifts)


def solution(mesh):
    placed = (P(None, None, "azi", "rad"), P(None, "rad"))
    return jax.shard_map(
        local, mesh=mesh, in_specs=placed, out_specs=P(None, None, "azi", "rad"), check_vma=False
    )
```
